512 devices in a mesh: ctx: 64 (over y, z), smp: 8 (over x, core).
Axes of the slice: x: 4, y: 4, z: 16, core: 2. Of those that a mesh axis runs over, the one named last changes fastest.
Arguments:
- queries: bfloat16 [8, 16384, 2048], P('smp', 'ctx'), may hold values from -200 to 200
- out_grad: bfloat16 [8, 16384, 2048], P('smp', 'ctx'), may hold values from -6 to 6
- local_keys: bfloat16 [8, 16384, 512], P('smp', 'ctx'), may hold values from -4 to 4
- trajectory_values: bfloat16 [8, 16384, 512], P('smp', 'ctx'), may hold values from -6 to 6
- journal_keys: bfloat16 [64, 256, 512], P('ctx'), may hold values from -6 to 6
- journal_values: bfloat16 [64, 256, 512], P('ctx'), may hold values from -6 to 6
- picks: int32 [8, 64, 3], P('smp', 'ctx'), may hold values from 0 to 63, all different within a row
- lengths: int32 [8], P('smp'), may hold values from 1 to 16384, as said below
Outputs:
- grad_queries: bfloat16 [8, 16384, 2048], P('smp', 'ctx')
- grad_local_keys: bfloat16 [8, 16384, 512], P('smp', 'ctx')
- grad_local_values: bfloat16 [8, 16384, 512], P('smp', 'ctx')
- grad_log_keys: bfloat16 [64, 256, 512], P('ctx', None, 'smp')
- grad_log_values: bfloat16 [64, 256, 512], P('ctx', None, 'smp')
The draws below stay inside these ranges and needn't reach their ends.
Inputs may be any that keep to these rules, and one draw needn't show every extreme that they name: `lengths`: each trajectory's length in tokens; some trajectory has all 16384 tokens. The 3 picks of a query block are different blocks.
All inputs are finite; a program needn't handle non-finite values.
Results may differ from the reference program's by a relative error of at most 0.028.
Values may be sent and summed in bfloat16 or wider, within the bound.
A program may use at most 64 MiB of HBM per device.

```python
import math
import jax
import jax.numpy as jnp
from jax import lax

QUERY_HEAD_COUNT = 16
KEY_VALUE_HEADS = 4
HEAD_SIZE = 128
LOG_BLOCK_TOKENS = 256
TOPK = 3
QUERY_BLOCK_LEN = 256
TRAJECTORY_COUNT = 8
QB = 64
LOG_BLOCK_COUNT = 64
TRAJECTORY_LEN = 16384


def shared_keys(key):
    return jnp.clip(jax.random.normal(key, (TRAJECTORY_COUNT, TRAJECTORY_LEN, KEY_VALUE_HEADS * HEAD_SIZE), jnp.float32), -4.0, 4.0)


def draw_local_keys(key, part):
    base_keys = shared_keys(key)
    return base_keys.astype(jnp.bfloat16)


def draw_queries(key, part):
    key = jax.random.fold_in(key, 3)
    values = jnp.clip(jax.random.normal(key, (TRAJECTORY_COUNT, TRAJECTORY_LEN, QUERY_HEAD_COUNT * HEAD_SIZE), jnp.float32), -6.0, 6.0)
    return values.astype(jnp.bfloat16)


def draw_lengths(key, part):
    key = jax.random.fold_in(key, 7)
    values = jax.random.randint(key, (TRAJECTORY_COUNT,), 1, TRAJECTORY_LEN + 1, dtype=jnp.int32)
    longest = jax.random.randint(jax.random.fold_in(key, 1), (), 0, TRAJECTORY_COUNT, dtype=jnp.int32)
    return values.at[longest].set(TRAJECTORY_LEN)


def steps_of(stream_key, dims, cuts, smallest, high):
    gain = 1.0
    for dim, parts in cuts:
        steps = jax.random.uniform(jax.random.fold_in(jax.random.fold_in(stream_key, 6), dim), (parts,), jnp.float32, smallest / len(cuts), high / len(cuts))
        gain = gain * jnp.repeat(jnp.exp(steps), dims[dim] // parts).reshape((-1,) + (1,) * (len(dims) - 1 - dim))
    return gain


def distinct(key, rows, amount, top, lift):
    ranking = jax.random.permutation(jax.random.fold_in(key, 1), amount)
    favour = ranking
    for power in range(3):
        favour = favour * favour // amount
    favour = favour * lift // amount
    lots = jax.random.randint(jax.random.fold_in(key, 2), (rows, amount), 0, 4096) + favour
    holders = jax.random.permutation(jax.random.fold_in(key, 3), rows)[jnp.arange(amount) % rows]
    lots = jnp.where(jnp.arange(rows)[:, None] == holders[None, :], 1 << 14, lots)
    merit = lots * amount + jnp.arange(amount)
    return lax.top_k(merit.astype(jnp.int32), top)[1].astype(jnp.int32)


def noise(stream_key, shape, deviation, limit, cuts=(), kind=jnp.bfloat16):
    drawn = jax.random.normal(stream_key, shape, jnp.float32) * deviation
    if len(cuts) > 0:
        drawn = steps_of(stream_key, shape, cuts, -0.22, 0.18) * drawn
    return jnp.clip(drawn, min=-limit, max=limit).astype(kind)


def setup_inputs(seed: int = 0) -> dict:
    key_list = jax.random.split(jax.random.key(seed), 9)
    return {
        "queries": draw_queries(jax.random.fold_in(key_list[8], 71), 0),
        "out_grad": noise(key_list[1], (TRAJECTORY_COUNT, TRAJECTORY_LEN, QUERY_HEAD_COUNT * HEAD_SIZE), 1.0, 6.0, ((0, 8), (1, 64))),
        "local_keys": draw_local_keys(jax.random.fold_in(key_list[8], 71), 0),
        "trajectory_values": noise(key_list[3], (TRAJECTORY_COUNT, TRAJECTORY_LEN, KEY_VALUE_HEADS * HEAD_SIZE), 1.0, 6.0, ((0, 8), (1, 64))),
        "journal_keys": noise(key_list[4], (LOG_BLOCK_COUNT, LOG_BLOCK_TOKENS, KEY_VALUE_HEADS * HEAD_SIZE), 1.0, 6.0, ((0, 64),)),
        "journal_values": noise(key_list[5], (LOG_BLOCK_COUNT, LOG_BLOCK_TOKENS, KEY_VALUE_HEADS * HEAD_SIZE), 1.0, 6.0, ((0, 64),)),
        "picks": distinct(key_list[6], TRAJECTORY_COUNT * QB, LOG_BLOCK_COUNT, TOPK, 768).reshape((TRAJECTORY_COUNT, QB, TOPK)),
        "lengths": draw_lengths(jax.random.fold_in(key_list[8], 71), 0),
    }


def head_grads(query_head, grad_head, key_head, value_head, visible):
    score_scale = 1.0 / math.sqrt(HEAD_SIZE)
    query_wide = query_head.astype(jnp.float32)
    grad_wide = grad_head.astype(jnp.float32)
    key_wide = key_head.astype(jnp.float32)
    value_wide = value_head.astype(jnp.float32)
    scores = jnp.einsum('tgd,kd->gtk', query_wide, key_wide) * score_scale
    scores = jnp.where(visible[None], scores, -1e+30)
    top_score = lax.optimization_barrier(jnp.max(scores, axis=-1, keepdims=True))
    weights = jnp.exp(scores - top_score)
    probs_full = weights / lax.optimization_barrier(jnp.sum(weights, axis=-1, keepdims=True))
    probs_low = lax.optimization_barrier(probs_full.astype(jnp.bfloat16)).astype(jnp.float32)
    output = jnp.einsum('gtk,kd->tgd', probs_low, value_wide)
    row_delta = lax.optimization_barrier(jnp.sum(grad_wide * output, axis=-1))
    grad_probs = jnp.einsum('tgd,kd->gtk', grad_wide, value_wide)
    grad_scores = probs_full * (grad_probs - row_delta.T[:, :, None])
    grad_low = lax.optimization_barrier(grad_scores.astype(jnp.bfloat16)).astype(jnp.float32)
    grad_query = jnp.einsum('gtk,kd->tgd', grad_low, key_wide) * score_scale
    key_gradient = jnp.einsum('gtk,tgd->kd', grad_low, query_wide) * score_scale
    value_gradient = jnp.einsum('gtk,tgd->kd', probs_low, grad_wide)
    return (grad_query, key_gradient, value_gradient)

def block_grads(block_of_queries, block_gradient, block_of_keys, block_of_values, visible):
    count_of_keys = block_of_keys.shape[0]
    head_group = QUERY_HEAD_COUNT // KEY_VALUE_HEADS
    heads_of_queries = block_of_queries.reshape(QUERY_BLOCK_LEN, KEY_VALUE_HEADS, head_group, HEAD_SIZE).transpose(1, 0, 2, 3)
    heads_gradient = block_gradient.reshape(QUERY_BLOCK_LEN, KEY_VALUE_HEADS, head_group, HEAD_SIZE).transpose(1, 0, 2, 3)
    heads_of_keys = block_of_keys.reshape(count_of_keys, KEY_VALUE_HEADS, HEAD_SIZE).transpose(1, 0, 2)
    heads_of_values = block_of_values.reshape(count_of_keys, KEY_VALUE_HEADS, HEAD_SIZE).transpose(1, 0, 2)
    grad_query, key_gradient, value_gradient = lax.map(lambda head_parts: head_grads(head_parts[0], head_parts[1], head_parts[2], head_parts[3], visible), (heads_of_queries, heads_gradient, heads_of_keys, heads_of_values))
    grad_query = grad_query.transpose(1, 0, 2, 3).reshape(QUERY_BLOCK_LEN, QUERY_HEAD_COUNT * HEAD_SIZE)
    key_gradient = key_gradient.transpose(1, 0, 2).reshape(count_of_keys, KEY_VALUE_HEADS * HEAD_SIZE)
    value_gradient = value_gradient.transpose(1, 0, 2).reshape(count_of_keys, KEY_VALUE_HEADS * HEAD_SIZE)
    return (grad_query, key_gradient, value_gradient)

def reference(queries, out_grad, local_keys, trajectory_values, journal_keys, journal_values, picks, lengths):
    feature_axis = KEY_VALUE_HEADS * HEAD_SIZE
    causal = jnp.arange(QUERY_BLOCK_LEN, dtype=jnp.int32)[:, None] >= jnp.arange(QUERY_BLOCK_LEN, dtype=jnp.int32)[None, :]
    visible = jnp.concatenate([jnp.ones((QUERY_BLOCK_LEN, TOPK * LOG_BLOCK_TOKENS), dtype=bool), causal], axis=1)

    def step(totals, flat_index):
        sum_keys, sum_values = totals
        trajectory = flat_index // QB
        block_index = flat_index % QB
        first_row = (block_index * QUERY_BLOCK_LEN).astype(jnp.int32)
        block_of_queries = lax.dynamic_slice_in_dim(queries[trajectory], first_row, QUERY_BLOCK_LEN, 0)
        grad_raw = lax.dynamic_slice_in_dim(out_grad[trajectory], first_row, QUERY_BLOCK_LEN, 0)
        own_keys = lax.dynamic_slice_in_dim(local_keys[trajectory], first_row, QUERY_BLOCK_LEN, 0)
        own_values = lax.dynamic_slice_in_dim(trajectory_values[trajectory], first_row, QUERY_BLOCK_LEN, 0)
        live_rows = first_row + jnp.arange(QUERY_BLOCK_LEN, dtype=jnp.int32) < lengths[trajectory]
        block_gradient = jnp.where(live_rows[:, None], grad_raw, jnp.zeros_like(grad_raw))
        chosen = picks[trajectory, block_index]
        block_of_keys = jnp.concatenate([journal_keys[chosen].reshape(TOPK * LOG_BLOCK_TOKENS, feature_axis), own_keys], axis=0)
        block_of_values = jnp.concatenate([journal_values[chosen].reshape(TOPK * LOG_BLOCK_TOKENS, feature_axis), own_values], axis=0)
        grad_query, key_gradient, value_gradient = block_grads(block_of_queries, block_gradient, block_of_keys, block_of_values, visible)
        sum_keys = sum_keys.at[chosen].add(key_gradient[:TOPK * LOG_BLOCK_TOKENS].reshape(TOPK, LOG_BLOCK_TOKENS, feature_axis))
        sum_values = sum_values.at[chosen].add(value_gradient[:TOPK * LOG_BLOCK_TOKENS].reshape(TOPK, LOG_BLOCK_TOKENS, feature_axis))
        outputs = (grad_query.astype(jnp.bfloat16), key_gradient[TOPK * LOG_BLOCK_TOKENS:].astype(jnp.bfloat16), value_gradient[TOPK * LOG_BLOCK_TOKENS:].astype(jnp.bfloat16))
        return ((sum_keys, sum_values), outputs)
    start_sums = (jnp.zeros((LOG_BLOCK_COUNT, LOG_BLOCK_TOKENS, feature_axis), jnp.float32), jnp.zeros((LOG_BLOCK_COUNT, LOG_BLOCK_TOKENS, feature_axis), jnp.float32))
    (sum_keys, sum_values), (grad_q, grad_lk, grad_lv) = lax.scan(step, start_sums, jnp.arange(TRAJECTORY_COUNT * QB, dtype=jnp.int32))
    grad_queries = grad_q.reshape(TRAJECTORY_COUNT, TRAJECTORY_LEN, QUERY_HEAD_COUNT * HEAD_SIZE)
    grad_local_keys = grad_lk.reshape(TRAJECTORY_COUNT, TRAJECTORY_LEN, feature_axis)
    grad_local_values = grad_lv.reshape(TRAJECTORY_COUNT, TRAJECTORY_LEN, feature_axis)
    return (grad_queries, grad_local_keys, grad_local_values, sum_keys.astype(jnp.bfloat16), sum_values.astype(jnp.bfloat16))
```

```python
import functools
import math

import jax
import jax.numpy as jnp
from jax import lax
from jax.experimental import pallas as pl
from jax.experimental.pallas import tpu as pltpu
from jax.sharding import PartitionSpec as P

HEAD = 128
Y_CHIPS = 4
SCALE = 1.0 / math.sqrt(HEAD)
MESH = pl.DeviceIdType.MESH
BF16 = jnp.bfloat16
F32 = jnp.float32


def place(z_chips):
    ctx = lax.axis_index("ctx")
    return ctx // z_chips, ctx % z_chips, lax.axis_index("smp")


def peer_of(offset, y, smp, smp_size):
    half = smp_size // 2
    ds = offset % smp_size
    py = (y + offset // smp_size) % Y_CHIPS
    px = (smp // 2 + ds // 2) % half
    pc = (smp + ds) % 2
    return py, px * 2 + pc


def source_of(offset, y, smp, smp_size):
    half = smp_size // 2
    ds = offset % smp_size
    py = (y + Y_CHIPS - offset // smp_size) % Y_CHIPS
    px = (smp // 2 + half - ds // 2) % half
    pc = (smp + ds) % 2
    return py, px * 2 + pc


def enter(y, z, smp, z_chips, smp_size):
    barrier = pltpu.get_barrier_semaphore()
    count = Y_CHIPS * smp_size

    def greet(offset, carry):
        py, ps = peer_of(offset, y, smp, smp_size)
        pl.semaphore_signal(barrier, 1, device_id=(py * z_chips + z, ps), device_id_type=MESH)
        return carry

    for step in (1, z_chips - 1):
        pl.semaphore_signal(
            barrier,
            1,
            device_id=(y * z_chips + (z + step) % z_chips, smp),
            device_id_type=MESH,
        )
    lax.fori_loop(1, count, greet, 0)
    pl.semaphore_wait(barrier, count + 1)


def fetch_kernel(
    z_chips,
    smp_size,
    picks_ref,
    keys_ref,
    values_ref,
    out_ref,
    where_ref,
    log,
    staged,
    named,
    named_s,
    spread_send,
    spread_recv,
    own_sem,
    name_send,
    name_recv,
    smem_sem,
    ring_send,
    ring_recv,
    pick_send,
    pick_recv,
):
    y, z, smp = place(z_chips)
    planes = Y_CHIPS * smp_size
    mine = y * smp_size + smp
    rows = log.shape[2]
    cols = log.shape[3]
    per_array = planes // 2
    lane = lax.broadcasted_iota(jnp.int32, (1, 128), 1)
    named[mine] = jnp.where(
        lane == 0,
        picks_ref[0, 0, 0],
        jnp.where(lane == 1, picks_ref[0, 0, 1], picks_ref[0, 0, 2]),
    )
    enter(y, z, smp, z_chips, smp_size)

    def piece(ref, owner, c):
        row = pl.multiple_of((owner % per_array) * rows, rows)
        return ref.at[0, pl.ds(row, rows), pl.ds(c * cols, cols)]

    def spread(py, c, ref):
        return pltpu.make_async_remote_copy(
            src_ref=piece(ref, py * smp_size + smp, c),
            dst_ref=log.at[c, z * Y_CHIPS + y],
            send_sem=spread_send.at[c, py],
            recv_sem=spread_recv.at[c, y],
            device_id=(py * z_chips + z, smp),
            device_id_type=MESH,
        )

    def arrived(py, c):
        return pltpu.make_async_remote_copy(
            src_ref=piece(keys_ref, mine, c),
            dst_ref=log.at[c, z * Y_CHIPS + py],
            send_sem=spread_send.at[c, py],
            recv_sem=spread_recv.at[c, py],
            device_id=(py * z_chips + z, smp),
            device_id_type=MESH,
        )

    def own(c, ref):
        return pltpu.make_async_copy(
            piece(ref, mine, c), log.at[c, z * Y_CHIPS + y], own_sem.at[c]
        )

    for c in range(2):
        for dy in range(1, Y_CHIPS):
            py = (y + dy) % Y_CHIPS

            @pl.when(py < Y_CHIPS // 2)
            def _():
                spread(py, c, keys_ref).start()

            @pl.when(py >= Y_CHIPS // 2)
            def _():
                spread(py, c, values_ref).start()

        @pl.when(y < Y_CHIPS // 2)
        def _():
            own(c, keys_ref).start()

        @pl.when(y >= Y_CHIPS // 2)
        def _():
            own(c, values_ref).start()

    def name(target, slot_send, slot_recv):
        py, ps = target
        return pltpu.make_async_remote_copy(
            src_ref=named.at[mine],
            dst_ref=named.at[slot_recv],
            send_sem=name_send.at[slot_send],
            recv_sem=name_recv.at[slot_recv],
            device_id=(py * z_chips + z, ps),
            device_id_type=MESH,
        )

    def tell(offset, carry):
        py, ps = peer_of(offset, y, smp, smp_size)
        name((py, ps), py * smp_size + ps, mine).start()
        return carry

    lax.fori_loop(1, planes, tell, 0)

    def ring(c, way, step):
        slot = (z + z_chips - step) % z_chips if way == 0 else (z + step) % z_chips
        to = (z + 1) % z_chips if way == 0 else (z + z_chips - 1) % z_chips
        part = log.at[c, pl.ds(slot * Y_CHIPS, Y_CHIPS)]
        return pltpu.make_async_remote_copy(
            src_ref=part,
            dst_ref=part,
            send_sem=ring_send.at[c, way, min(step, z_chips // 2 - 1)],
            recv_sem=ring_recv.at[c, slot],
            device_id=(y * z_chips + to, smp),
            device_id_type=MESH,
        )

    for c in range(2):
        for dy in range(1, Y_CHIPS):
            arrived((y + dy) % Y_CHIPS, c).wait_recv()
        own(c, keys_ref).wait()
        for way in range(2):
            ring(c, way, 0).start()
    half = z_chips // 2
    for step in range(1, half + 1):
        for c in range(2):
            for way in range(2):
                last = half if way == c else half - 1
                if step <= last:
                    arriving = ring(c, way, step)
                    arriving.wait_recv()
                    if step < last:
                        arriving.start()

    def told(offset, carry):
        py, ps = source_of(offset, y, smp, smp_size)
        name((py, ps), py * smp_size + ps, py * smp_size + ps).wait_recv()
        return carry

    lax.fori_loop(1, planes, told, 0)
    to_smem = pltpu.make_async_copy(named, named_s, smem_sem)
    to_smem.start()
    to_smem.wait()

    def give(c, target, slot_send, slot_recv):
        py, ps = target
        return pltpu.make_async_remote_copy(
            src_ref=staged.at[c, slot_send],
            dst_ref=out_ref.at[c, slot_recv],
            send_sem=pick_send.at[c, slot_send],
            recv_sem=pick_recv.at[c, slot_recv],
            device_id=(py * z_chips + z, ps),
            device_id_type=MESH,
        )

    def stage(target):
        for i in range(3):
            block = named_s[target, 0, i]
            at = (block % z_chips) * Y_CHIPS + block // z_chips
            for c in range(2):
                staged[c, target, i] = log[c, at]

    def send_picks(offset, carry):
        py, ps = peer_of(offset, y, smp, smp_size)
        target = py * smp_size + ps
        stage(target)
        for c in range(2):
            give(c, (py, ps), target, mine).start()
        return carry

    lax.fori_loop(1, planes, send_picks, 0)
    stage(mine)
    keep = [
        pltpu.make_async_copy(staged.at[c, mine], out_ref.at[c, mine], own_sem.at[c])
        for c in range(2)
    ]
    for c in range(2):
        keep[c].start()

    def locate(k, carry):
        found = jnp.full((1, 128), 3 * planes, jnp.int32)
        for i in range(3):
            found = jnp.where(lane == named_s[k, 0, i], 3 * k + i, found)
        where_ref[k] = found
        return carry

    lax.fori_loop(0, planes, locate, 0)

    for c in range(2):
        for dy in range(1, Y_CHIPS):
            spread((y + dy) % Y_CHIPS, c, keys_ref).wait_send()
        for way in range(2):
            for step in range(half if way == c else half - 1):
                ring(c, way, step).wait_send()

    def finish(offset, carry):
        py, ps = peer_of(offset, y, smp, smp_size)
        target = py * smp_size + ps
        name((py, ps), target, mine).wait_send()
        for c in range(2):
            give(c, (py, ps), target, mine).wait_send()
        sy, ss = source_of(offset, y, smp, smp_size)
        source = sy * smp_size + ss
        for c in range(2):
            give(c, (sy, ss), source, source).wait_recv()
        return carry

    lax.fori_loop(1, planes, finish, 0)
    for c in range(2):
        keep[c].wait()


def grads_kernel(
    length_ref,
    queries_ref,
    grad_ref,
    own_keys_ref,
    own_values_ref,
    fetched_ref,
    grad_queries_ref,
    grad_keys_ref,
    grad_values_ref,
    strips_ref,
    scores,
    grad_probs,
):
    tq = queries_ref.shape[1]
    group = queries_ref.shape[2] // HEAD
    width = group * tq
    planes = fetched_ref.shape[1]
    half = planes // 2
    live_rows = length_ref[0] - lax.axis_index("ctx") * tq
    live = lax.broadcasted_iota(jnp.int32, (tq, HEAD), 0) < live_rows
    heads_q = []
    heads_g = []
    for h in range(group):
        heads_q.append(queries_ref[0, :, h * HEAD : (h + 1) * HEAD])
        raw = grad_ref[0, :, h * HEAD : (h + 1) * HEAD]
        heads_g.append(jnp.where(live, raw, jnp.zeros_like(raw)))
    q = jnp.concatenate(heads_q, axis=0)
    g = jnp.concatenate(heads_g, axis=0)

    def keys_of(i):
        if i == 3:
            return own_keys_ref[0]
        return fetched_ref[0, :half, i].reshape(tq, HEAD)

    def values_of(i):
        if i == 3:
            return own_values_ref[0]
        return fetched_ref[0, half:, i].reshape(tq, HEAD)

    across = (((1,), (1,)), ((), ()))
    top = None
    for i in range(4):
        s = lax.dot_general(keys_of(i), q, across, preferred_element_type=F32)
        if i == 3:
            row = lax.broadcasted_iota(jnp.int32, (tq, width), 0)
            col = lax.broadcasted_iota(jnp.int32, (tq, width), 1) % tq
            s = jnp.where(col >= row, s, -1e30)
        scores[i] = s
        best = jnp.max(s, axis=0, keepdims=True)
        top = best if top is None else jnp.maximum(top, best)
        grad_probs[i] = lax.dot_general(values_of(i), g, across, preferred_element_type=F32)
    total = jnp.zeros((1, width), F32)
    delta = jnp.zeros((1, width), F32)
    for i in range(4):
        w = jnp.exp((scores[i] - top) * SCALE)
        scores[i] = w
        total = total + jnp.sum(w, axis=0, keepdims=True)
        delta = delta + jnp.sum(w * grad_probs[i], axis=0, keepdims=True)
    inverse = 1.0 / total
    delta = delta * inverse
    dq = None
    lane = lax.broadcasted_iota(jnp.int32, (tq, HEAD), 1)
    low = lane < HEAD // 2
    for i in range(4):
        probs = scores[i] * inverse
        grad_low = (probs * (grad_probs[i] - delta)).astype(BF16)
        probs_low = probs.astype(BF16)
        dv = jnp.dot(probs_low, g, preferred_element_type=F32)
        dk = jnp.dot(grad_low, q, preferred_element_type=F32) * SCALE
        part = lax.dot_general(
            grad_low, keys_of(i), (((0,), (0,)), ((), ())), preferred_element_type=F32
        )
        dq = part if dq is None else dq + part
        if i == 3:
            grad_keys_ref[0] = dk.astype(BF16)
            grad_values_ref[0] = dv.astype(BF16)
        else:
            first = jnp.where(low, dk, pltpu.roll(dv, HEAD // 2, 1))
            second = jnp.where(low, pltpu.roll(dk, HEAD // 2, 1), dv)
            strips_ref[0, :, i] = first.astype(BF16).reshape(Y_CHIPS, tq // Y_CHIPS, HEAD)
            strips_ref[1, :, i] = second.astype(BF16).reshape(Y_CHIPS, tq // Y_CHIPS, HEAD)
    for h in range(group):
        grad_queries_ref[0, :, h * HEAD : (h + 1) * HEAD] = (
            dq[h * tq : (h + 1) * tq] * SCALE
        ).astype(BF16)


def reduce_kernel(
    z_chips,
    smp_size,
    where_ref,
    strips_ref,
    out_ref,
    held,
    part,
    sending,
    arriving,
    final,
    give_send,
    give_recv,
    own_sem,
    ring_send,
    ring_recv,
    last_send,
    last_recv,
):
    y, z, smp = place(z_chips)
    planes = Y_CHIPS * smp_size
    mine = y * smp_size + smp
    half = z_chips // 2
    enter(y, z, smp, z_chips, smp_size)

    def give(target, slot_send, slot_recv):
        py, ps = target
        return pltpu.make_async_remote_copy(
            src_ref=strips_ref.at[ps, py],
            dst_ref=held.at[pl.ds(3 * slot_recv, 3)],
            send_sem=give_send.at[slot_send],
            recv_sem=give_recv.at[slot_recv],
            device_id=(py * z_chips + z, ps),
            device_id_type=MESH,
        )

    def send(offset, carry):
        py, ps = peer_of(offset, y, smp, smp_size)
        give((py, ps), py * smp_size + ps, mine).start()
        return carry

    lax.fori_loop(1, planes, send, 0)
    keep = pltpu.make_async_copy(
        strips_ref.at[smp, y], held.at[pl.ds(3 * mine, 3)], own_sem.at[0]
    )
    keep.start()
    held[3 * planes] = jnp.zeros(held.shape[1:], BF16)

    def receive(offset, carry):
        sy, ss = source_of(offset, y, smp, smp_size)
        source = sy * smp_size + ss
        give((sy, ss), source, source).wait_recv()
        return carry

    lax.fori_loop(1, planes, receive, 0)
    keep.wait()

    def contribute(dest):
        def block(yb, carry):
            b = yb * z_chips + dest
            acc = held[where_ref[0, 0, b]].astype(F32)
            for k in range(1, planes):
                acc = acc + held[where_ref[k, 0, b]].astype(F32)
            part[yb] = acc
            return carry

        lax.fori_loop(0, Y_CHIPS, block, 0)

    def ring(way, step):
        to = (z + z_chips - 1) % z_chips if way == 0 else (z + 1) % z_chips
        return pltpu.make_async_remote_copy(
            src_ref=sending.at[way, step],
            dst_ref=arriving.at[way, step],
            send_sem=ring_send.at[way, step],
            recv_sem=ring_recv.at[way, step],
            device_id=(y * z_chips + to, smp),
            device_id_type=MESH,
        )

    def dest_of(way, step):
        far = half - step
        return (z + z_chips - far) % z_chips if way == 0 else (z + far) % z_chips

    def advance(way, step, first):
        contribute(dest_of(way, step))
        if first:
            sending[way, step] = part[...].astype(BF16)
        else:
            ring(way, step - 1).wait_recv()
            sending[way, step] = (part[...] + arriving[way, step - 1].astype(F32)).astype(BF16)
        ring(way, step).start()

    advance(0, 0, True)
    advance(1, 1, True)
    advance(0, 1, False)

    def both(step, carry):
        advance(1, step, False)
        advance(0, step, False)
        return carry

    lax.fori_loop(2, half, both, 0)
    contribute(z)
    for way in range(2):
        ring(way, half - 1).wait_recv()
    final[...] = (
        part[...]
        + arriving[0, half - 1].astype(F32)
        + arriving[1, half - 1].astype(F32)
    ).astype(BF16)

    rows = final.shape[1]

    def last(py, slot_recv):
        return pltpu.make_async_remote_copy(
            src_ref=final.at[py],
            dst_ref=out_ref.at[pl.ds(pl.multiple_of(slot_recv * rows, rows), rows)],
            send_sem=last_send.at[py],
            recv_sem=last_recv.at[slot_recv],
            device_id=(py * z_chips + z, smp),
            device_id_type=MESH,
        )

    for dy in range(1, Y_CHIPS):
        last((y + dy) % Y_CHIPS, y).start()
    out_ref[pl.ds(pl.multiple_of(y * rows, rows), rows)] = final[y]

    def finish(offset, carry):
        py, ps = peer_of(offset, y, smp, smp_size)
        give((py, ps), py * smp_size + ps, mine).wait_send()
        return carry

    lax.fori_loop(1, planes, finish, 0)
    for step in range(half):
        ring(0, step).wait_send()
        if step > 0:
            ring(1, step).wait_send()
    for dy in range(1, Y_CHIPS):
        last((y + dy) % Y_CHIPS, y).wait_send()
        py = (y + dy) % Y_CHIPS
        last(py, py).wait_recv()


def body(
    queries, out_grad, local_keys, trajectory_values, journal_keys, journal_values, picks, lengths
):
    smp_size = lax.axis_size("smp")
    z_chips = lax.axis_size("ctx") // Y_CHIPS
    planes = Y_CHIPS * smp_size
    block_rows, features = journal_keys.shape[1:]
    kv_heads = features // HEAD
    blocks = Y_CHIPS * z_chips
    rows = 2 * block_rows // planes
    cols = features // 2
    tq = queries.shape[1]
    wide = queries.shape[2] // kv_heads
    dma = pltpu.SemaphoreType.DMA
    any_space = pl.BlockSpec(memory_space=pl.ANY)
    in_smem = pl.BlockSpec(memory_space=pltpu.SMEM)
    in_vmem = pl.BlockSpec(memory_space=pltpu.VMEM)

    fetched, where = pl.pallas_call(
        functools.partial(fetch_kernel, z_chips, smp_size),
        out_shape=(
            jax.ShapeDtypeStruct((2, planes, 3, rows, cols), BF16),
            jax.ShapeDtypeStruct((planes, 1, 128), jnp.int32),
        ),
        in_specs=[in_smem, any_space, any_space],
        out_specs=(any_space, in_vmem),
        scratch_shapes=[
            pltpu.VMEM((2, blocks, rows, cols), BF16),
            pltpu.VMEM((2, planes, 3, rows, cols), BF16),
            pltpu.VMEM((planes, 1, 128), jnp.int32),
            pltpu.SMEM((planes, 1, 128), jnp.int32),
            dma((2, Y_CHIPS)),
            dma((2, Y_CHIPS)),
            dma((2,)),
            dma((planes,)),
            dma((planes,)),
            dma,
            dma((2, 2, z_chips // 2)),
            dma((2, z_chips)),
            dma((2, planes)),
            dma((2, planes)),
        ],
        compiler_params=pltpu.CompilerParams(
            collective_id=0, has_side_effects=True, vmem_limit_bytes=24 << 20
        ),
        name="fetch",
    )(picks, journal_keys, journal_values)

    head_wide = pl.BlockSpec((1, tq, wide), lambda g: (0, 0, g))
    head_narrow = pl.BlockSpec((1, tq, HEAD), lambda g: (0, 0, g))
    half_heads = kv_heads // 2
    grad_queries, grad_local_keys, grad_local_values, strips = pl.pallas_call(
        grads_kernel,
        grid=(kv_heads,),
        out_shape=(
            jax.ShapeDtypeStruct(queries.shape, BF16),
            jax.ShapeDtypeStruct(local_keys.shape, BF16),
            jax.ShapeDtypeStruct(local_keys.shape, BF16),
            jax.ShapeDtypeStruct((smp_size, Y_CHIPS, 3, tq // Y_CHIPS, HEAD), BF16),
        ),
        in_specs=[
            in_smem,
            head_wide,
            head_wide,
            head_narrow,
            head_narrow,
            pl.BlockSpec(
                (1, planes, 3, rows, HEAD), lambda g: (g // half_heads, 0, 0, 0, g % half_heads)
            ),
        ],
        out_specs=(
            head_wide,
            head_narrow,
            head_narrow,
            pl.BlockSpec((2, Y_CHIPS, 3, tq // Y_CHIPS, HEAD), lambda g: (g, 0, 0, 0, 0)),
        ),
        scratch_shapes=[
            pltpu.VMEM((4, tq, wide // HEAD * tq), F32),
            pltpu.VMEM((4, tq, wide // HEAD * tq), F32),
        ],
        compiler_params=pltpu.CompilerParams(vmem_limit_bytes=48 << 20),
        name="grads",
    )(lengths, queries, out_grad, local_keys, trajectory_values, fetched)

    piece = (tq // Y_CHIPS, HEAD)
    half = z_chips // 2
    summed = pl.pallas_call(
        functools.partial(reduce_kernel, z_chips, smp_size),
        out_shape=jax.ShapeDtypeStruct((block_rows, HEAD), BF16),
        in_specs=[in_smem, any_space],
        out_specs=in_vmem,
        scratch_shapes=[
            pltpu.VMEM((3 * planes + 1, *piece), BF16),
            pltpu.VMEM((Y_CHIPS, *piece), F32),
            pltpu.VMEM((2, half, Y_CHIPS, *piece), BF16),
            pltpu.VMEM((2, half, Y_CHIPS, *piece), BF16),
            pltpu.VMEM((Y_CHIPS, *piece), BF16),
            dma((planes,)),
            dma((planes,)),
            dma((1,)),
            dma((2, half)),
            dma((2, half)),
            dma((Y_CHIPS,)),
            dma((Y_CHIPS,)),
        ],
        compiler_params=pltpu.CompilerParams(
            collective_id=1, has_side_effects=True, vmem_limit_bytes=24 << 20
        ),
        name="reduce",
    )(where, strips)
    return (
        grad_queries,
        grad_local_keys,
        grad_local_values,
        summed[None, :, : HEAD // 2],
        summed[None, :, HEAD // 2 :],
    )


def solution(mesh):
    in_specs = (
        P("smp", "ctx", None),
        P("smp", "ctx", None),
        P("smp", "ctx", None),
        P("smp", "ctx", None),
        P("ctx", None, None),
        P("ctx", None, None),
        P("smp", "ctx", None),
        P("smp"),
    )
    out_specs = (
        P("smp", "ctx", None),
        P("smp", "ctx", None),
        P("smp", "ctx", None),
        P("ctx", None, "smp"),
        P("ctx", None, "smp"),
    )
    return jax.shard_map(body, mesh=mesh, in_specs=in_specs, out_specs=out_specs, check_vma=False)
```

```python
import functools
import math

import jax
import jax.numpy as jnp
from jax import lax
from jax.experimental import pallas as pl
from jax.experimental.pallas import tpu as pltpu
from jax.sharding import PartitionSpec as P

HEAD = 128
Y_CHIPS = 4
SCALE = 1.0 / math.sqrt(HEAD)
CHUNKS = 2
TOP = 3
MESH = pl.DeviceIdType.MESH
BF16 = jnp.bfloat16
F32 = jnp.float32


def place(z_chips):
    ctx = lax.axis_index("ctx")
    return ctx // z_chips, ctx % z_chips, lax.axis_index("smp")


def peer_of(offset, y, smp, smp_size):
    half = smp_size // 2
    ds = offset % smp_size
    py = (y + offset // smp_size) % Y_CHIPS
    px = (smp // 2 + ds // 2) % half
    pc = (smp + ds) % 2
    return py, px * 2 + pc


def source_of(offset, y, smp, smp_size):
    half = smp_size // 2
    ds = offset % smp_size
    py = (y + Y_CHIPS - offset // smp_size) % Y_CHIPS
    px = (smp // 2 + half - ds // 2) % half
    pc = (smp + ds) % 2
    return py, px * 2 + pc


def enter(y, z, smp, z_chips, smp_size):
    barrier = pltpu.get_barrier_semaphore()
    count = Y_CHIPS * smp_size

    def greet(offset, carry):
        py, ps = peer_of(offset, y, smp, smp_size)
        pl.semaphore_signal(barrier, 1, device_id=(py * z_chips + z, ps), device_id_type=MESH)
        return carry

    for step in (1, z_chips - 1):
        pl.semaphore_signal(
            barrier,
            1,
            device_id=(y * z_chips + (z + step) % z_chips, smp),
            device_id_type=MESH,
        )
    lax.fori_loop(1, count, greet, 0)
    pl.semaphore_wait(barrier, count + 1)


def fused_kernel(
    z_chips,
    smp_size,
    picks_ref,
    length_ref,
    queries_ref,
    grad_ref,
    own_keys_ref,
    own_values_ref,
    keys_ref,
    values_ref,
    grad_queries_ref,
    grad_keys_ref,
    grad_values_ref,
    out_ref,
    log_0,
    log_1,
    staged,
    fetched,
    named,
    named_s,
    where_v,
    where_s,
    q_all,
    g_all,
    k_own,
    v_own,
    dq_all,
    dk_own,
    dv_own,
    scores,
    grad_probs,
    strips,
    held_0,
    held_1,
    part,
    sending,
    arriving,
    final,
    gathered,
    load_sem,
    store_sem,
    spread_send,
    spread_recv,
    own_sem,
    name_send,
    name_recv,
    smem_sem,
    ring_send,
    ring_recv,
    pick_send,
    pick_recv,
    give_send,
    give_recv,
    back_send,
    back_recv,
    last_send,
    last_recv,
):
    y, z, smp = place(z_chips)
    planes = Y_CHIPS * smp_size
    mine = y * smp_size + smp
    log = (log_0, log_1)
    held = (held_0, held_1)
    rows, cols = log_0.shape[1:]
    per_array = planes // 2
    half = z_chips // 2
    chunk_heads = cols // HEAD
    tq = q_all.shape[0]
    group = q_all.shape[1] // (CHUNKS * cols)
    width = group * tq
    lane = lax.broadcasted_iota(jnp.int32, (1, 128), 1)

    loads = [
        pltpu.make_async_copy(ref.at[0], scratch, load_sem.at[n])
        for n, (ref, scratch) in enumerate(
            (
                (queries_ref, q_all),
                (grad_ref, g_all),
                (own_keys_ref, k_own),
                (own_values_ref, v_own),
            )
        )
    ]
    named[mine] = jnp.where(
        lane == 0,
        picks_ref[0, 0, 0],
        jnp.where(lane == 1, picks_ref[0, 0, 1], picks_ref[0, 0, 2]),
    )
    enter(y, z, smp, z_chips, smp_size)

    def piece(ref, owner, c):
        row = pl.multiple_of((owner % per_array) * rows, rows)
        return ref.at[0, pl.ds(row, rows), pl.ds(c * cols, cols)]

    def spread(py, c, ref):
        return pltpu.make_async_remote_copy(
            src_ref=piece(ref, py * smp_size + smp, c),
            dst_ref=log[c].at[z * Y_CHIPS + y],
            send_sem=spread_send.at[c, py],
            recv_sem=spread_recv.at[c, y],
            device_id=(py * z_chips + z, smp),
            device_id_type=MESH,
        )

    def spread_in(py, c):
        return pltpu.make_async_remote_copy(
            src_ref=piece(keys_ref, mine, c),
            dst_ref=log[c].at[z * Y_CHIPS + py],
            send_sem=spread_send.at[c, py],
            recv_sem=spread_recv.at[c, py],
            device_id=(py * z_chips + z, smp),
            device_id_type=MESH,
        )

    def own(c, ref):
        return pltpu.make_async_copy(
            piece(ref, mine, c), log[c].at[z * Y_CHIPS + y], own_sem.at[c]
        )

    for c in range(CHUNKS):
        for dy in range(1, Y_CHIPS):
            py = (y + dy) % Y_CHIPS

            @pl.when(py < Y_CHIPS // 2)
            def _():
                spread(py, c, keys_ref).start()

            @pl.when(py >= Y_CHIPS // 2)
            def _():
                spread(py, c, values_ref).start()

        @pl.when(y < Y_CHIPS // 2)
        def _():
            own(c, keys_ref).start()

        @pl.when(y >= Y_CHIPS // 2)
        def _():
            own(c, values_ref).start()

    def name(target, slot_send, slot_recv):
        py, ps = target
        return pltpu.make_async_remote_copy(
            src_ref=named.at[mine],
            dst_ref=named.at[slot_recv],
            send_sem=name_send.at[slot_send],
            recv_sem=name_recv.at[slot_recv],
            device_id=(py * z_chips + z, ps),
            device_id_type=MESH,
        )

    def tell(offset, carry):
        py, ps = peer_of(offset, y, smp, smp_size)
        name((py, ps), py * smp_size + ps, mine).start()
        return carry

    lax.fori_loop(1, planes, tell, 0)
    for load in loads:
        load.start()

    def ring(c, way, step):
        slot = (z + z_chips - step) % z_chips if way == 0 else (z + step) % z_chips
        to = (z + 1) % z_chips if way == 0 else (z + z_chips - 1) % z_chips
        those = log[c].at[pl.ds(slot * Y_CHIPS, Y_CHIPS)]
        return pltpu.make_async_remote_copy(
            src_ref=those,
            dst_ref=those,
            send_sem=ring_send.at[c, way, min(step, half - 1)],
            recv_sem=ring_recv.at[c, slot],
            device_id=(y * z_chips + to, smp),
            device_id_type=MESH,
        )

    def ring_steps(c, way):
        return half if way == c % 2 else half - 1

    def begin(c):
        for dy in range(1, Y_CHIPS):
            spread_in((y + dy) % Y_CHIPS, c).wait_recv()
        own(c, keys_ref).wait()
        for way in range(2):
            ring(c, way, 0).start()

    def relay(c, step):
        for way in range(2):
            if step <= ring_steps(c, way):
                come = ring(c, way, step)
                come.wait_recv()
                if step < ring_steps(c, way):
                    come.start()

    def told(offset, carry):
        py, ps = source_of(offset, y, smp, smp_size)
        name((py, ps), py * smp_size + ps, py * smp_size + ps).wait_recv()
        return carry

    def locate(k, carry):
        found = jnp.full((1, 128), TOP * planes, jnp.int32)
        for i in range(TOP):
            found = jnp.where(lane == named_s[k, 0, i], TOP * k + i, found)
        where_v[k] = found
        return carry

    def give(c, target, slot_send, slot_recv):
        py, ps = target
        return pltpu.make_async_remote_copy(
            src_ref=staged.at[c, slot_send],
            dst_ref=fetched.at[c, slot_recv],
            send_sem=pick_send.at[c, slot_send],
            recv_sem=pick_recv.at[c, slot_recv],
            device_id=(py * z_chips + z, ps),
            device_id_type=MESH,
        )

    def place_of(target, i):
        block = named_s[target, 0, i]
        return (block % z_chips) * Y_CHIPS + block // z_chips

    def send_picks(c, first, end):
        def one(offset, carry):
            py, ps = peer_of(offset, y, smp, smp_size)
            target = py * smp_size + ps
            for i in range(TOP):
                staged[c, target, i] = log[c][place_of(target, i)]
            give(c, (py, ps), target, mine).start()
            return carry

        lax.fori_loop(first, end, one, 0)

    def keep_picks(c):
        for i in range(TOP):
            fetched[c, mine, i] = log[c][place_of(mine, i)]

    def take_picks(c):
        def one(offset, carry):
            py, ps = source_of(offset, y, smp, smp_size)
            source = py * smp_size + ps
            give(c, (py, ps), source, source).wait_recv()
            return carry

        lax.fori_loop(1, planes, one, 0)

    def grads(c):
        live_rows = length_ref[0] - lax.axis_index("ctx") * tq
        live = lax.broadcasted_iota(jnp.int32, (tq, HEAD), 0) < live_rows
        across = (((1,), (1,)), ((), ()))
        down = (((0,), (0,)), ((), ()))

        def one(n, carry):
            inner = pl.ds(pl.multiple_of(n * HEAD, HEAD), HEAD)
            lanes = pl.ds(pl.multiple_of(c * cols + n * HEAD, HEAD), HEAD)
            base = (c * chunk_heads + n) * group * HEAD
            wide = [pl.ds(pl.multiple_of(base + h * HEAD, HEAD), HEAD) for h in range(group)]
            q = jnp.concatenate([q_all[:, w] for w in wide], axis=0)
            raw = [g_all[:, w] for w in wide]
            g = jnp.concatenate([jnp.where(live, r, jnp.zeros_like(r)) for r in raw], axis=0)

            def keys_of(i):
                if i == TOP:
                    return k_own[:, lanes]
                return fetched[c, :per_array, i, :, inner].reshape(tq, HEAD)

            def values_of(i):
                if i == TOP:
                    return v_own[:, lanes]
                return fetched[c, per_array:, i, :, inner].reshape(tq, HEAD)

            top = None
            for i in range(TOP + 1):
                s = lax.dot_general(keys_of(i), q, across, preferred_element_type=F32)
                if i == TOP:
                    row = lax.broadcasted_iota(jnp.int32, (tq, width), 0)
                    col = lax.broadcasted_iota(jnp.int32, (tq, width), 1) % tq
                    s = jnp.where(col >= row, s, -1e30)
                scores[i] = s
                best = jnp.max(s, axis=0, keepdims=True)
                top = best if top is None else jnp.maximum(top, best)
                grad_probs[i] = lax.dot_general(
                    values_of(i), g, across, preferred_element_type=F32
                )
            total = jnp.zeros((1, width), F32)
            delta = jnp.zeros((1, width), F32)
            for i in range(TOP + 1):
                w = jnp.exp((scores[i] - top) * SCALE)
                scores[i] = w
                total = total + jnp.sum(w, axis=0, keepdims=True)
                delta = delta + jnp.sum(w * grad_probs[i], axis=0, keepdims=True)
            inverse = 1.0 / total
            delta = delta * inverse
            dq = None
            for i in range(TOP + 1):
                probs = scores[i] * inverse
                grad_low = (probs * (grad_probs[i] - delta)).astype(BF16)
                probs_low = probs.astype(BF16)
                dv = jnp.dot(probs_low, g, preferred_element_type=F32).astype(BF16)
                dk = jnp.dot(grad_low, q, preferred_element_type=F32) * SCALE
                dk = dk.astype(BF16)
                some = lax.dot_general(grad_low, keys_of(i), down, preferred_element_type=F32)
                dq = some if dq is None else dq + some
                if i == TOP:
                    dk_own[:, lanes] = dk
                    dv_own[:, lanes] = dv
                else:
                    strips[c, :per_array, i, :, inner] = dk.reshape(per_array, rows, HEAD)
                    strips[c, per_array:, i, :, inner] = dv.reshape(per_array, rows, HEAD)
            for h in range(group):
                dq_all[:, wide[h]] = (dq[h * tq : (h + 1) * tq] * SCALE).astype(BF16)
            return carry

        lax.fori_loop(0, chunk_heads, one, 0)

    def back(c, target, slot_send, slot_recv):
        py, ps = target
        return pltpu.make_async_remote_copy(
            src_ref=strips.at[c, slot_send],
            dst_ref=held[c].at[pl.ds(TOP * slot_recv, TOP)],
            send_sem=give_send.at[c, slot_send],
            recv_sem=give_recv.at[c, slot_recv],
            device_id=(py * z_chips + z, ps),
            device_id_type=MESH,
        )

    def send_partials(c):
        def one(offset, carry):
            py, ps = peer_of(offset, y, smp, smp_size)
            back(c, (py, ps), py * smp_size + ps, mine).start()
            return carry

        lax.fori_loop(1, planes, one, 0)
        for i in range(TOP):
            held[c][TOP * mine + i] = strips[c, mine, i]

    def take_partials(c):
        def one(offset, carry):
            py, ps = source_of(offset, y, smp, smp_size)
            source = py * smp_size + ps
            back(c, (py, ps), source, source).wait_recv()
            return carry

        lax.fori_loop(1, planes, one, 0)

    def contribute(c, way, dest):
        def block(yb, carry):
            b = yb * z_chips + dest
            acc = held[c][where_s[0, 0, b]].astype(F32)
            for k in range(1, planes):
                acc = acc + held[c][where_s[k, 0, b]].astype(F32)
            part[way, yb] = acc
            return carry

        lax.fori_loop(0, Y_CHIPS, block, 0)

    def ring_back(c, way, step):
        to = (z + z_chips - 1) % z_chips if way == 0 else (z + 1) % z_chips
        return pltpu.make_async_remote_copy(
            src_ref=sending.at[c, way, step],
            dst_ref=arriving.at[c, way, step],
            send_sem=back_send.at[c, way, step],
            recv_sem=back_recv.at[c, way, step],
            device_id=(y * z_chips + to, smp),
            device_id_type=MESH,
        )

    def first_step(c, way):
        return 0 if way == c % 2 else 1

    def relay_back(c, step):
        ways = [way for way in range(2) if step >= first_step(c, way)]
        for way in ways:
            far = half - step
            contribute(
                c, way, (z + z_chips - far) % z_chips if way == 0 else (z + far) % z_chips
            )
        for way in ways:
            if step == first_step(c, way):
                sending[c, way, step] = part[way].astype(BF16)
            else:
                ring_back(c, way, step - 1).wait_recv()
                sending[c, way, step] = (
                    part[way] + arriving[c, way, step - 1].astype(F32)
                ).astype(BF16)
            ring_back(c, way, step).start()

    def last(c, py, ps, slot_send, slot_recv):
        return pltpu.make_async_remote_copy(
            src_ref=final.at[c, (ps // 2) % chunk_heads, py],
            dst_ref=gathered.at[slot_recv],
            send_sem=last_send.at[slot_send],
            recv_sem=last_recv.at[slot_recv],
            device_id=(py * z_chips + z, ps),
            device_id_type=MESH,
        )

    owners = smp_size // CHUNKS

    def owner_of(c, n):
        return (y + n // owners) % Y_CHIPS, c * owners + (smp + n) % owners

    def close(c):
        contribute(c, 0, z)
        for way in range(2):
            ring_back(c, way, half - 1).wait_recv()
        whole = (
            part[0]
            + arriving[c, 0, half - 1].astype(F32)
            + arriving[c, 1, half - 1].astype(F32)
        ).astype(BF16)
        for n in range(chunk_heads):
            final[c, n] = whole[:, :, n * HEAD : (n + 1) * HEAD]

        def one(n, carry):
            py, ps = owner_of(c, n)
            target = py * smp_size + ps

            @pl.when(target != mine)
            def _():
                last(c, py, ps, target, mine).start()

            return carry

        lax.fori_loop(0, Y_CHIPS * owners, one, 0)

    def stores(c):
        narrow = pl.ds(c * cols, cols)
        wide = pl.ds(c * cols * group, cols * group)
        return [
            pltpu.make_async_copy(
                scratch.at[:, part_of], ref.at[0, :, part_of], store_sem.at[c, n]
            )
            for n, (scratch, ref, part_of) in enumerate(
                (
                    (dq_all, grad_queries_ref, wide),
                    (dk_own, grad_keys_ref, narrow),
                    (dv_own, grad_values_ref, narrow),
                )
            )
        ]

    lag = 2
    begin(0)
    begin(1)
    lax.fori_loop(1, planes, told, 0)
    to_smem = pltpu.make_async_copy(named, named_s, smem_sem.at[0])
    to_smem.start()
    for step in range(1, half + 1):
        relay(0, step)
        if step > lag:
            relay(1, step - lag)
        if step == 1:
            to_smem.wait()
    lead = planes // (lag + 1)
    send_picks(0, 1, lead)
    for n in range(lag):
        relay(1, half - lag + 1 + n)
        send_picks(0, lead * (n + 1), planes if n == lag - 1 else lead * (n + 2))
    keep_picks(0)
    send_picks(1, 1, planes)
    keep_picks(1)
    lax.fori_loop(0, planes, locate, 0)
    where_copy = pltpu.make_async_copy(where_v, where_s, smem_sem.at[1])
    where_copy.start()
    for c in range(CHUNKS):
        held[c][TOP * planes] = jnp.zeros((rows, cols), BF16)
    for load in loads:
        load.wait()
    take_picks(0)
    grads(0)
    send_partials(0)
    for copy in stores(0):
        copy.start()
    take_picks(1)
    grads(1)
    send_partials(1)
    for copy in stores(1):
        copy.start()
    where_copy.wait()
    take_partials(0)
    back_lag = 3
    for step in range(half + back_lag):
        if step < half:
            relay_back(0, step)
        if step == half:
            close(0)
        if step == back_lag:
            take_partials(1)
        if step >= back_lag:
            relay_back(1, step - back_lag)
    close(1)

    for c in range(CHUNKS):
        @pl.when(smp // owners == c)
        def _():
            gathered[mine] = final[c, (smp // 2) % chunk_heads, y]

    def take_last(offset, carry):
        sy, ss = source_of(offset, y, smp, smp_size)
        source = sy * smp_size + ss
        last(0, sy, ss, source, source).wait_recv()
        return carry

    lax.fori_loop(1, planes, take_last, 0)
    got_keys = gathered[:per_array].reshape(per_array * rows, HEAD)
    got_values = gathered[per_array:].reshape(per_array * rows, HEAD)
    low = lax.broadcasted_iota(jnp.int32, got_keys.shape, 1) < HEAD // 2
    got_keys = got_keys.astype(F32)
    got_values = got_values.astype(F32)
    even = jnp.where(low, got_keys, pltpu.roll(got_values, HEAD // 2, 1))
    odd = jnp.where(low, pltpu.roll(got_keys, HEAD // 2, 1), got_values)
    out_ref[...] = jnp.where(smp % 2 == 0, even, odd).astype(BF16)

    for c in range(CHUNKS):
        for dy in range(1, Y_CHIPS):
            spread((y + dy) % Y_CHIPS, c, keys_ref).wait_send()
        for way in range(2):
            for step in range(ring_steps(c, way)):
                ring(c, way, step).wait_send()
            for step in range(first_step(c, way), half):
                ring_back(c, way, step).wait_send()
        for copy in stores(c):
            copy.wait()

    def finish(offset, carry):
        py, ps = peer_of(offset, y, smp, smp_size)
        target = py * smp_size + ps
        name((py, ps), target, mine).wait_send()
        for c in range(CHUNKS):
            give(c, (py, ps), target, mine).wait_send()
            back(c, (py, ps), target, mine).wait_send()
        last(0, py, ps, target, mine).wait_send()
        return carry

    lax.fori_loop(1, planes, finish, 0)


def body(
    queries, out_grad, local_keys, trajectory_values, journal_keys, journal_values, picks, lengths
):
    smp_size = lax.axis_size("smp")
    z_chips = lax.axis_size("ctx") // Y_CHIPS
    planes = Y_CHIPS * smp_size
    block_rows, features = journal_keys.shape[1:]
    blocks = Y_CHIPS * z_chips
    rows = 2 * block_rows // planes
    cols = features // CHUNKS
    tq = queries.shape[1]
    width = queries.shape[2] // (features // HEAD) // HEAD * tq
    half = z_chips // 2
    heads = cols // HEAD
    dma = pltpu.SemaphoreType.DMA
    vmem = pltpu.VMEM
    any_space = pl.BlockSpec(memory_space=pl.ANY)
    in_smem = pl.BlockSpec(memory_space=pltpu.SMEM)
    in_vmem = pl.BlockSpec(memory_space=pltpu.VMEM)
    grad_queries, grad_local_keys, grad_local_values, summed = pl.pallas_call(
        functools.partial(fused_kernel, z_chips, smp_size),
        out_shape=(
            jax.ShapeDtypeStruct(queries.shape, BF16),
            jax.ShapeDtypeStruct(local_keys.shape, BF16),
            jax.ShapeDtypeStruct(local_keys.shape, BF16),
            jax.ShapeDtypeStruct((block_rows, HEAD), BF16),
        ),
        in_specs=[in_smem, in_smem] + [any_space] * 6,
        out_specs=(any_space, any_space, any_space, in_vmem),
        scratch_shapes=[
            vmem((blocks, rows, cols), BF16),
            vmem((blocks, rows, cols), BF16),
            vmem((CHUNKS, planes, TOP, rows, cols), BF16),
            vmem((CHUNKS, planes, TOP, rows, cols), BF16),
            vmem((planes, 1, 128), jnp.int32),
            pltpu.SMEM((planes, 1, 128), jnp.int32),
            vmem((planes, 1, 128), jnp.int32),
            pltpu.SMEM((planes, 1, 128), jnp.int32),
            vmem(queries.shape[1:], BF16),
            vmem(queries.shape[1:], BF16),
            vmem(local_keys.shape[1:], BF16),
            vmem(local_keys.shape[1:], BF16),
            vmem(queries.shape[1:], BF16),
            vmem(local_keys.shape[1:], BF16),
            vmem(local_keys.shape[1:], BF16),
            vmem((TOP + 1, tq, width), F32),
            vmem((TOP + 1, tq, width), F32),
            vmem((CHUNKS, planes, TOP, rows, cols), BF16),
            vmem((TOP * planes + 1, rows, cols), BF16),
            vmem((TOP * planes + 1, rows, cols), BF16),
            vmem((2, Y_CHIPS, rows, cols), F32),
            vmem((CHUNKS, 2, half, Y_CHIPS, rows, cols), BF16),
            vmem((CHUNKS, 2, half, Y_CHIPS, rows, cols), BF16),
            vmem((CHUNKS, heads, Y_CHIPS, rows, HEAD), BF16),
            vmem((planes, rows, HEAD), BF16),
            dma((4,)),
            dma((CHUNKS, 3)),
            dma((CHUNKS, Y_CHIPS)),
            dma((CHUNKS, Y_CHIPS)),
            dma((CHUNKS,)),
            dma((planes,)),
            dma((planes,)),
            dma((2,)),
            dma((CHUNKS, 2, half)),
            dma((CHUNKS, z_chips)),
            dma((CHUNKS, planes)),
            dma((CHUNKS, planes)),
            dma((CHUNKS, planes)),
            dma((CHUNKS, planes)),
            dma((CHUNKS, 2, half)),
            dma((CHUNKS, 2, half)),
            dma((planes,)),
            dma((planes,)),
        ],
        compiler_params=pltpu.CompilerParams(
            collective_id=0, has_side_effects=True, vmem_limit_bytes=56 << 20
        ),
        name="sparse_attention_grads",
    )(
        picks,
        lengths,
        queries,
        out_grad,
        local_keys,
        trajectory_values,
        journal_keys,
        journal_values,
    )
    return (
        grad_queries,
        grad_local_keys,
        grad_local_values,
        summed[None, :, : HEAD // 2],
        summed[None, :, HEAD // 2 :],
    )


def solution(mesh):
    in_specs = (
        P("smp", "ctx", None),
        P("smp", "ctx", None),
        P("smp", "ctx", None),
        P("smp", "ctx", None),
        P("ctx", None, None),
        P("ctx", None, None),
        P("smp", "ctx", None),
        P("smp"),
    )
    out_specs = (
        P("smp", "ctx", None),
        P("smp", "ctx", None),
        P("smp", "ctx", None),
        P("ctx", None, "smp"),
        P("ctx", None, "smp"),
    )
    return jax.shard_map(body, mesh=mesh, in_specs=in_specs, out_specs=out_specs, check_vma=False)
```

```python
import functools
import math

import jax
import jax.numpy as jnp
from jax import lax
from jax.experimental import pallas as pl
from jax.experimental.pallas import tpu as pltpu
from jax.sharding import PartitionSpec as P

HEAD = 128
Y_CHIPS = 4
SCALE = 1.0 / math.sqrt(HEAD)
CHUNKS = 2
TOP = 3
MESH = pl.DeviceIdType.MESH
BF16 = jnp.bfloat16
F32 = jnp.float32


def place(z_chips):
    ctx = lax.axis_index("ctx")
    return ctx // z_chips, ctx % z_chips, lax.axis_index("smp")


def plane_of(y, z, smp, z_chips, smp_size):
    xs = smp_size // 2
    x, core = smp // 2, lax.rem(smp, 2)
    along_y = [lax.rem(y + d, Y_CHIPS) for d in range(Y_CHIPS)]
    along_smp = [
        lax.rem(x + d // 2, xs) * 2 + lax.rem(core + d % 2, 2) for d in range(smp_size)
    ]
    peers = []
    for dy in range(Y_CHIPS):
        for ds in range(smp_size):
            if dy + ds > 0:
                peers.append(
                    (
                        (along_y[dy] * z_chips + z, along_smp[ds]),
                        along_y[dy] * smp_size + along_smp[ds],
                    )
                )
    return peers


def enter(y, z, smp, z_chips, peers):
    barrier = pltpu.get_barrier_semaphore()
    near = [(y * z_chips + lax.rem(z + d, z_chips), smp) for d in along_z(z_chips)]
    for device in near + [device for device, _ in peers]:
        pl.semaphore_signal(barrier, 1, device_id=device, device_id_type=MESH)
    pl.semaphore_wait(barrier, len(near) + len(peers))


def along_z(z_chips):
    return [d % z_chips for d in (1, -1, 2, -2, 3, -3)]


def eight(c):
    return 1 if c % 2 == 0 else -1


def down_tree(c):
    sends = [(0, 3), (0, -3), (0, 1), (0, -1)]
    for side in (1, -1):
        sends += [(3 * side, 3 * side), (3 * side, side), (3 * side, -side)]
    for side in (1, -1):
        sends += [(6 * side, side), (6 * side, -side)]
    return sends + [(6 * eight(c), 2 * eight(c))]


UP_LEAVES = (5, 7, 2, 4, 1)
UP = {1: -1, 2: 1, 3: -3, 4: -1, 5: 1, 6: -3, 7: -1, 8: -2}


def up_tree(c):
    roles = [(r * side, UP[r] * side) for r in range(1, 8) for side in (1, -1)]
    return roles + [(8 * eight(c), UP[8] * eight(c))]


def fused_kernel(
    z_chips,
    smp_size,
    picks_ref,
    length_ref,
    queries_ref,
    grad_ref,
    own_keys_ref,
    own_values_ref,
    keys_ref,
    values_ref,
    grad_queries_ref,
    grad_keys_ref,
    grad_values_ref,
    out_ref,
    log_0,
    log_1,
    staged,
    fetched,
    named,
    named_s,
    where_v,
    where_s,
    q_all,
    g_all,
    k_own,
    v_own,
    dq_all,
    dk_own,
    dv_own,
    scores,
    grad_probs,
    strips,
    held_0,
    held_1,
    sending,
    arriving,
    final,
    gathered,
    load_sem,
    store_sem,
    spread_send,
    spread_recv,
    own_sem,
    name_send,
    name_recv,
    smem_sem,
    ring_send,
    ring_recv,
    pick_send,
    pick_recv,
    give_send,
    give_recv,
    back_send,
    back_recv,
    last_send,
    last_recv,
):
    y, z, smp = place(z_chips)
    planes = Y_CHIPS * smp_size
    mine = y * smp_size + smp
    peers = plane_of(y, z, smp, z_chips, smp_size)
    others = planes - 1
    log = (log_0, log_1)
    held = (held_0, held_1)
    rows, cols = log_0.shape[1:]
    per_array = planes // 2
    chunk_heads = cols // HEAD
    tq = q_all.shape[0]
    group = q_all.shape[1] // (CHUNKS * cols)
    width = group * tq
    lane = lax.broadcasted_iota(jnp.int32, (1, 128), 1)

    loads = [
        pltpu.make_async_copy(ref.at[0], scratch, load_sem.at[n])
        for n, (ref, scratch) in enumerate(
            (
                (queries_ref, q_all),
                (grad_ref, g_all),
                (own_keys_ref, k_own),
                (own_values_ref, v_own),
            )
        )
    ]
    named[mine] = jnp.where(
        lane == 0,
        picks_ref[0, 0, 0],
        jnp.where(lane == 1, picks_ref[0, 0, 1], picks_ref[0, 0, 2]),
    )
    enter(y, z, smp, z_chips, peers)

    def piece(ref, owner, c):
        row = pl.multiple_of((owner % per_array) * rows, rows)
        return ref.at[0, pl.ds(row, rows), pl.ds(c * cols, cols)]

    def spread(py, c, ref):
        return pltpu.make_async_remote_copy(
            src_ref=piece(ref, py * smp_size + smp, c),
            dst_ref=log[c].at[z * Y_CHIPS + y],
            send_sem=spread_send.at[c, py],
            recv_sem=spread_recv.at[c, y],
            device_id=(py * z_chips + z, smp),
            device_id_type=MESH,
        )

    def spread_in(py, c):
        return pltpu.make_async_remote_copy(
            src_ref=piece(keys_ref, mine, c),
            dst_ref=log[c].at[z * Y_CHIPS + py],
            send_sem=spread_send.at[c, py],
            recv_sem=spread_recv.at[c, py],
            device_id=(py * z_chips + z, smp),
            device_id_type=MESH,
        )

    def own(c, ref):
        return pltpu.make_async_copy(
            piece(ref, mine, c), log[c].at[z * Y_CHIPS + y], own_sem.at[c]
        )

    for c in range(CHUNKS):
        for dy in range(1, Y_CHIPS):
            py = (y + dy) % Y_CHIPS

            @pl.when(py < Y_CHIPS // 2)
            def _():
                spread(py, c, keys_ref).start()

            @pl.when(py >= Y_CHIPS // 2)
            def _():
                spread(py, c, values_ref).start()

        @pl.when(y < Y_CHIPS // 2)
        def _():
            own(c, keys_ref).start()

        @pl.when(y >= Y_CHIPS // 2)
        def _():
            own(c, values_ref).start()

    def name(device, slots):
        return pltpu.make_async_remote_copy(
            src_ref=named.at[mine] if slots is None else named.at[slots],
            dst_ref=named.at[mine] if slots is None else named.at[slots],
            send_sem=name_send.at[0],
            recv_sem=name_recv.at[0],
            device_id=device,
            device_id_type=MESH,
        )

    one_peer = peers[0][0]
    for device, _ in peers:
        name(device, None).start()
    for load in loads:
        load.start()

    def pass_on(c, source, step):
        slot = lax.rem(z + (z_chips - source) % z_chips, z_chips)
        to = lax.rem(z + step % z_chips, z_chips)
        those = log[c].at[pl.ds(slot * Y_CHIPS, Y_CHIPS)]
        return pltpu.make_async_remote_copy(
            src_ref=those,
            dst_ref=those,
            send_sem=ring_send.at[c, down_tree(c).index((source, step))],
            recv_sem=ring_recv.at[c, slot],
            device_id=(y * z_chips + to, smp),
            device_id_type=MESH,
        )

    def arrived(c, source):
        slot = lax.rem(z + (z_chips - source) % z_chips, z_chips)
        those = log[c].at[pl.ds(slot * Y_CHIPS, Y_CHIPS)]
        pltpu.make_async_remote_copy(
            src_ref=those,
            dst_ref=those,
            send_sem=ring_send.at[c, 0],
            recv_sem=ring_recv.at[c, slot],
            device_id=one_peer,
            device_id_type=MESH,
        ).wait_recv()

    def begin(c):
        for dy in range(1, Y_CHIPS):
            spread_in((y + dy) % Y_CHIPS, c).wait_recv()
        own(c, keys_ref).wait()
        relay(c, 0)

    def relay(c, distance):
        for side in (1, -1) if distance else (1,):
            source = distance * side
            if distance:
                arrived(c, source)
            for start, step in down_tree(c):
                if start == source:
                    pass_on(c, start, step).start()

    def leaves(c):
        for distance in (1, 2, 4, 5, 7):
            for side in (1, -1):
                arrived(c, distance * side)
        arrived(c, 8 * eight(c))

    def locate(k, carry):
        found = jnp.full((1, 128), TOP * planes, jnp.int32)
        for i in range(TOP):
            found = jnp.where(lane == named_s[k, 0, i], TOP * k + i, found)
        where_v[k] = found
        return carry

    def give(c, device, slot_send, slot_recv):
        return pltpu.make_async_remote_copy(
            src_ref=staged.at[c, slot_send],
            dst_ref=fetched.at[c, slot_recv],
            send_sem=pick_send.at[c],
            recv_sem=pick_recv.at[c],
            device_id=device,
            device_id_type=MESH,
        )

    def place_of(target, i):
        block = named_s[target, 0, i]
        return lax.rem(block, z_chips) * Y_CHIPS + lax.div(block, z_chips)

    def send_picks(c, some):
        for device, target in some:
            for i in range(TOP):
                staged[c, target, i] = log[c][place_of(target, i)]
            give(c, device, target, mine).start()

    def keep_picks(c):
        for i in range(TOP):
            fetched[c, mine, i] = log[c][place_of(mine, i)]

    def all_picks(c):
        return give(c, one_peer, pl.ds(0, others), pl.ds(0, others))

    def grads(c):
        live_rows = length_ref[0] - lax.axis_index("ctx") * tq
        live = lax.broadcasted_iota(jnp.int32, (tq, HEAD), 0) < live_rows
        across = (((1,), (1,)), ((), ()))
        down = (((0,), (0,)), ((), ()))

        def one(n, carry):
            inner = pl.ds(pl.multiple_of(n * HEAD, HEAD), HEAD)
            lanes = pl.ds(pl.multiple_of(c * cols + n * HEAD, HEAD), HEAD)
            base = (c * chunk_heads + n) * group * HEAD
            wide = [pl.ds(pl.multiple_of(base + h * HEAD, HEAD), HEAD) for h in range(group)]
            q = jnp.concatenate([q_all[:, w] for w in wide], axis=0)
            raw = [g_all[:, w] for w in wide]
            g = jnp.concatenate([jnp.where(live, r, jnp.zeros_like(r)) for r in raw], axis=0)

            def keys_of(i):
                if i == TOP:
                    return k_own[:, lanes]
                return fetched[c, :per_array, i, :, inner].reshape(tq, HEAD)

            def values_of(i):
                if i == TOP:
                    return v_own[:, lanes]
                return fetched[c, per_array:, i, :, inner].reshape(tq, HEAD)

            top = None
            for i in range(TOP + 1):
                s = lax.dot_general(keys_of(i), q, across, preferred_element_type=F32)
                if i == TOP:
                    row = lax.broadcasted_iota(jnp.int32, (tq, width), 0)
                    col = lax.broadcasted_iota(jnp.int32, (tq, width), 1) % tq
                    s = jnp.where(col >= row, s, -1e30)
                scores[i] = s
                best = jnp.max(s, axis=0, keepdims=True)
                top = best if top is None else jnp.maximum(top, best)
                grad_probs[i] = lax.dot_general(
                    values_of(i), g, across, preferred_element_type=F32
                )
            total = jnp.zeros((1, width), F32)
            delta = jnp.zeros((1, width), F32)
            for i in range(TOP + 1):
                w = jnp.exp((scores[i] - top) * SCALE)
                scores[i] = w
                total = total + jnp.sum(w, axis=0, keepdims=True)
                delta = delta + jnp.sum(w * grad_probs[i], axis=0, keepdims=True)
            inverse = 1.0 / total
            delta = delta * inverse
            dq = None
            for i in range(TOP + 1):
                probs = scores[i] * inverse
                grad_low = (probs * (grad_probs[i] - delta)).astype(BF16)
                probs_low = probs.astype(BF16)
                dv = jnp.dot(probs_low, g, preferred_element_type=F32).astype(BF16)
                dk = jnp.dot(grad_low, q, preferred_element_type=F32) * SCALE
                dk = dk.astype(BF16)
                some = lax.dot_general(grad_low, keys_of(i), down, preferred_element_type=F32)
                dq = some if dq is None else dq + some
                if i == TOP:
                    dk_own[:, lanes] = dk
                    dv_own[:, lanes] = dv
                else:
                    strips[c, :per_array, i, :, inner] = dk.reshape(per_array, rows, HEAD)
                    strips[c, per_array:, i, :, inner] = dv.reshape(per_array, rows, HEAD)
            for h in range(group):
                dq_all[:, wide[h]] = (dq[h * tq : (h + 1) * tq] * SCALE).astype(BF16)
            return carry

        lax.fori_loop(0, chunk_heads, one, 0)

    def back(c, device, slot_send, slot_recv):
        return pltpu.make_async_remote_copy(
            src_ref=strips.at[c, slot_send],
            dst_ref=held[c].at[slot_recv],
            send_sem=give_send.at[c],
            recv_sem=give_recv.at[c],
            device_id=device,
            device_id_type=MESH,
        )

    def send_partials(c):
        for device, target in peers:
            back(c, device, target, pl.ds(TOP * mine, TOP)).start()
        for i in range(TOP):
            held[c][TOP * mine + i] = strips[c, mine, i]

    def all_partials(c):
        return pltpu.make_async_remote_copy(
            src_ref=held[c].at[pl.ds(0, TOP * others)],
            dst_ref=held[c].at[pl.ds(0, TOP * others)],
            send_sem=give_send.at[c],
            recv_sem=give_recv.at[c],
            device_id=one_peer,
            device_id_type=MESH,
        )

    def total_of(c, role, yb, feeders):
        b = yb * z_chips + lax.rem(z + (z_chips - role) % z_chips, z_chips)
        acc = held[c][where_s[0, 0, b]].astype(F32)
        for k in range(1, planes):
            acc = acc + held[c][where_s[k, 0, b]].astype(F32)
        for feeder in feeders:
            acc = acc + arriving[c, slot_of(c, feeder), yb].astype(F32)
        return acc

    def slot_of(c, role):
        return [r for r, _ in up_tree(c)].index(role)

    def pass_up(c, role):
        slot = slot_of(c, role)
        to = lax.rem(z + up_tree(c)[slot][1] % z_chips, z_chips)
        return pltpu.make_async_remote_copy(
            src_ref=sending.at[c, slot],
            dst_ref=arriving.at[c, slot],
            send_sem=back_send.at[c, slot],
            recv_sem=back_recv.at[c, slot],
            device_id=(y * z_chips + to, smp),
            device_id_type=MESH,
        )

    def feeders_of(c, role):
        side = 1 if role > 0 else -1
        if abs(role) == 3:
            return [2 * side, 4 * side, 6 * side]
        if abs(role) == 6:
            return [5 * side, 7 * side] + ([8 * side] if side == eight(c) else [])
        return [1, -1, 3, -3] if role == 0 else []

    def send_up(c, role):
        feeders = feeders_of(c, role)
        slot = slot_of(c, role)
        for feeder in feeders:
            pass_up(c, feeder).wait_recv()

        def block(yb, carry):
            sending[c, slot, yb] = total_of(c, role, yb, feeders).astype(BF16)
            return carry

        lax.fori_loop(0, Y_CHIPS, block, 0)
        pass_up(c, role).start()

    def last(c, device, head, py, slot_recv):
        return pltpu.make_async_remote_copy(
            src_ref=final.at[c, head, py],
            dst_ref=gathered.at[slot_recv],
            send_sem=last_send.at[0],
            recv_sem=last_recv.at[0],
            device_id=device,
            device_id_type=MESH,
        )

    owners = smp_size // CHUNKS

    def close(c):
        for feeder in feeders_of(c, 0):
            pass_up(c, feeder).wait_recv()

        def block(yb, carry):
            whole = total_of(c, 0, yb, feeders_of(c, 0)).astype(BF16)
            for n in range(chunk_heads):
                final[c, n, yb] = whole[:, n * HEAD : (n + 1) * HEAD]
            return carry

        lax.fori_loop(0, Y_CHIPS, block, 0)
        first = c * owners
        turns = [
            (lax.rem(y + n // owners, Y_CHIPS), first + lax.rem(smp + n % owners, owners))
            for n in range(Y_CHIPS * owners)
        ]
        for py, ps in turns:

            @pl.when(py * smp_size + ps != mine)
            def _():
                last(c, (py * z_chips + z, ps), (ps - first) // 2, py, mine).start()

    def stores(c):
        narrow = pl.ds(c * cols, cols)
        wide = pl.ds(c * cols * group, cols * group)
        return [
            pltpu.make_async_copy(
                scratch.at[:, part_of], ref.at[0, :, part_of], store_sem.at[c, n]
            )
            for n, (scratch, ref, part_of) in enumerate(
                (
                    (dq_all, grad_queries_ref, wide),
                    (dk_own, grad_keys_ref, narrow),
                    (dv_own, grad_values_ref, narrow),
                )
            )
        ]

    begin(0)
    name(one_peer, pl.ds(0, others)).wait_recv()
    to_smem = pltpu.make_async_copy(named, named_s, smem_sem.at[0])
    to_smem.start()
    relay(0, 3)
    begin(1)
    relay(0, 6)
    relay(1, 3)
    to_smem.wait()
    leaves(0)
    middle = planes // 3
    send_picks(0, peers[:middle])
    relay(1, 6)
    send_picks(0, peers[middle:])
    leaves(1)
    send_picks(1, peers)
    for c in range(CHUNKS):
        keep_picks(c)
        held[c][TOP * planes] = jnp.zeros((rows, cols), BF16)
    lax.fori_loop(0, planes, locate, 0)
    where_copy = pltpu.make_async_copy(where_v, where_s, smem_sem.at[1])
    where_copy.start()
    for load in loads:
        load.wait()
    for c in range(CHUNKS):
        all_picks(c).wait_recv()
        grads(c)
        send_partials(c)
        for copy in stores(c):
            copy.start()
    where_copy.wait()
    all_partials(0).wait_recv()
    for role in UP_LEAVES:
        send_up(0, role)
        send_up(0, -role)
    send_up(0, 8 * eight(0))
    send_up(0, 6)
    send_up(0, -6)
    all_partials(1).wait_recv()
    for n, role in enumerate(UP_LEAVES):
        send_up(1, role)
        send_up(1, -role)
        if n == 1:
            send_up(1, 8 * eight(1))
            send_up(0, 3)
            send_up(0, -3)
    send_up(1, 6)
    send_up(1, -6)
    close(0)
    send_up(1, 3)
    send_up(1, -3)
    close(1)

    for c in range(CHUNKS):

        @pl.when(smp // owners == c)
        def _():
            gathered[mine] = final[c, (smp // 2) % chunk_heads, y]

    all_last = pltpu.make_async_remote_copy(
        src_ref=gathered.at[pl.ds(0, others)],
        dst_ref=gathered.at[pl.ds(0, others)],
        send_sem=last_send.at[0],
        recv_sem=last_recv.at[0],
        device_id=one_peer,
        device_id_type=MESH,
    )
    all_last.wait_recv()
    got_keys = gathered[:per_array].reshape(per_array * rows, HEAD).astype(F32)
    got_values = gathered[per_array:].reshape(per_array * rows, HEAD).astype(F32)
    low = lax.broadcasted_iota(jnp.int32, got_keys.shape, 1) < HEAD // 2
    even = jnp.where(low, got_keys, pltpu.roll(got_values, HEAD // 2, 1))
    odd = jnp.where(low, pltpu.roll(got_keys, HEAD // 2, 1), got_values)
    out_ref[...] = jnp.where(smp % 2 == 0, even, odd).T.astype(BF16)

    name(one_peer, pl.ds(0, others)).wait_send()
    for c in range(CHUNKS):
        for dy in range(1, Y_CHIPS):
            spread((y + dy) % Y_CHIPS, c, keys_ref).wait_send()
        for source, step in down_tree(c):
            pass_on(c, source, step).wait_send()
        for role, _ in up_tree(c):
            pass_up(c, role).wait_send()
        for copy in stores(c):
            copy.wait()
        all_picks(c).wait_send()
        all_partials(c).wait_send()
    all_last.wait_send()


def body(
    queries, out_grad, local_keys, trajectory_values, journal_keys, journal_values, picks, lengths
):
    smp_size = lax.axis_size("smp")
    z_chips = lax.axis_size("ctx") // Y_CHIPS
    planes = Y_CHIPS * smp_size
    block_rows, features = journal_keys.shape[1:]
    blocks = Y_CHIPS * z_chips
    rows = 2 * block_rows // planes
    cols = features // CHUNKS
    tq = queries.shape[1]
    width = queries.shape[2] // (features // HEAD) // HEAD * tq
    heads = cols // HEAD
    dma = pltpu.SemaphoreType.DMA
    vmem = pltpu.VMEM
    any_space = pl.BlockSpec(memory_space=pl.ANY)
    in_smem = pl.BlockSpec(memory_space=pltpu.SMEM)
    in_vmem = pl.BlockSpec(memory_space=pltpu.VMEM)
    grad_queries, grad_local_keys, grad_local_values, summed = pl.pallas_call(
        functools.partial(fused_kernel, z_chips, smp_size),
        out_shape=(
            jax.ShapeDtypeStruct(queries.shape, BF16),
            jax.ShapeDtypeStruct(local_keys.shape, BF16),
            jax.ShapeDtypeStruct(local_keys.shape, BF16),
            jax.ShapeDtypeStruct((HEAD, block_rows), BF16),
        ),
        in_specs=[in_smem, in_smem] + [any_space] * 6,
        out_specs=(any_space, any_space, any_space, in_vmem),
        scratch_shapes=[
            vmem((blocks, rows, cols), BF16),
            vmem((blocks, rows, cols), BF16),
            vmem((CHUNKS, planes, TOP, rows, cols), BF16),
            vmem((CHUNKS, planes, TOP, rows, cols), BF16),
            vmem((planes, 1, 128), jnp.int32),
            pltpu.SMEM((planes, 1, 128), jnp.int32),
            vmem((planes, 1, 128), jnp.int32),
            pltpu.SMEM((planes, 1, 128), jnp.int32),
            vmem(queries.shape[1:], BF16),
            vmem(queries.shape[1:], BF16),
            vmem(local_keys.shape[1:], BF16),
            vmem(local_keys.shape[1:], BF16),
            vmem(queries.shape[1:], BF16),
            vmem(local_keys.shape[1:], BF16),
            vmem(local_keys.shape[1:], BF16),
            vmem((TOP + 1, tq, width), F32),
            vmem((TOP + 1, tq, width), F32),
            vmem((CHUNKS, planes, TOP, rows, cols), BF16),
            vmem((TOP * planes + 1, rows, cols), BF16),
            vmem((TOP * planes + 1, rows, cols), BF16),
            vmem((CHUNKS, z_chips - 1, Y_CHIPS, rows, cols), BF16),
            vmem((CHUNKS, z_chips - 1, Y_CHIPS, rows, cols), BF16),
            vmem((CHUNKS, heads, Y_CHIPS, rows, HEAD), BF16),
            vmem((planes, rows, HEAD), BF16),
            dma((4,)),
            dma((CHUNKS, 3)),
            dma((CHUNKS, Y_CHIPS)),
            dma((CHUNKS, Y_CHIPS)),
            dma((CHUNKS,)),
            dma((1,)),
            dma((1,)),
            dma((2,)),
            dma((CHUNKS, z_chips - 1)),
            dma((CHUNKS, z_chips)),
            dma((CHUNKS,)),
            dma((CHUNKS,)),
            dma((CHUNKS,)),
            dma((CHUNKS,)),
            dma((CHUNKS, z_chips - 1)),
            dma((CHUNKS, z_chips - 1)),
            dma((1,)),
            dma((1,)),
        ],
        compiler_params=pltpu.CompilerParams(
            collective_id=0, has_side_effects=True, vmem_limit_bytes=56 << 20
        ),
        name="sparse_attention_grads",
    )(
        picks,
        lengths,
        queries,
        out_grad,
        local_keys,
        trajectory_values,
        journal_keys,
        journal_values,
    )
    return (
        grad_queries,
        grad_local_keys,
        grad_local_values,
        summed[: HEAD // 2].T[None],
        summed[HEAD // 2 :].T[None],
    )


def solution(mesh):
    in_specs = (
        P("smp", "ctx", None),
        P("smp", "ctx", None),
        P("smp", "ctx", None),
        P("smp", "ctx", None),
        P("ctx", None, None),
        P("ctx", None, None),
        P("smp", "ctx", None),
        P("smp"),
    )
    out_specs = (
        P("smp", "ctx", None),
        P("smp", "ctx", None),
        P("smp", "ctx", None),
        P("ctx", None, "smp"),
        P("ctx", None, "smp"),
    )
    return jax.shard_map(body, mesh=mesh, in_specs=in_specs, out_specs=out_specs, check_vma=False)
```

```python
import functools
import math

import jax
import jax.numpy as jnp
from jax import lax
from jax.experimental import pallas as pl
from jax.experimental.pallas import tpu as pltpu
from jax.sharding import PartitionSpec as P

HEAD = 128
Y_CHIPS = 4
SCALE = 1.0 / math.sqrt(HEAD)
LOG2_E = math.log2(math.e)
CHUNKS = 2
TOP = 3
MESH = pl.DeviceIdType.MESH
BF16 = jnp.bfloat16
F32 = jnp.float32


def place(z_chips):
    ctx = lax.axis_index("ctx")
    return ctx // z_chips, ctx % z_chips, lax.axis_index("smp")


def plane_of(y, z, smp, z_chips, smp_size):
    xs = smp_size // 2
    x, core = smp // 2, lax.rem(smp, 2)
    along_y = [lax.rem(y + d, Y_CHIPS) for d in range(Y_CHIPS)]
    along_smp = [
        lax.rem(x + d // 2, xs) * 2 + lax.rem(core + d % 2, 2) for d in range(smp_size)
    ]
    peers = []
    for dy in range(Y_CHIPS):
        for ds in range(smp_size):
            if dy + ds > 0:
                peers.append(
                    (
                        (along_y[dy] * z_chips + z, along_smp[ds]),
                        along_y[dy] * smp_size + along_smp[ds],
                    )
                )
    return peers


def enter(y, z, smp, z_chips, peers):
    barrier = pltpu.get_barrier_semaphore()
    near = [(y * z_chips + lax.rem(z + d, z_chips), smp) for d in along_z(z_chips)]
    for device in near + [device for device, _ in peers]:
        pl.semaphore_signal(barrier, 1, device_id=device, device_id_type=MESH)
    pl.semaphore_wait(barrier, len(near) + len(peers))


def along_z(z_chips):
    return [d % z_chips for d in (1, -1, 2, -2, 3, -3)]


def eight(c):
    return 1 if c % 2 == 0 else -1


def down_tree(c):
    sends = [(0, 3), (0, -3), (0, 1), (0, -1)]
    for side in (1, -1):
        sends += [(3 * side, 3 * side), (3 * side, side), (3 * side, -side)]
    for side in (1, -1):
        sends += [(6 * side, side), (6 * side, -side)]
    return sends + [(6 * eight(c), 2 * eight(c))]


UP_LEAVES = (5, 7, 2, 4, 1)
UP = {1: -1, 2: 1, 3: -3, 4: -1, 5: 1, 6: -3, 7: -1, 8: -2}


def up_tree(c):
    roles = [(r * side, UP[r] * side) for r in range(1, 8) for side in (1, -1)]
    return roles + [(8 * eight(c), UP[8] * eight(c))]


def fused_kernel(
    z_chips,
    smp_size,
    picks_ref,
    length_ref,
    queries_ref,
    grad_ref,
    own_keys_ref,
    own_values_ref,
    keys_ref,
    values_ref,
    grad_queries_ref,
    grad_keys_ref,
    grad_values_ref,
    out_ref,
    log_0,
    log_1,
    staged,
    fetched,
    named,
    named_s,
    chosen,
    sums,
    q_all,
    g_all,
    k_own,
    v_own,
    dq_all,
    dk_own,
    dv_own,
    scores,
    grad_probs,
    strips,
    held_0,
    held_1,
    sending,
    arriving,
    final,
    gathered,
    load_sem,
    store_sem,
    spread_send,
    spread_recv,
    own_sem,
    name_send,
    name_recv,
    smem_sem,
    ring_send,
    ring_recv,
    pick_send,
    pick_recv,
    give_send,
    give_recv,
    back_send,
    back_recv,
    last_send,
    last_recv,
):
    y, z, smp = place(z_chips)
    planes = Y_CHIPS * smp_size
    mine = y * smp_size + smp
    peers = plane_of(y, z, smp, z_chips, smp_size)
    others = planes - 1
    log = (log_0, log_1)
    held = (held_0, held_1)
    rows, cols = log_0.shape[1:]
    per_array = planes // 2
    chunk_heads = cols // HEAD
    tq = q_all.shape[0]
    group = q_all.shape[1] // (CHUNKS * cols)
    width = group * tq
    lane = lax.broadcasted_iota(jnp.int32, (1, 128), 1)

    loads = [
        pltpu.make_async_copy(ref.at[0], scratch, load_sem.at[n])
        for n, (ref, scratch) in enumerate(
            (
                (queries_ref, q_all),
                (grad_ref, g_all),
                (own_keys_ref, k_own),
                (own_values_ref, v_own),
            )
        )
    ]
    named[mine] = jnp.where(
        lane == 0,
        picks_ref[0, 0, 0],
        jnp.where(lane == 1, picks_ref[0, 0, 1], picks_ref[0, 0, 2]),
    )
    enter(y, z, smp, z_chips, peers)

    def piece(ref, owner, c):
        row = pl.multiple_of((owner % per_array) * rows, rows)
        return ref.at[0, pl.ds(row, rows), pl.ds(c * cols, cols)]

    def spread(py, c, ref):
        return pltpu.make_async_remote_copy(
            src_ref=piece(ref, py * smp_size + smp, c),
            dst_ref=log[c].at[z * Y_CHIPS + y],
            send_sem=spread_send.at[c, py],
            recv_sem=spread_recv.at[c, y],
            device_id=(py * z_chips + z, smp),
            device_id_type=MESH,
        )

    def spread_in(py, c):
        return pltpu.make_async_remote_copy(
            src_ref=piece(keys_ref, mine, c),
            dst_ref=log[c].at[z * Y_CHIPS + py],
            send_sem=spread_send.at[c, py],
            recv_sem=spread_recv.at[c, py],
            device_id=(py * z_chips + z, smp),
            device_id_type=MESH,
        )

    def own(c, ref):
        return pltpu.make_async_copy(
            piece(ref, mine, c), log[c].at[z * Y_CHIPS + y], own_sem.at[c]
        )

    for c in range(CHUNKS):
        for dy in range(1, Y_CHIPS):
            py = (y + dy) % Y_CHIPS

            @pl.when(py < Y_CHIPS // 2)
            def _():
                spread(py, c, keys_ref).start()

            @pl.when(py >= Y_CHIPS // 2)
            def _():
                spread(py, c, values_ref).start()

        @pl.when(y < Y_CHIPS // 2)
        def _():
            own(c, keys_ref).start()

        @pl.when(y >= Y_CHIPS // 2)
        def _():
            own(c, values_ref).start()

    def name(device, slots):
        return pltpu.make_async_remote_copy(
            src_ref=named.at[mine] if slots is None else named.at[slots],
            dst_ref=named.at[mine] if slots is None else named.at[slots],
            send_sem=name_send.at[0],
            recv_sem=name_recv.at[0],
            device_id=device,
            device_id_type=MESH,
        )

    one_peer = peers[0][0]
    for device, _ in peers:
        name(device, None).start()
    for load in loads:
        load.start()

    def pass_on(c, source, step):
        slot = lax.rem(z + (z_chips - source) % z_chips, z_chips)
        to = lax.rem(z + step % z_chips, z_chips)
        those = log[c].at[pl.ds(slot * Y_CHIPS, Y_CHIPS)]
        return pltpu.make_async_remote_copy(
            src_ref=those,
            dst_ref=those,
            send_sem=ring_send.at[c, down_tree(c).index((source, step))],
            recv_sem=ring_recv.at[c, slot],
            device_id=(y * z_chips + to, smp),
            device_id_type=MESH,
        )

    def arrived(c, source):
        slot = lax.rem(z + (z_chips - source) % z_chips, z_chips)
        those = log[c].at[pl.ds(slot * Y_CHIPS, Y_CHIPS)]
        pltpu.make_async_remote_copy(
            src_ref=those,
            dst_ref=those,
            send_sem=ring_send.at[c, 0],
            recv_sem=ring_recv.at[c, slot],
            device_id=one_peer,
            device_id_type=MESH,
        ).wait_recv()

    def begin(c):
        for dy in range(1, Y_CHIPS):
            spread_in((y + dy) % Y_CHIPS, c).wait_recv()
        own(c, keys_ref).wait()
        relay(c, 0)

    def relay(c, distance):
        for side in (1, -1) if distance else (1,):
            source = distance * side
            if distance:
                arrived(c, source)
            for start, step in down_tree(c):
                if start == source:
                    pass_on(c, start, step).start()

    def leaves(c):
        for distance in (1, 2, 4, 5, 7):
            for side in (1, -1):
                arrived(c, distance * side)
        arrived(c, 8 * eight(c))

    def choose():
        lane_of = lax.broadcasted_iota(jnp.int32, (1, 128), 1)
        slot, row = lane_of // rows, lane_of % rows
        per_vector = 128 // rows
        codes = []
        for first in range(0, TOP * planes, per_vector):
            code = jnp.zeros((1, 128), jnp.int32)
            for j in range(per_vector):
                pick = place_of((first + j) // TOP, (first + j) % TOP)
                code = jnp.where(slot == j, pick * rows, code)
            codes.append(code + row)
        step = Y_CHIPS * rows

        def one(n, carry):
            start = pl.multiple_of(n * step, step)
            number = lax.broadcasted_iota(jnp.int32, (step, 128), 0) + start
            for m, code in enumerate(codes):
                hit = jnp.where(number == code, 1.0, 0.0)
                chosen[pl.ds(start, step), m * 128 : (m + 1) * 128] = hit.astype(BF16)
            return carry

        lax.fori_loop(0, z_chips, one, 0)

    def give(c, device, slot_send, slot_recv):
        return pltpu.make_async_remote_copy(
            src_ref=staged.at[c, slot_send],
            dst_ref=fetched.at[c, slot_recv],
            send_sem=pick_send.at[c],
            recv_sem=pick_recv.at[c],
            device_id=device,
            device_id_type=MESH,
        )

    def place_of(target, i):
        block = named_s[target, 0, i]
        return lax.rem(block, z_chips) * Y_CHIPS + lax.div(block, z_chips)

    def send_picks(c, some):
        for device, target in some:
            for i in range(TOP):
                staged[c, target, i] = log[c][place_of(target, i)]
            give(c, device, target, mine).start()

    def keep_picks(c):
        for i in range(TOP):
            fetched[c, mine, i] = log[c][place_of(mine, i)]

    def all_picks(c):
        return give(c, one_peer, pl.ds(0, others), pl.ds(0, others))

    def grads(c):
        live_rows = length_ref[0] - lax.axis_index("ctx") * tq
        live = lax.broadcasted_iota(jnp.int32, (tq, HEAD), 0) < live_rows
        across = (((1,), (1,)), ((), ()))
        down = (((0,), (0,)), ((), ()))

        def one(n, carry):
            inner = pl.ds(pl.multiple_of(n * HEAD, HEAD), HEAD)
            lanes = pl.ds(pl.multiple_of(c * cols + n * HEAD, HEAD), HEAD)
            base = (c * chunk_heads + n) * group * HEAD
            wide = [pl.ds(pl.multiple_of(base + h * HEAD, HEAD), HEAD) for h in range(group)]
            q = jnp.concatenate([q_all[:, w] for w in wide], axis=0)
            raw = [g_all[:, w] for w in wide]
            g = jnp.concatenate([jnp.where(live, r, jnp.zeros_like(r)) for r in raw], axis=0)

            def keys_of(i):
                if i == TOP:
                    return k_own[:, lanes]
                return fetched[c, :per_array, i, :, inner].reshape(tq, HEAD)

            def values_of(i):
                if i == TOP:
                    return v_own[:, lanes]
                return fetched[c, per_array:, i, :, inner].reshape(tq, HEAD)

            top = None
            for i in range(TOP + 1):
                s = lax.dot_general(keys_of(i), q, across, preferred_element_type=F32)
                if i == TOP:
                    row = lax.broadcasted_iota(jnp.int32, (tq, width), 0)
                    col = lax.broadcasted_iota(jnp.int32, (tq, width), 1) % tq
                    s = jnp.where(col >= row, s, -1e30)
                scores[i] = s
                best = jnp.max(s, axis=0, keepdims=True)
                top = best if top is None else jnp.maximum(top, best)
                grad_probs[i] = lax.dot_general(
                    values_of(i), g, across, preferred_element_type=F32
                )
            total = jnp.zeros((1, width), F32)
            delta = jnp.zeros((1, width), F32)
            for i in range(TOP + 1):
                w = jnp.exp2((scores[i] - top) * (SCALE * LOG2_E))
                scores[i] = w
                total = total + jnp.sum(w, axis=0, keepdims=True)
                delta = delta + jnp.sum(w * grad_probs[i], axis=0, keepdims=True)
            inverse = 1.0 / total
            delta = delta * inverse
            dq = None
            for i in range(TOP + 1):
                probs = scores[i] * inverse
                grad_low = (probs * (grad_probs[i] - delta)).astype(BF16)
                probs_low = probs.astype(BF16)
                dv = jnp.dot(probs_low, g, preferred_element_type=F32).astype(BF16)
                dk = jnp.dot(grad_low, q, preferred_element_type=F32) * SCALE
                dk = dk.astype(BF16)
                some = lax.dot_general(grad_low, keys_of(i), down, preferred_element_type=F32)
                dq = some if dq is None else dq + some
                if i == TOP:
                    dk_own[:, lanes] = dk
                    dv_own[:, lanes] = dv
                else:
                    strips[c, :per_array, i, :, inner] = dk.reshape(per_array, rows, HEAD)
                    strips[c, per_array:, i, :, inner] = dv.reshape(per_array, rows, HEAD)
            for h in range(group):
                dq_all[:, wide[h]] = (dq[h * tq : (h + 1) * tq] * SCALE).astype(BF16)
            return carry

        lax.fori_loop(0, chunk_heads, one, 0)

    def back(c, device, slot_send, slot_recv):
        return pltpu.make_async_remote_copy(
            src_ref=strips.at[c, slot_send],
            dst_ref=held[c].at[slot_recv],
            send_sem=give_send.at[c],
            recv_sem=give_recv.at[c],
            device_id=device,
            device_id_type=MESH,
        )

    def send_partials(c):
        for device, target in peers:
            back(c, device, target, pl.ds(TOP * mine, TOP)).start()
        for i in range(TOP):
            held[c][TOP * mine + i] = strips[c, mine, i]

    def all_partials(c):
        return pltpu.make_async_remote_copy(
            src_ref=held[c].at[pl.ds(0, TOP * others)],
            dst_ref=held[c].at[pl.ds(0, TOP * others)],
            send_sem=give_send.at[c],
            recv_sem=give_recv.at[c],
            device_id=one_peer,
            device_id_type=MESH,
        )

    def add_up(c):
        step = 4 * Y_CHIPS * rows
        those = held[c][...].reshape(TOP * planes * rows, cols)

        def one(n, carry):
            part = pl.ds(pl.multiple_of(n * step, step), step)
            sums[c, part] = jnp.dot(chosen[part], those, preferred_element_type=F32)
            return carry

        lax.fori_loop(0, z_chips // 4, one, 0)

    def total_of(c, role, feeders):
        step = Y_CHIPS * rows
        dest = lax.rem(z + (z_chips - role) % z_chips, z_chips)
        acc = sums[c, pl.ds(pl.multiple_of(dest * step, step), step)]
        acc = acc.reshape(Y_CHIPS, rows, cols)
        for feeder in feeders:
            acc = acc + arriving[c, slot_of(c, feeder)].astype(F32)
        return acc

    def slot_of(c, role):
        return [r for r, _ in up_tree(c)].index(role)

    def pass_up(c, role):
        slot = slot_of(c, role)
        to = lax.rem(z + up_tree(c)[slot][1] % z_chips, z_chips)
        return pltpu.make_async_remote_copy(
            src_ref=sending.at[c, slot],
            dst_ref=arriving.at[c, slot],
            send_sem=back_send.at[c, slot],
            recv_sem=back_recv.at[c, slot],
            device_id=(y * z_chips + to, smp),
            device_id_type=MESH,
        )

    def feeders_of(c, role):
        side = 1 if role > 0 else -1
        if abs(role) == 3:
            return [2 * side, 4 * side, 6 * side]
        if abs(role) == 6:
            return [5 * side, 7 * side] + ([8 * side] if side == eight(c) else [])
        return [1, -1, 3, -3] if role == 0 else []

    def send_up(c, role):
        feeders = feeders_of(c, role)
        slot = slot_of(c, role)
        for feeder in feeders:
            pass_up(c, feeder).wait_recv()

        sending[c, slot] = total_of(c, role, feeders).astype(BF16)
        pass_up(c, role).start()

    def last(c, device, head, py, slot_recv):
        return pltpu.make_async_remote_copy(
            src_ref=final.at[c, head, py],
            dst_ref=gathered.at[slot_recv],
            send_sem=last_send.at[0],
            recv_sem=last_recv.at[0],
            device_id=device,
            device_id_type=MESH,
        )

    owners = smp_size // CHUNKS

    def close(c):
        for feeder in feeders_of(c, 0):
            pass_up(c, feeder).wait_recv()

        whole = total_of(c, 0, feeders_of(c, 0)).astype(BF16)
        for n in range(chunk_heads):
            final[c, n] = whole[:, :, n * HEAD : (n + 1) * HEAD]
        first = c * owners
        turns = [
            (lax.rem(y + n // owners, Y_CHIPS), first + lax.rem(smp + n % owners, owners))
            for n in range(Y_CHIPS * owners)
        ]
        for py, ps in turns:

            @pl.when(py * smp_size + ps != mine)
            def _():
                last(c, (py * z_chips + z, ps), (ps - first) // 2, py, mine).start()

    def stores(c):
        narrow = pl.ds(c * cols, cols)
        wide = pl.ds(c * cols * group, cols * group)
        return [
            pltpu.make_async_copy(
                scratch.at[:, part_of], ref.at[0, :, part_of], store_sem.at[c, n]
            )
            for n, (scratch, ref, part_of) in enumerate(
                (
                    (dq_all, grad_queries_ref, wide),
                    (dk_own, grad_keys_ref, narrow),
                    (dv_own, grad_values_ref, narrow),
                )
            )
        ]

    begin(0)
    name(one_peer, pl.ds(0, others)).wait_recv()
    to_smem = pltpu.make_async_copy(named, named_s, smem_sem.at[0])
    to_smem.start()
    relay(0, 3)
    begin(1)
    relay(0, 6)
    relay(1, 3)
    to_smem.wait()
    leaves(0)
    middle = planes // 3
    send_picks(0, peers[:middle])
    relay(1, 6)
    send_picks(0, peers[middle:])
    leaves(1)
    send_picks(1, peers)
    for c in range(CHUNKS):
        keep_picks(c)
    choose()
    for load in loads:
        load.wait()
    for c in range(CHUNKS):
        all_picks(c).wait_recv()
        grads(c)
        send_partials(c)
        for copy in stores(c):
            copy.start()
    all_partials(0).wait_recv()
    add_up(0)
    for role in UP_LEAVES:
        send_up(0, role)
        send_up(0, -role)
    send_up(0, 8 * eight(0))
    send_up(0, 6)
    send_up(0, -6)
    all_partials(1).wait_recv()
    add_up(1)
    for n, role in enumerate(UP_LEAVES):
        send_up(1, role)
        send_up(1, -role)
        if n == 1:
            send_up(1, 8 * eight(1))
            send_up(0, 3)
            send_up(0, -3)
    send_up(1, 6)
    send_up(1, -6)
    close(0)
    send_up(1, 3)
    send_up(1, -3)
    close(1)

    for c in range(CHUNKS):

        @pl.when(smp // owners == c)
        def _():
            gathered[mine] = final[c, (smp // 2) % chunk_heads, y]

    all_last = pltpu.make_async_remote_copy(
        src_ref=gathered.at[pl.ds(0, others)],
        dst_ref=gathered.at[pl.ds(0, others)],
        send_sem=last_send.at[0],
        recv_sem=last_recv.at[0],
        device_id=one_peer,
        device_id_type=MESH,
    )
    all_last.wait_recv()
    got_keys = gathered[:per_array].reshape(per_array * rows, HEAD).astype(F32)
    got_values = gathered[per_array:].reshape(per_array * rows, HEAD).astype(F32)
    low = lax.broadcasted_iota(jnp.int32, got_keys.shape, 1) < HEAD // 2
    even = jnp.where(low, got_keys, pltpu.roll(got_values, HEAD // 2, 1))
    odd = jnp.where(low, pltpu.roll(got_keys, HEAD // 2, 1), got_values)
    out_ref[...] = jnp.where(smp % 2 == 0, even, odd).T.astype(BF16)

    name(one_peer, pl.ds(0, others)).wait_send()
    for c in range(CHUNKS):
        for dy in range(1, Y_CHIPS):
            spread((y + dy) % Y_CHIPS, c, keys_ref).wait_send()
        for source, step in down_tree(c):
            pass_on(c, source, step).wait_send()
        for role, _ in up_tree(c):
            pass_up(c, role).wait_send()
        for copy in stores(c):
            copy.wait()
        all_picks(c).wait_send()
        all_partials(c).wait_send()
    all_last.wait_send()


def body(
    queries, out_grad, local_keys, trajectory_values, journal_keys, journal_values, picks, lengths
):
    smp_size = lax.axis_size("smp")
    z_chips = lax.axis_size("ctx") // Y_CHIPS
    planes = Y_CHIPS * smp_size
    block_rows, features = journal_keys.shape[1:]
    blocks = Y_CHIPS * z_chips
    rows = 2 * block_rows // planes
    cols = features // CHUNKS
    tq = queries.shape[1]
    width = queries.shape[2] // (features // HEAD) // HEAD * tq
    heads = cols // HEAD
    dma = pltpu.SemaphoreType.DMA
    vmem = pltpu.VMEM
    any_space = pl.BlockSpec(memory_space=pl.ANY)
    in_smem = pl.BlockSpec(memory_space=pltpu.SMEM)
    in_vmem = pl.BlockSpec(memory_space=pltpu.VMEM)
    grad_queries, grad_local_keys, grad_local_values, summed = pl.pallas_call(
        functools.partial(fused_kernel, z_chips, smp_size),
        out_shape=(
            jax.ShapeDtypeStruct(queries.shape, BF16),
            jax.ShapeDtypeStruct(local_keys.shape, BF16),
            jax.ShapeDtypeStruct(local_keys.shape, BF16),
            jax.ShapeDtypeStruct((HEAD, block_rows), BF16),
        ),
        in_specs=[in_smem, in_smem] + [any_space] * 6,
        out_specs=(any_space, any_space, any_space, in_vmem),
        scratch_shapes=[
            vmem((blocks, rows, cols), BF16),
            vmem((blocks, rows, cols), BF16),
            vmem((CHUNKS, planes, TOP, rows, cols), BF16),
            vmem((CHUNKS, planes, TOP, rows, cols), BF16),
            vmem((planes, 1, 128), jnp.int32),
            pltpu.SMEM((planes, 1, 128), jnp.int32),
            vmem((blocks * rows, TOP * planes * rows), BF16),
            vmem((CHUNKS, blocks * rows, cols), F32),
            vmem(queries.shape[1:], BF16),
            vmem(queries.shape[1:], BF16),
            vmem(local_keys.shape[1:], BF16),
            vmem(local_keys.shape[1:], BF16),
            vmem(queries.shape[1:], BF16),
            vmem(local_keys.shape[1:], BF16),
            vmem(local_keys.shape[1:], BF16),
            vmem((TOP + 1, tq, width), F32),
            vmem((TOP + 1, tq, width), F32),
            vmem((CHUNKS, planes, TOP, rows, cols), BF16),
            vmem((TOP * planes, rows, cols), BF16),
            vmem((TOP * planes, rows, cols), BF16),
            vmem((CHUNKS, z_chips - 1, Y_CHIPS, rows, cols), BF16),
            vmem((CHUNKS, z_chips - 1, Y_CHIPS, rows, cols), BF16),
            vmem((CHUNKS, heads, Y_CHIPS, rows, HEAD), BF16),
            vmem((planes, rows, HEAD), BF16),
            dma((4,)),
            dma((CHUNKS, 3)),
            dma((CHUNKS, Y_CHIPS)),
            dma((CHUNKS, Y_CHIPS)),
            dma((CHUNKS,)),
            dma((1,)),
            dma((1,)),
            dma((2,)),
            dma((CHUNKS, z_chips - 1)),
            dma((CHUNKS, z_chips)),
            dma((CHUNKS,)),
            dma((CHUNKS,)),
            dma((CHUNKS,)),
            dma((CHUNKS,)),
            dma((CHUNKS, z_chips - 1)),
            dma((CHUNKS, z_chips - 1)),
            dma((1,)),
            dma((1,)),
        ],
        compiler_params=pltpu.CompilerParams(
            collective_id=0, has_side_effects=True, vmem_limit_bytes=56 << 20
        ),
        name="sparse_attention_grads",
    )(
        picks,
        lengths,
        queries,
        out_grad,
        local_keys,
        trajectory_values,
        journal_keys,
        journal_values,
    )
    return (
        grad_queries,
        grad_local_keys,
        grad_local_values,
        summed[: HEAD // 2].T[None],
        summed[HEAD // 2 :].T[None],
    )


def solution(mesh):
    in_specs = (
        P("smp", "ctx", None),
        P("smp", "ctx", None),
        P("smp", "ctx", None),
        P("smp", "ctx", None),
        P("ctx", None, None),
        P("ctx", None, None),
        P("smp", "ctx", None),
        P("smp"),
    )
    out_specs = (
        P("smp", "ctx", None),
        P("smp", "ctx", None),
        P("smp", "ctx", None),
        P("ctx", None, "smp"),
        P("ctx", None, "smp"),
    )
    return jax.shard_map(body, mesh=mesh, in_specs=in_specs, out_specs=out_specs, check_vma=False)
```

```python
import functools
import math

import jax
import jax.numpy as jnp
from jax import lax
from jax.experimental import pallas as pl
from jax.experimental.pallas import tpu as pltpu
from jax.sharding import PartitionSpec as P

HEAD = 128
Y_CHIPS = 4
SCALE = 1.0 / math.sqrt(HEAD)
LOG2_E = math.log2(math.e)
CHUNKS = 4
TOP = 3
MESH = pl.DeviceIdType.MESH
BF16 = jnp.bfloat16
F32 = jnp.float32


def place(z_chips):
    ctx = lax.axis_index("ctx")
    return ctx // z_chips, ctx % z_chips, lax.axis_index("smp")


def plane_of(y, z, smp, z_chips, smp_size):
    xs = smp_size // 2
    x, core = smp // 2, lax.rem(smp, 2)
    along_y = [lax.rem(y + d, Y_CHIPS) for d in range(Y_CHIPS)]
    along_smp = [
        lax.rem(x + d // 2, xs) * 2 + lax.rem(core + d % 2, 2) for d in range(smp_size)
    ]
    peers = []
    for dy in range(Y_CHIPS):
        for ds in range(smp_size):
            if dy + ds > 0:
                peers.append(
                    (
                        (along_y[dy] * z_chips + z, along_smp[ds]),
                        along_y[dy] * smp_size + along_smp[ds],
                    )
                )
    return peers


def enter(y, z, smp, z_chips, peers):
    barrier = pltpu.get_barrier_semaphore()
    near = [(y * z_chips + lax.rem(z + d, z_chips), smp) for d in along_z(z_chips)]
    for device in near + [device for device, _ in peers]:
        pl.semaphore_signal(barrier, 1, device_id=device, device_id_type=MESH)
    pl.semaphore_wait(barrier, len(near) + len(peers))


def along_z(z_chips):
    return [d % z_chips for d in (1, -1, 2, -2, 3, -3)]


def eight(c):
    return 1 if c % 2 == 0 else -1


def down_tree(c):
    sends = [(0, 3), (0, -3), (0, 1), (0, -1)]
    for side in (1, -1):
        sends += [(3 * side, 3 * side), (3 * side, side), (3 * side, -side)]
    for side in (1, -1):
        sends += [(6 * side, side), (6 * side, -side)]
    return sends + [(6 * eight(c), 2 * eight(c))]


UP_LEAVES = (5, 7, 2, 4, 1)
UP = {1: -1, 2: 1, 3: -3, 4: -1, 5: 1, 6: -3, 7: -1, 8: -2}


def up_tree(c):
    roles = [(r * side, UP[r] * side) for r in range(1, 8) for side in (1, -1)]
    return roles + [(8 * eight(c), UP[8] * eight(c))]


def fused_kernel(
    z_chips,
    smp_size,
    picks_ref,
    length_ref,
    queries_ref,
    grad_ref,
    own_keys_ref,
    own_values_ref,
    keys_ref,
    values_ref,
    grad_queries_ref,
    grad_keys_ref,
    grad_values_ref,
    out_ref,
    log_0,
    log_1,
    log_2,
    log_3,
    staged,
    fetched,
    named,
    named_s,
    chosen,
    sums,
    q_all,
    g_all,
    k_own,
    v_own,
    dq_all,
    dk_own,
    dv_own,
    scores,
    grad_probs,
    strips,
    held,
    sending,
    arriving,
    final,
    gathered,
    load_sem,
    store_sem,
    spread_send,
    spread_recv,
    own_sem,
    name_send,
    name_recv,
    smem_sem,
    ring_send,
    ring_recv,
    pick_send,
    pick_recv,
    give_send,
    give_recv,
    back_send,
    back_recv,
    last_send,
    last_recv,
):
    y, z, smp = place(z_chips)
    planes = Y_CHIPS * smp_size
    mine = y * smp_size + smp
    peers = plane_of(y, z, smp, z_chips, smp_size)
    others = planes - 1
    log = (log_0, log_1, log_2, log_3)
    rows, cols = log_0.shape[1:]
    per_array = planes // 2
    chunk_heads = cols // HEAD
    tq = q_all.shape[0]
    group = q_all.shape[1] // (CHUNKS * cols)
    width = group * tq
    lane = lax.broadcasted_iota(jnp.int32, (1, 128), 1)

    loads = [
        pltpu.make_async_copy(ref.at[0], scratch, load_sem.at[n])
        for n, (ref, scratch) in enumerate(
            (
                (queries_ref, q_all),
                (grad_ref, g_all),
                (own_keys_ref, k_own),
                (own_values_ref, v_own),
            )
        )
    ]
    named[mine] = jnp.where(
        lane == 0,
        picks_ref[0, 0, 0],
        jnp.where(lane == 1, picks_ref[0, 0, 1], picks_ref[0, 0, 2]),
    )
    enter(y, z, smp, z_chips, peers)

    def piece(ref, owner, c):
        row = pl.multiple_of((owner % per_array) * rows, rows)
        return ref.at[0, pl.ds(row, rows), pl.ds(c * cols, cols)]

    def spread(py, c, ref):
        return pltpu.make_async_remote_copy(
            src_ref=piece(ref, py * smp_size + smp, c),
            dst_ref=log[c].at[z * Y_CHIPS + y],
            send_sem=spread_send.at[c, py],
            recv_sem=spread_recv.at[c, y],
            device_id=(py * z_chips + z, smp),
            device_id_type=MESH,
        )

    def spread_in(py, c):
        return pltpu.make_async_remote_copy(
            src_ref=piece(keys_ref, mine, c),
            dst_ref=log[c].at[z * Y_CHIPS + py],
            send_sem=spread_send.at[c, py],
            recv_sem=spread_recv.at[c, py],
            device_id=(py * z_chips + z, smp),
            device_id_type=MESH,
        )

    def own(c, ref):
        return pltpu.make_async_copy(
            piece(ref, mine, c), log[c].at[z * Y_CHIPS + y], own_sem.at[c]
        )

    for c in range(CHUNKS):
        for dy in range(1, Y_CHIPS):
            py = (y + dy) % Y_CHIPS

            @pl.when(py < Y_CHIPS // 2)
            def _():
                spread(py, c, keys_ref).start()

            @pl.when(py >= Y_CHIPS // 2)
            def _():
                spread(py, c, values_ref).start()

        @pl.when(y < Y_CHIPS // 2)
        def _():
            own(c, keys_ref).start()

        @pl.when(y >= Y_CHIPS // 2)
        def _():
            own(c, values_ref).start()

    def name(device, slots):
        return pltpu.make_async_remote_copy(
            src_ref=named.at[mine] if slots is None else named.at[slots],
            dst_ref=named.at[mine] if slots is None else named.at[slots],
            send_sem=name_send.at[0],
            recv_sem=name_recv.at[0],
            device_id=device,
            device_id_type=MESH,
        )

    one_peer = peers[0][0]
    for device, _ in peers:
        name(device, None).start()
    for load in loads:
        load.start()

    def pass_on(c, source, step):
        slot = lax.rem(z + (z_chips - source) % z_chips, z_chips)
        to = lax.rem(z + step % z_chips, z_chips)
        those = log[c].at[pl.ds(slot * Y_CHIPS, Y_CHIPS)]
        return pltpu.make_async_remote_copy(
            src_ref=those,
            dst_ref=those,
            send_sem=ring_send.at[c, down_tree(c).index((source, step))],
            recv_sem=ring_recv.at[c, slot],
            device_id=(y * z_chips + to, smp),
            device_id_type=MESH,
        )

    def arrived(c, source):
        slot = lax.rem(z + (z_chips - source) % z_chips, z_chips)
        those = log[c].at[pl.ds(slot * Y_CHIPS, Y_CHIPS)]
        pltpu.make_async_remote_copy(
            src_ref=those,
            dst_ref=those,
            send_sem=ring_send.at[c, 0],
            recv_sem=ring_recv.at[c, slot],
            device_id=one_peer,
            device_id_type=MESH,
        ).wait_recv()

    def begin(c):
        for dy in range(1, Y_CHIPS):
            spread_in((y + dy) % Y_CHIPS, c).wait_recv()
        own(c, keys_ref).wait()
        relay(c, 0)

    def relay(c, distance):
        for side in (1, -1) if distance else (1,):
            source = distance * side
            if distance:
                arrived(c, source)
            for start, step in down_tree(c):
                if start == source:
                    pass_on(c, start, step).start()

    def leaves(c):
        for distance in (1, 2, 4, 5, 7):
            for side in (1, -1):
                arrived(c, distance * side)
        arrived(c, 8 * eight(c))

    def choose():
        lane_of = lax.broadcasted_iota(jnp.int32, (1, 128), 1)
        slot, row = lane_of // rows, lane_of % rows
        per_vector = 128 // rows
        codes = []
        for first in range(0, TOP * planes, per_vector):
            code = jnp.zeros((1, 128), jnp.int32)
            for j in range(per_vector):
                pick = place_of((first + j) // TOP, (first + j) % TOP)
                code = jnp.where(slot == j, pick * rows, code)
            codes.append(code + row)
        step = Y_CHIPS * rows

        def one(n, carry):
            start = pl.multiple_of(n * step, step)
            number = lax.broadcasted_iota(jnp.int32, (step, 128), 0) + start
            for m, code in enumerate(codes):
                hit = jnp.where(number == code, 1.0, 0.0)
                chosen[pl.ds(start, step), m * 128 : (m + 1) * 128] = hit.astype(BF16)
            return carry

        lax.fori_loop(0, z_chips, one, 0)

    def give(c, device, slot_send, slot_recv):
        return pltpu.make_async_remote_copy(
            src_ref=staged.at[c, slot_send],
            dst_ref=fetched.at[c, slot_recv],
            send_sem=pick_send.at[c],
            recv_sem=pick_recv.at[c],
            device_id=device,
            device_id_type=MESH,
        )

    def place_of(target, i):
        block = named_s[target, 0, i]
        return lax.rem(block, z_chips) * Y_CHIPS + lax.div(block, z_chips)

    def send_picks(c, some):
        for device, target in some:
            for i in range(TOP):
                staged[c, target, i] = log[c][place_of(target, i)]
            give(c, device, target, mine).start()

    def keep_picks(c):
        for i in range(TOP):
            fetched[c, mine, i] = log[c][place_of(mine, i)]

    def all_picks(c):
        return give(c, one_peer, pl.ds(0, others), pl.ds(0, others))

    def grads(c):
        live_rows = length_ref[0] - lax.axis_index("ctx") * tq
        live = lax.broadcasted_iota(jnp.int32, (tq, HEAD), 0) < live_rows
        across = (((1,), (1,)), ((), ()))
        down = (((0,), (0,)), ((), ()))

        def one(n, carry):
            inner = pl.ds(pl.multiple_of(n * HEAD, HEAD), HEAD)
            lanes = pl.ds(pl.multiple_of(c * cols + n * HEAD, HEAD), HEAD)
            base = (c * chunk_heads + n) * group * HEAD
            wide = [pl.ds(pl.multiple_of(base + h * HEAD, HEAD), HEAD) for h in range(group)]
            q = jnp.concatenate([q_all[:, w] for w in wide], axis=0)
            raw = [g_all[:, w] for w in wide]
            g = jnp.concatenate([jnp.where(live, r, jnp.zeros_like(r)) for r in raw], axis=0)

            def keys_of(i):
                if i == TOP:
                    return k_own[:, lanes]
                return fetched[c, :per_array, i, :, inner].reshape(tq, HEAD)

            def values_of(i):
                if i == TOP:
                    return v_own[:, lanes]
                return fetched[c, per_array:, i, :, inner].reshape(tq, HEAD)

            top = None
            for i in range(TOP + 1):
                s = lax.dot_general(keys_of(i), q, across, preferred_element_type=F32)
                if i == TOP:
                    row = lax.broadcasted_iota(jnp.int32, (tq, width), 0)
                    col = lax.broadcasted_iota(jnp.int32, (tq, width), 1) % tq
                    s = jnp.where(col >= row, s, -1e30)
                scores[i] = s
                best = jnp.max(s, axis=0, keepdims=True)
                top = best if top is None else jnp.maximum(top, best)
                grad_probs[i] = lax.dot_general(
                    values_of(i), g, across, preferred_element_type=F32
                )
            total = jnp.zeros((1, width), F32)
            delta = jnp.zeros((1, width), F32)
            for i in range(TOP + 1):
                w = jnp.exp2((scores[i] - top) * (SCALE * LOG2_E))
                scores[i] = w
                total = total + jnp.sum(w, axis=0, keepdims=True)
                delta = delta + jnp.sum(w * grad_probs[i], axis=0, keepdims=True)
            inverse = 1.0 / total
            delta = delta * inverse
            dq = None
            for i in range(TOP + 1):
                probs = scores[i] * inverse
                grad_low = (probs * (grad_probs[i] - delta)).astype(BF16)
                probs_low = probs.astype(BF16)
                dv = jnp.dot(probs_low, g, preferred_element_type=F32).astype(BF16)
                dk = jnp.dot(grad_low, q, preferred_element_type=F32) * SCALE
                dk = dk.astype(BF16)
                some = lax.dot_general(grad_low, keys_of(i), down, preferred_element_type=F32)
                dq = some if dq is None else dq + some
                if i == TOP:
                    dk_own[:, lanes] = dk
                    dv_own[:, lanes] = dv
                else:
                    strips[c, :per_array, i, :, inner] = dk.reshape(per_array, rows, HEAD)
                    strips[c, per_array:, i, :, inner] = dv.reshape(per_array, rows, HEAD)
            for h in range(group):
                dq_all[:, wide[h]] = (dq[h * tq : (h + 1) * tq] * SCALE).astype(BF16)
            return carry

        lax.fori_loop(0, chunk_heads, one, 0)

    def back(c, device, slot_send, slot_recv):
        return pltpu.make_async_remote_copy(
            src_ref=strips.at[c, slot_send],
            dst_ref=held.at[c, slot_recv],
            send_sem=give_send.at[c],
            recv_sem=give_recv.at[c],
            device_id=device,
            device_id_type=MESH,
        )

    def send_partials(c):
        for device, target in peers:
            back(c, device, target, pl.ds(TOP * mine, TOP)).start()
        for i in range(TOP):
            held[c, TOP * mine + i] = strips[c, mine, i]

    def all_partials(c):
        return pltpu.make_async_remote_copy(
            src_ref=held.at[c, pl.ds(0, TOP * others)],
            dst_ref=held.at[c, pl.ds(0, TOP * others)],
            send_sem=give_send.at[c],
            recv_sem=give_recv.at[c],
            device_id=one_peer,
            device_id_type=MESH,
        )

    def add_up(c):
        step = 4 * Y_CHIPS * rows
        those = held[c].reshape(TOP * planes * rows, cols)

        def one(n, carry):
            part = pl.ds(pl.multiple_of(n * step, step), step)
            sums[c, part] = jnp.dot(chosen[part], those, preferred_element_type=F32)
            return carry

        lax.fori_loop(0, z_chips // 4, one, 0)

    def total_of(c, role, feeders):
        step = Y_CHIPS * rows
        dest = lax.rem(z + (z_chips - role) % z_chips, z_chips)
        acc = sums[c, pl.ds(pl.multiple_of(dest * step, step), step)]
        acc = acc.reshape(Y_CHIPS, rows, cols)
        for feeder in feeders:
            acc = acc + arriving[c, slot_of(c, feeder)].astype(F32)
        return acc

    def slot_of(c, role):
        return [r for r, _ in up_tree(c)].index(role)

    def pass_up(c, role):
        slot = slot_of(c, role)
        to = lax.rem(z + up_tree(c)[slot][1] % z_chips, z_chips)
        return pltpu.make_async_remote_copy(
            src_ref=sending.at[c, slot],
            dst_ref=arriving.at[c, slot],
            send_sem=back_send.at[c, slot],
            recv_sem=back_recv.at[c, slot],
            device_id=(y * z_chips + to, smp),
            device_id_type=MESH,
        )

    def feeders_of(c, role):
        side = 1 if role > 0 else -1
        if abs(role) == 3:
            return [2 * side, 4 * side, 6 * side]
        if abs(role) == 6:
            return [5 * side, 7 * side] + ([8 * side] if side == eight(c) else [])
        return [1, -1, 3, -3] if role == 0 else []

    def send_up(c, role):
        feeders = feeders_of(c, role)
        slot = slot_of(c, role)
        for feeder in feeders:
            pass_up(c, feeder).wait_recv()

        sending[c, slot] = total_of(c, role, feeders).astype(BF16)
        pass_up(c, role).start()

    def last(c, device, head, py, slot_recv):
        return pltpu.make_async_remote_copy(
            src_ref=final.at[c, head, py],
            dst_ref=gathered.at[slot_recv],
            send_sem=last_send.at[0],
            recv_sem=last_recv.at[0],
            device_id=device,
            device_id_type=MESH,
        )

    owners = smp_size // CHUNKS

    def close(c):
        for feeder in feeders_of(c, 0):
            pass_up(c, feeder).wait_recv()

        whole = total_of(c, 0, feeders_of(c, 0)).astype(BF16)
        for n in range(chunk_heads):
            final[c, n] = whole[:, :, n * HEAD : (n + 1) * HEAD]
        first = c * owners
        turns = [
            (lax.rem(y + n // owners, Y_CHIPS), first + lax.rem(smp + n % owners, owners))
            for n in range(Y_CHIPS * owners)
        ]
        for py, ps in turns:

            @pl.when(py * smp_size + ps != mine)
            def _():
                last(c, (py * z_chips + z, ps), (ps - first) // 2, py, mine).start()

    def stores(c):
        narrow = pl.ds(pl.multiple_of(c * cols, cols), cols)
        wide = pl.ds(pl.multiple_of(c * cols * group, cols), cols * group)
        return [
            pltpu.make_async_copy(
                scratch.at[:, part_of], ref.at[0, :, part_of], store_sem.at[c, n]
            )
            for n, (scratch, ref, part_of) in enumerate(
                (
                    (dq_all, grad_queries_ref, wide),
                    (dk_own, grad_keys_ref, narrow),
                    (dv_own, grad_values_ref, narrow),
                )
            )
        ]

    begin(0)
    name(one_peer, pl.ds(0, others)).wait_recv()
    to_smem = pltpu.make_async_copy(named, named_s, smem_sem.at[0])
    to_smem.start()
    for stage in range(CHUNKS + 3):
        if stage == 2:
            to_smem.wait()
        if 0 <= stage - 2 < CHUNKS:
            relay(stage - 2, 6)
        if 0 <= stage - 1 < CHUNKS:
            relay(stage - 1, 3)
        if 0 < stage < CHUNKS:
            begin(stage)
        if 0 <= stage - 3 < CHUNKS:
            leaves(stage - 3)
            send_picks(stage - 3, peers)
            keep_picks(stage - 3)
    choose()
    for load in loads:
        load.wait()

    def heads(c, carry):
        all_picks(c).wait_recv()
        grads(c)
        send_partials(c)
        for copy in stores(c):
            copy.start()
        return carry

    lax.fori_loop(0, CHUNKS, heads, 0)
    for stage in range(CHUNKS + 3):
        if 0 <= stage < CHUNKS:
            all_partials(stage).wait_recv()
            add_up(stage)
            for role in UP_LEAVES:
                send_up(stage, role)
                send_up(stage, -role)
            send_up(stage, 8 * eight(stage))
        if 0 <= stage - 1 < CHUNKS:
            send_up(stage - 1, 6)
            send_up(stage - 1, -6)
        if 0 <= stage - 2 < CHUNKS:
            send_up(stage - 2, 3)
            send_up(stage - 2, -3)
        if 0 <= stage - 3 < CHUNKS:
            close(stage - 3)

    for c in range(CHUNKS):

        @pl.when(smp // owners == c)
        def _():
            gathered[mine] = final[c, (smp // 2) % chunk_heads, y]

    all_last = pltpu.make_async_remote_copy(
        src_ref=gathered.at[pl.ds(0, others)],
        dst_ref=gathered.at[pl.ds(0, others)],
        send_sem=last_send.at[0],
        recv_sem=last_recv.at[0],
        device_id=one_peer,
        device_id_type=MESH,
    )
    all_last.wait_recv()
    got_keys = gathered[:per_array].reshape(per_array * rows, HEAD).astype(F32)
    got_values = gathered[per_array:].reshape(per_array * rows, HEAD).astype(F32)
    low = lax.broadcasted_iota(jnp.int32, got_keys.shape, 1) < HEAD // 2
    even = jnp.where(low, got_keys, pltpu.roll(got_values, HEAD // 2, 1))
    odd = jnp.where(low, pltpu.roll(got_keys, HEAD // 2, 1), got_values)
    out_ref[...] = jnp.where(smp % 2 == 0, even, odd).T.astype(BF16)

    name(one_peer, pl.ds(0, others)).wait_send()
    for c in range(CHUNKS):
        for dy in range(1, Y_CHIPS):
            spread((y + dy) % Y_CHIPS, c, keys_ref).wait_send()
        for source, step in down_tree(c):
            pass_on(c, source, step).wait_send()
        for role, _ in up_tree(c):
            pass_up(c, role).wait_send()
        for copy in stores(c):
            copy.wait()
        all_picks(c).wait_send()
        all_partials(c).wait_send()
    all_last.wait_send()


def hand_over_kernel(grad_queries, grad_keys, grad_values, summed, *rest):
    outs, sem = rest[:5], rest[5]
    quarter = grad_queries.shape[1] // 4
    parts = [
        (grad_queries.at[:, n * quarter : (n + 1) * quarter], outs[0].at[:, n * quarter : (n + 1) * quarter])
        for n in range(4)
    ]
    parts += [(grad_keys, outs[1]), (grad_values, outs[2])]
    parts += [(summed.at[: HEAD // 2], outs[3]), (summed.at[HEAD // 2 :], outs[4])]
    copies = [pltpu.make_async_copy(a, b, sem.at[n]) for n, (a, b) in enumerate(parts)]
    for copy in copies:
        copy.start()
    for copy in copies:
        copy.wait()


def body(
    queries, out_grad, local_keys, trajectory_values, journal_keys, journal_values, picks, lengths
):
    smp_size = lax.axis_size("smp")
    z_chips = lax.axis_size("ctx") // Y_CHIPS
    planes = Y_CHIPS * smp_size
    block_rows, features = journal_keys.shape[1:]
    blocks = Y_CHIPS * z_chips
    rows = 2 * block_rows // planes
    cols = features // CHUNKS
    tq = queries.shape[1]
    width = queries.shape[2] // (features // HEAD) // HEAD * tq
    heads = cols // HEAD
    dma = pltpu.SemaphoreType.DMA
    vmem = pltpu.VMEM
    any_space = pl.BlockSpec(memory_space=pl.ANY)
    in_smem = pl.BlockSpec(memory_space=pltpu.SMEM)
    in_vmem = pl.BlockSpec(memory_space=pltpu.VMEM)
    grad_queries, grad_local_keys, grad_local_values, summed = pl.pallas_call(
        functools.partial(fused_kernel, z_chips, smp_size),
        out_shape=(
            jax.ShapeDtypeStruct(queries.shape, BF16),
            jax.ShapeDtypeStruct(local_keys.shape, BF16),
            jax.ShapeDtypeStruct(local_keys.shape, BF16),
            jax.ShapeDtypeStruct((HEAD, block_rows), BF16),
        ),
        in_specs=[in_smem, in_smem] + [any_space] * 6,
        out_specs=(any_space, any_space, any_space, in_vmem),
        scratch_shapes=[
            vmem((blocks, rows, cols), BF16),
            vmem((blocks, rows, cols), BF16),
            vmem((blocks, rows, cols), BF16),
            vmem((blocks, rows, cols), BF16),
            vmem((CHUNKS, planes, TOP, rows, cols), BF16),
            vmem((CHUNKS, planes, TOP, rows, cols), BF16),
            vmem((planes, 1, 128), jnp.int32),
            pltpu.SMEM((planes, 1, 128), jnp.int32),
            vmem((blocks * rows, TOP * planes * rows), BF16),
            vmem((CHUNKS, blocks * rows, cols), F32),
            vmem(queries.shape[1:], BF16),
            vmem(queries.shape[1:], BF16),
            vmem(local_keys.shape[1:], BF16),
            vmem(local_keys.shape[1:], BF16),
            vmem(queries.shape[1:], BF16),
            vmem(local_keys.shape[1:], BF16),
            vmem(local_keys.shape[1:], BF16),
            vmem((TOP + 1, tq, width), F32),
            vmem((TOP + 1, tq, width), F32),
            vmem((CHUNKS, planes, TOP, rows, cols), BF16),
            vmem((CHUNKS, TOP * planes, rows, cols), BF16),
            vmem((CHUNKS, z_chips - 1, Y_CHIPS, rows, cols), BF16),
            vmem((CHUNKS, z_chips - 1, Y_CHIPS, rows, cols), BF16),
            vmem((CHUNKS, heads, Y_CHIPS, rows, HEAD), BF16),
            vmem((planes, rows, HEAD), BF16),
            dma((4,)),
            dma((CHUNKS, 3)),
            dma((CHUNKS, Y_CHIPS)),
            dma((CHUNKS, Y_CHIPS)),
            dma((CHUNKS,)),
            dma((1,)),
            dma((1,)),
            dma((2,)),
            dma((CHUNKS, z_chips - 1)),
            dma((CHUNKS, z_chips)),
            dma((CHUNKS,)),
            dma((CHUNKS,)),
            dma((CHUNKS,)),
            dma((CHUNKS,)),
            dma((CHUNKS, z_chips - 1)),
            dma((CHUNKS, z_chips - 1)),
            dma((1,)),
            dma((1,)),
        ],
        compiler_params=pltpu.CompilerParams(
            collective_id=0, has_side_effects=True, vmem_limit_bytes=56 << 20
        ),
        name="sparse_attention_grads",
    )(
        picks,
        lengths,
        queries,
        out_grad,
        local_keys,
        trajectory_values,
        journal_keys,
        journal_values,
    )
    half_head = jax.ShapeDtypeStruct((HEAD // 2, block_rows), BF16)
    results = pl.pallas_call(
        hand_over_kernel,
        out_shape=(
            jax.ShapeDtypeStruct(queries.shape, BF16),
            jax.ShapeDtypeStruct(local_keys.shape, BF16),
            jax.ShapeDtypeStruct(local_keys.shape, BF16),
            half_head,
            half_head,
        ),
        in_specs=[any_space] * 4,
        out_specs=(any_space,) * 5,
        scratch_shapes=[dma((8,))],
        compiler_params=pltpu.CompilerParams(vmem_limit_bytes=56 << 20),
        name="hand_over",
    )(grad_queries, grad_local_keys, grad_local_values, summed)
    return results[:3] + (results[3].T[None], results[4].T[None])


def solution(mesh):
    in_specs = (
        P("smp", "ctx", None),
        P("smp", "ctx", None),
        P("smp", "ctx", None),
        P("smp", "ctx", None),
        P("ctx", None, None),
        P("ctx", None, None),
        P("smp", "ctx", None),
        P("smp"),
    )
    out_specs = (
        P("smp", "ctx", None),
        P("smp", "ctx", None),
        P("smp", "ctx", None),
        P("ctx", None, "smp"),
        P("ctx", None, "smp"),
    )
    return jax.shard_map(body, mesh=mesh, in_specs=in_specs, out_specs=out_specs, check_vma=False)
```

```python
import functools
import math

import jax
import jax.numpy as jnp
from jax import lax
from jax.experimental import pallas as pl
from jax.experimental.pallas import tpu as pltpu
from jax.sharding import PartitionSpec as P

HEAD = 128
Y_CHIPS = 4
SCALE = 1.0 / math.sqrt(HEAD)
LOG2_E = math.log2(math.e)
CHUNKS = 4
TOP = 3
MESH = pl.DeviceIdType.MESH
BF16 = jnp.bfloat16
F32 = jnp.float32


def place(z_chips):
    ctx = lax.axis_index("ctx")
    return ctx // z_chips, ctx % z_chips, lax.axis_index("smp")


def plane_of(y, z, smp, z_chips, smp_size):
    xs = smp_size // 2
    x, core = smp // 2, lax.rem(smp, 2)
    along_y = [lax.rem(y + d, Y_CHIPS) for d in range(Y_CHIPS)]
    along_smp = [
        lax.rem(x + d // 2, xs) * 2 + lax.rem(core + d % 2, 2) for d in range(smp_size)
    ]
    peers = []
    for dy in range(Y_CHIPS):
        for ds in range(smp_size):
            if dy + ds > 0:
                peers.append(
                    (
                        (along_y[dy] * z_chips + z, along_smp[ds]),
                        along_y[dy] * smp_size + along_smp[ds],
                    )
                )
    return [peers[(12 * n) % len(peers)] for n in range(len(peers))]


def enter(y, z, smp, z_chips, peers):
    barrier = pltpu.get_barrier_semaphore()
    near = [(y * z_chips + lax.rem(z + d, z_chips), smp) for d in along_z(z_chips)]
    for device in near + [device for device, _ in peers]:
        pl.semaphore_signal(barrier, 1, device_id=device, device_id_type=MESH)
    pl.semaphore_wait(barrier, len(near) + len(peers))


def along_z(z_chips):
    return [d % z_chips for d in (1, -1, 2, -2, 3, -3)]


def eight(c):
    return 1 if c % 2 == 0 else -1


def down_tree(c):
    sends = [(0, 3), (0, -3), (0, 1), (0, -1)]
    for side in (1, -1):
        sends += [(3 * side, 3 * side), (3 * side, side), (3 * side, -side)]
    for side in (1, -1):
        sends += [(6 * side, side), (6 * side, -side)]
    return sends + [(6 * eight(c), 2 * eight(c))]


UP_LEAVES = (5, 7, 2, 4, 1)
UP = {1: -1, 2: 1, 3: -3, 4: -1, 5: 1, 6: -3, 7: -1, 8: -2}


def up_tree(c):
    roles = [(r * side, UP[r] * side) for r in range(1, 8) for side in (1, -1)]
    return roles + [(8 * eight(c), UP[8] * eight(c))]


def fused_kernel(
    z_chips,
    smp_size,
    picks_ref,
    length_ref,
    queries_ref,
    grad_ref,
    own_keys_ref,
    own_values_ref,
    keys_ref,
    values_ref,
    grad_queries_ref,
    grad_keys_ref,
    grad_values_ref,
    out_ref,
    log_0,
    log_1,
    log_2,
    log_3,
    staged,
    fetched,
    named,
    named_s,
    chosen,
    sums,
    q_all,
    g_all,
    k_own,
    v_own,
    dq_all,
    dk_own,
    dv_own,
    scores,
    grad_probs,
    strips,
    held,
    sending,
    arriving,
    final,
    gathered,
    load_sem,
    store_sem,
    spread_send,
    spread_recv,
    own_sem,
    name_send,
    name_recv,
    smem_sem,
    ring_send,
    ring_recv,
    pick_send,
    pick_recv,
    give_send,
    give_recv,
    back_send,
    back_recv,
    last_send,
    last_recv,
):
    y, z, smp = place(z_chips)
    planes = Y_CHIPS * smp_size
    mine = y * smp_size + smp
    peers = plane_of(y, z, smp, z_chips, smp_size)
    others = planes - 1
    log = (log_0, log_1, log_2, log_3)
    rows, cols = log_0.shape[1:]
    per_array = planes // 2
    chunk_heads = cols // HEAD
    tq = q_all.shape[0]
    group = q_all.shape[1] // (CHUNKS * cols)
    width = group * tq
    lane = lax.broadcasted_iota(jnp.int32, (1, 128), 1)

    loads = [
        pltpu.make_async_copy(ref.at[0], scratch, load_sem.at[n])
        for n, (ref, scratch) in enumerate(
            (
                (queries_ref, q_all),
                (grad_ref, g_all),
                (own_keys_ref, k_own),
                (own_values_ref, v_own),
            )
        )
    ]
    named[mine] = jnp.where(
        lane == 0,
        picks_ref[0, 0, 0],
        jnp.where(lane == 1, picks_ref[0, 0, 1], picks_ref[0, 0, 2]),
    )
    enter(y, z, smp, z_chips, peers)

    def piece(ref, owner, c):
        row = pl.multiple_of((owner % per_array) * rows, rows)
        return ref.at[0, pl.ds(row, rows), pl.ds(c * cols, cols)]

    def spread(py, c, ref):
        return pltpu.make_async_remote_copy(
            src_ref=piece(ref, py * smp_size + smp, c),
            dst_ref=log[c].at[z * Y_CHIPS + y],
            send_sem=spread_send.at[c, py],
            recv_sem=spread_recv.at[c, y],
            device_id=(py * z_chips + z, smp),
            device_id_type=MESH,
        )

    def spread_in(py, c):
        return pltpu.make_async_remote_copy(
            src_ref=piece(keys_ref, mine, c),
            dst_ref=log[c].at[z * Y_CHIPS + py],
            send_sem=spread_send.at[c, py],
            recv_sem=spread_recv.at[c, py],
            device_id=(py * z_chips + z, smp),
            device_id_type=MESH,
        )

    def own(c, ref):
        return pltpu.make_async_copy(
            piece(ref, mine, c), log[c].at[z * Y_CHIPS + y], own_sem.at[c]
        )

    for c in range(CHUNKS):
        for dy in range(1, Y_CHIPS):
            py = (y + dy) % Y_CHIPS

            @pl.when(py < Y_CHIPS // 2)
            def _():
                spread(py, c, keys_ref).start()

            @pl.when(py >= Y_CHIPS // 2)
            def _():
                spread(py, c, values_ref).start()

        @pl.when(y < Y_CHIPS // 2)
        def _():
            own(c, keys_ref).start()

        @pl.when(y >= Y_CHIPS // 2)
        def _():
            own(c, values_ref).start()

    def name(device, slots):
        return pltpu.make_async_remote_copy(
            src_ref=named.at[mine] if slots is None else named.at[slots],
            dst_ref=named.at[mine] if slots is None else named.at[slots],
            send_sem=name_send.at[0],
            recv_sem=name_recv.at[0],
            device_id=device,
            device_id_type=MESH,
        )

    one_peer = peers[0][0]
    for device, _ in peers:
        name(device, None).start()
    for load in loads:
        load.start()

    def pass_on(c, source, step):
        slot = lax.rem(z + (z_chips - source) % z_chips, z_chips)
        to = lax.rem(z + step % z_chips, z_chips)
        those = log[c].at[pl.ds(slot * Y_CHIPS, Y_CHIPS)]
        return pltpu.make_async_remote_copy(
            src_ref=those,
            dst_ref=those,
            send_sem=ring_send.at[c, down_tree(c).index((source, step))],
            recv_sem=ring_recv.at[c, slot],
            device_id=(y * z_chips + to, smp),
            device_id_type=MESH,
        )

    def arrived(c, source):
        slot = lax.rem(z + (z_chips - source) % z_chips, z_chips)
        those = log[c].at[pl.ds(slot * Y_CHIPS, Y_CHIPS)]
        pltpu.make_async_remote_copy(
            src_ref=those,
            dst_ref=those,
            send_sem=ring_send.at[c, 0],
            recv_sem=ring_recv.at[c, slot],
            device_id=one_peer,
            device_id_type=MESH,
        ).wait_recv()

    def begin(c):
        for dy in range(1, Y_CHIPS):
            spread_in((y + dy) % Y_CHIPS, c).wait_recv()
        own(c, keys_ref).wait()
        relay(c, 0)

    def relay(c, distance):
        for side in (1, -1) if distance else (1,):
            source = distance * side
            if distance:
                arrived(c, source)
            for start, step in down_tree(c):
                if start == source:
                    pass_on(c, start, step).start()

    def leaves(c):
        for distance in (1, 2, 4, 5, 7):
            for side in (1, -1):
                arrived(c, distance * side)
        arrived(c, 8 * eight(c))

    def choose():
        lane_of = lax.broadcasted_iota(jnp.int32, (1, 128), 1)
        slot, row = lane_of // rows, lane_of % rows
        per_vector = 128 // rows
        codes = []
        for first in range(0, TOP * planes, per_vector):
            code = jnp.zeros((1, 128), jnp.int32)
            for j in range(per_vector):
                pick = place_of((first + j) // TOP, (first + j) % TOP)
                code = jnp.where(slot == j, pick * rows, code)
            codes.append(code + row)
        step = Y_CHIPS * rows

        def one(n, carry):
            start = pl.multiple_of(n * step, step)
            number = lax.broadcasted_iota(jnp.int32, (step, 128), 0) + start
            for m, code in enumerate(codes):
                hit = jnp.where(number == code, 1.0, 0.0)
                chosen[pl.ds(start, step), m * 128 : (m + 1) * 128] = hit.astype(BF16)
            return carry

        lax.fori_loop(0, z_chips, one, 0)

    def give(c, device, slot_send, slot_recv):
        return pltpu.make_async_remote_copy(
            src_ref=staged.at[c, slot_send],
            dst_ref=fetched.at[c, slot_recv],
            send_sem=pick_send.at[c],
            recv_sem=pick_recv.at[c],
            device_id=device,
            device_id_type=MESH,
        )

    def place_of(target, i):
        block = named_s[target, 0, i]
        return lax.rem(block, z_chips) * Y_CHIPS + lax.div(block, z_chips)

    def send_picks(c, some):
        for device, target in some:
            for i in range(TOP):
                staged[c, target, i] = log[c][place_of(target, i)]
            give(c, device, target, mine).start()

    def keep_picks(c):
        for i in range(TOP):
            fetched[c, mine, i] = log[c][place_of(mine, i)]

    def all_picks(c):
        return give(c, one_peer, pl.ds(0, others), pl.ds(0, others))

    def grads(c):
        live_rows = length_ref[0] - lax.axis_index("ctx") * tq
        live = lax.broadcasted_iota(jnp.int32, (tq, HEAD), 0) < live_rows
        across = (((1,), (1,)), ((), ()))
        down = (((0,), (0,)), ((), ()))

        def one(n, carry):
            inner = pl.ds(pl.multiple_of(n * HEAD, HEAD), HEAD)
            lanes = pl.ds(pl.multiple_of(c * cols + n * HEAD, HEAD), HEAD)
            base = (c * chunk_heads + n) * group * HEAD
            wide = [pl.ds(pl.multiple_of(base + h * HEAD, HEAD), HEAD) for h in range(group)]
            q = jnp.concatenate([q_all[:, w] for w in wide], axis=0)
            raw = [g_all[:, w] for w in wide]
            g = jnp.concatenate([jnp.where(live, r, jnp.zeros_like(r)) for r in raw], axis=0)

            def keys_of(i):
                if i == TOP:
                    return k_own[:, lanes]
                return fetched[c, :per_array, i, :, inner].reshape(tq, HEAD)

            def values_of(i):
                if i == TOP:
                    return v_own[:, lanes]
                return fetched[c, per_array:, i, :, inner].reshape(tq, HEAD)

            top = None
            for i in range(TOP + 1):
                s = lax.dot_general(keys_of(i), q, across, preferred_element_type=F32)
                if i == TOP:
                    row = lax.broadcasted_iota(jnp.int32, (tq, width), 0)
                    col = lax.broadcasted_iota(jnp.int32, (tq, width), 1) % tq
                    s = jnp.where(col >= row, s, -1e30)
                scores[i] = s
                best = jnp.max(s, axis=0, keepdims=True)
                top = best if top is None else jnp.maximum(top, best)
                grad_probs[i] = lax.dot_general(
                    values_of(i), g, across, preferred_element_type=F32
                )
            total = jnp.zeros((1, width), F32)
            delta = jnp.zeros((1, width), F32)
            for i in range(TOP + 1):
                w = jnp.exp2((scores[i] - top) * (SCALE * LOG2_E))
                scores[i] = w
                total = total + jnp.sum(w, axis=0, keepdims=True)
                delta = delta + jnp.sum(w * grad_probs[i], axis=0, keepdims=True)
            inverse = 1.0 / total
            delta = delta * inverse
            dq = None
            for i in range(TOP + 1):
                probs = scores[i] * inverse
                grad_low = (probs * (grad_probs[i] - delta)).astype(BF16)
                probs_low = probs.astype(BF16)
                dv = jnp.dot(probs_low, g, preferred_element_type=F32).astype(BF16)
                dk = jnp.dot(grad_low, q, preferred_element_type=F32) * SCALE
                dk = dk.astype(BF16)
                some = lax.dot_general(grad_low, keys_of(i), down, preferred_element_type=F32)
                dq = some if dq is None else dq + some
                if i == TOP:
                    dk_own[:, lanes] = dk
                    dv_own[:, lanes] = dv
                else:
                    strips[c, :per_array, i, :, inner] = dk.reshape(per_array, rows, HEAD)
                    strips[c, per_array:, i, :, inner] = dv.reshape(per_array, rows, HEAD)
            for h in range(group):
                dq_all[:, wide[h]] = (dq[h * tq : (h + 1) * tq] * SCALE).astype(BF16)
            return carry

        lax.fori_loop(0, chunk_heads, one, 0)

    def back(c, device, slot_send, slot_recv):
        return pltpu.make_async_remote_copy(
            src_ref=strips.at[c, slot_send],
            dst_ref=held.at[c, slot_recv],
            send_sem=give_send.at[c],
            recv_sem=give_recv.at[c],
            device_id=device,
            device_id_type=MESH,
        )

    def send_partials(c):
        for device, target in peers:
            back(c, device, target, pl.ds(TOP * mine, TOP)).start()
        for i in range(TOP):
            held[c, TOP * mine + i] = strips[c, mine, i]

    def all_partials(c):
        return pltpu.make_async_remote_copy(
            src_ref=held.at[c, pl.ds(0, TOP * others)],
            dst_ref=held.at[c, pl.ds(0, TOP * others)],
            send_sem=give_send.at[c],
            recv_sem=give_recv.at[c],
            device_id=one_peer,
            device_id_type=MESH,
        )

    def add_up(c):
        step = 4 * Y_CHIPS * rows
        those = held[c].reshape(TOP * planes * rows, cols)

        def one(n, carry):
            part = pl.ds(pl.multiple_of(n * step, step), step)
            sums[c, part] = jnp.dot(chosen[part], those, preferred_element_type=F32)
            return carry

        lax.fori_loop(0, z_chips // 4, one, 0)

    def total_of(c, role, feeders):
        step = Y_CHIPS * rows
        dest = lax.rem(z + (z_chips - role) % z_chips, z_chips)
        acc = sums[c, pl.ds(pl.multiple_of(dest * step, step), step)]
        acc = acc.reshape(Y_CHIPS, rows, cols)
        for feeder in feeders:
            acc = acc + arriving[c, slot_of(c, feeder)].astype(F32)
        return acc

    def slot_of(c, role):
        return [r for r, _ in up_tree(c)].index(role)

    def pass_up(c, role):
        slot = slot_of(c, role)
        to = lax.rem(z + up_tree(c)[slot][1] % z_chips, z_chips)
        return pltpu.make_async_remote_copy(
            src_ref=sending.at[c, slot],
            dst_ref=arriving.at[c, slot],
            send_sem=back_send.at[c, slot],
            recv_sem=back_recv.at[c, slot],
            device_id=(y * z_chips + to, smp),
            device_id_type=MESH,
        )

    def feeders_of(c, role):
        side = 1 if role > 0 else -1
        if abs(role) == 3:
            return [2 * side, 4 * side, 6 * side]
        if abs(role) == 6:
            return [5 * side, 7 * side] + ([8 * side] if side == eight(c) else [])
        return [1, -1, 3, -3] if role == 0 else []

    def send_up(c, role):
        feeders = feeders_of(c, role)
        slot = slot_of(c, role)
        for feeder in feeders:
            pass_up(c, feeder).wait_recv()

        sending[c, slot] = total_of(c, role, feeders).astype(BF16)
        pass_up(c, role).start()

    def last(c, device, head, py, slot_recv):
        return pltpu.make_async_remote_copy(
            src_ref=final.at[c, head, py],
            dst_ref=gathered.at[slot_recv],
            send_sem=last_send.at[0],
            recv_sem=last_recv.at[0],
            device_id=device,
            device_id_type=MESH,
        )

    owners = smp_size // CHUNKS

    def close(c):
        for feeder in feeders_of(c, 0):
            pass_up(c, feeder).wait_recv()

        whole = total_of(c, 0, feeders_of(c, 0)).astype(BF16)
        for n in range(chunk_heads):
            final[c, n] = whole[:, :, n * HEAD : (n + 1) * HEAD]
        first = c * owners
        turns = [
            (lax.rem(y + n // owners, Y_CHIPS), first + lax.rem(smp + n % owners, owners))
            for n in range(Y_CHIPS * owners)
        ]
        for py, ps in turns:

            @pl.when(py * smp_size + ps != mine)
            def _():
                last(c, (py * z_chips + z, ps), (ps - first) // 2, py, mine).start()

    def stores(c):
        narrow = pl.ds(pl.multiple_of(c * cols, cols), cols)
        wide = pl.ds(pl.multiple_of(c * cols * group, cols), cols * group)
        return [
            pltpu.make_async_copy(
                scratch.at[:, part_of], ref.at[0, :, part_of], store_sem.at[c, n]
            )
            for n, (scratch, ref, part_of) in enumerate(
                (
                    (dq_all, grad_queries_ref, wide),
                    (dk_own, grad_keys_ref, narrow),
                    (dv_own, grad_values_ref, narrow),
                )
            )
        ]

    begin(0)
    name(one_peer, pl.ds(0, others)).wait_recv()
    to_smem = pltpu.make_async_copy(named, named_s, smem_sem.at[0])
    to_smem.start()
    for stage in range(CHUNKS + 3):
        if stage == 2:
            to_smem.wait()
        if 0 <= stage - 2 < CHUNKS:
            relay(stage - 2, 6)
        if 0 <= stage - 1 < CHUNKS:
            relay(stage - 1, 3)
        if 0 < stage < CHUNKS:
            begin(stage)
        if 0 <= stage - 3 < CHUNKS:
            leaves(stage - 3)
            send_picks(stage - 3, peers)
            keep_picks(stage - 3)
    choose()
    for load in loads:
        load.wait()

    def heads(c, carry):
        all_picks(c).wait_recv()
        grads(c)
        send_partials(c)
        for copy in stores(c):
            copy.start()
        return carry

    lax.fori_loop(0, CHUNKS, heads, 0)
    for stage in range(CHUNKS + 3):
        if 0 <= stage < CHUNKS:
            all_partials(stage).wait_recv()
            add_up(stage)
            for role in UP_LEAVES:
                send_up(stage, role)
                send_up(stage, -role)
            send_up(stage, 8 * eight(stage))
        if 0 <= stage - 1 < CHUNKS:
            send_up(stage - 1, 6)
            send_up(stage - 1, -6)
        if 0 <= stage - 2 < CHUNKS:
            send_up(stage - 2, 3)
            send_up(stage - 2, -3)
        if 0 <= stage - 3 < CHUNKS:
            close(stage - 3)

    for c in range(CHUNKS):

        @pl.when(smp // owners == c)
        def _():
            gathered[mine] = final[c, (smp // 2) % chunk_heads, y]

    all_last = pltpu.make_async_remote_copy(
        src_ref=gathered.at[pl.ds(0, others)],
        dst_ref=gathered.at[pl.ds(0, others)],
        send_sem=last_send.at[0],
        recv_sem=last_recv.at[0],
        device_id=one_peer,
        device_id_type=MESH,
    )
    all_last.wait_recv()
    got_keys = gathered[:per_array].reshape(per_array * rows, HEAD).astype(F32)
    got_values = gathered[per_array:].reshape(per_array * rows, HEAD).astype(F32)
    low = lax.broadcasted_iota(jnp.int32, got_keys.shape, 1) < HEAD // 2
    even = jnp.where(low, got_keys, pltpu.roll(got_values, HEAD // 2, 1))
    odd = jnp.where(low, pltpu.roll(got_keys, HEAD // 2, 1), got_values)
    out_ref[...] = jnp.where(smp % 2 == 0, even, odd).T.astype(BF16)

    name(one_peer, pl.ds(0, others)).wait_send()
    for c in range(CHUNKS):
        for dy in range(1, Y_CHIPS):
            spread((y + dy) % Y_CHIPS, c, keys_ref).wait_send()
        for source, step in down_tree(c):
            pass_on(c, source, step).wait_send()
        for role, _ in up_tree(c):
            pass_up(c, role).wait_send()
        for copy in stores(c):
            copy.wait()
        all_picks(c).wait_send()
        all_partials(c).wait_send()
    all_last.wait_send()


def hand_over_kernel(
    grad_queries, grad_keys, grad_values, summed, out_q, out_k, out_v, out_gk, out_gv, q, k, v, both,
    load_sem, store_sem
):
    quarter = q.shape[1] // 4
    steps = []
    for n in range(4):
        rows = pl.ds(n * quarter, quarter)
        steps.append((grad_queries.at[:, rows], q.at[:, rows], out_q.at[:, rows]))
    steps.append((grad_keys, k, out_k))
    steps.append((grad_values, v, out_v))
    steps.append((summed.at[: HEAD // 2], both.at[: HEAD // 2], out_gk))
    steps.append((summed.at[HEAD // 2 :], both.at[HEAD // 2 :], out_gv))
    loads = [
        pltpu.make_async_copy(source, held, load_sem.at[n])
        for n, (source, held, _) in enumerate(steps)
    ]
    stores = [
        pltpu.make_async_copy(held, target, store_sem.at[n])
        for n, (_, held, target) in enumerate(steps)
    ]
    for load in loads:
        load.start()
    for load, store in zip(loads, stores):
        load.wait()
        store.start()
    for store in stores:
        store.wait()


def body(
    queries, out_grad, local_keys, trajectory_values, journal_keys, journal_values, picks, lengths
):
    smp_size = lax.axis_size("smp")
    z_chips = lax.axis_size("ctx") // Y_CHIPS
    planes = Y_CHIPS * smp_size
    block_rows, features = journal_keys.shape[1:]
    blocks = Y_CHIPS * z_chips
    rows = 2 * block_rows // planes
    cols = features // CHUNKS
    tq = queries.shape[1]
    width = queries.shape[2] // (features // HEAD) // HEAD * tq
    heads = cols // HEAD
    dma = pltpu.SemaphoreType.DMA
    vmem = pltpu.VMEM
    any_space = pl.BlockSpec(memory_space=pl.ANY)
    in_smem = pl.BlockSpec(memory_space=pltpu.SMEM)
    in_vmem = pl.BlockSpec(memory_space=pltpu.VMEM)
    grad_queries, grad_local_keys, grad_local_values, summed = pl.pallas_call(
        functools.partial(fused_kernel, z_chips, smp_size),
        out_shape=(
            jax.ShapeDtypeStruct(queries.shape, BF16),
            jax.ShapeDtypeStruct(local_keys.shape, BF16),
            jax.ShapeDtypeStruct(local_keys.shape, BF16),
            jax.ShapeDtypeStruct((HEAD, block_rows), BF16),
        ),
        in_specs=[in_smem, in_smem] + [any_space] * 6,
        out_specs=(any_space, any_space, any_space, in_vmem),
        scratch_shapes=[
            vmem((blocks, rows, cols), BF16),
            vmem((blocks, rows, cols), BF16),
            vmem((blocks, rows, cols), BF16),
            vmem((blocks, rows, cols), BF16),
            vmem((CHUNKS, planes, TOP, rows, cols), BF16),
            vmem((CHUNKS, planes, TOP, rows, cols), BF16),
            vmem((planes, 1, 128), jnp.int32),
            pltpu.SMEM((planes, 1, 128), jnp.int32),
            vmem((blocks * rows, TOP * planes * rows), BF16),
            vmem((CHUNKS, blocks * rows, cols), F32),
            vmem(queries.shape[1:], BF16),
            vmem(queries.shape[1:], BF16),
            vmem(local_keys.shape[1:], BF16),
            vmem(local_keys.shape[1:], BF16),
            vmem(queries.shape[1:], BF16),
            vmem(local_keys.shape[1:], BF16),
            vmem(local_keys.shape[1:], BF16),
            vmem((TOP + 1, tq, width), F32),
            vmem((TOP + 1, tq, width), F32),
            vmem((CHUNKS, planes, TOP, rows, cols), BF16),
            vmem((CHUNKS, TOP * planes, rows, cols), BF16),
            vmem((CHUNKS, z_chips - 1, Y_CHIPS, rows, cols), BF16),
            vmem((CHUNKS, z_chips - 1, Y_CHIPS, rows, cols), BF16),
            vmem((CHUNKS, heads, Y_CHIPS, rows, HEAD), BF16),
            vmem((planes, rows, HEAD), BF16),
            dma((4,)),
            dma((CHUNKS, 3)),
            dma((CHUNKS, Y_CHIPS)),
            dma((CHUNKS, Y_CHIPS)),
            dma((CHUNKS,)),
            dma((1,)),
            dma((1,)),
            dma((2,)),
            dma((CHUNKS, z_chips - 1)),
            dma((CHUNKS, z_chips)),
            dma((CHUNKS,)),
            dma((CHUNKS,)),
            dma((CHUNKS,)),
            dma((CHUNKS,)),
            dma((CHUNKS, z_chips - 1)),
            dma((CHUNKS, z_chips - 1)),
            dma((1,)),
            dma((1,)),
        ],
        compiler_params=pltpu.CompilerParams(
            collective_id=0, has_side_effects=True, vmem_limit_bytes=56 << 20
        ),
        name="sparse_attention_grads",
    )(
        picks,
        lengths,
        queries,
        out_grad,
        local_keys,
        trajectory_values,
        journal_keys,
        journal_values,
    )
    half_head = jax.ShapeDtypeStruct((HEAD // 2, block_rows), BF16)
    results = pl.pallas_call(
        hand_over_kernel,
        out_shape=(
            jax.ShapeDtypeStruct(queries.shape, BF16),
            jax.ShapeDtypeStruct(local_keys.shape, BF16),
            jax.ShapeDtypeStruct(local_keys.shape, BF16),
            half_head,
            half_head,
        ),
        in_specs=[any_space] * 4,
        out_specs=(any_space,) * 5,
        scratch_shapes=[
            vmem(queries.shape, BF16),
            vmem(local_keys.shape, BF16),
            vmem(local_keys.shape, BF16),
            vmem((HEAD, block_rows), BF16),
            dma((8,)),
            dma((8,)),
        ],
        compiler_params=pltpu.CompilerParams(vmem_limit_bytes=56 << 20),
        name="hand_over",
    )(grad_queries, grad_local_keys, grad_local_values, summed)
    return results[:3] + (results[3].T[None], results[4].T[None])


def solution(mesh):
    in_specs = (
        P("smp", "ctx", None),
        P("smp", "ctx", None),
        P("smp", "ctx", None),
        P("smp", "ctx", None),
        P("ctx", None, None),
        P("ctx", None, None),
        P("smp", "ctx", None),
        P("smp"),
    )
    out_specs = (
        P("smp", "ctx", None),
        P("smp", "ctx", None),
        P("smp", "ctx", None),
        P("ctx", None, "smp"),
        P("ctx", None, "smp"),
    )
    return jax.shard_map(body, mesh=mesh, in_specs=in_specs, out_specs=out_specs, check_vma=False)
```

```python
import functools
import math

import jax
import jax.numpy as jnp
from jax import lax
from jax.experimental import pallas as pl
from jax.experimental.pallas import tpu as pltpu
from jax.sharding import PartitionSpec as P

HEAD = 128
Y_CHIPS = 4
SCALE = 1.0 / math.sqrt(HEAD)
LOG2_E = math.log2(math.e)
CHUNKS = 4
TOP = 3
MESH = pl.DeviceIdType.MESH
BF16 = jnp.bfloat16
F32 = jnp.float32


def place(z_chips):
    ctx = lax.axis_index("ctx")
    return ctx // z_chips, ctx % z_chips, lax.axis_index("smp")


def plane_of(y, z, smp, z_chips, smp_size):
    xs = smp_size // 2
    x, core = smp // 2, lax.rem(smp, 2)
    along_y = [lax.rem(y + d, Y_CHIPS) for d in range(Y_CHIPS)]
    along_smp = [
        lax.rem(x + d // 2, xs) * 2 + lax.rem(core + d % 2, 2) for d in range(smp_size)
    ]
    peers = []
    for dy in range(Y_CHIPS):
        for ds in range(smp_size):
            if dy + ds > 0:
                peers.append(
                    (
                        (along_y[dy] * z_chips + z, along_smp[ds]),
                        along_y[dy] * smp_size + along_smp[ds],
                    )
                )
    return [peers[(12 * n) % len(peers)] for n in range(len(peers))]


def enter(y, z, smp, z_chips, peers):
    barrier = pltpu.get_barrier_semaphore()
    near = [(y * z_chips + lax.rem(z + d, z_chips), smp) for d in along_z(z_chips)]
    for device in near + [device for device, _ in peers]:
        pl.semaphore_signal(barrier, 1, device_id=device, device_id_type=MESH)
    pl.semaphore_wait(barrier, len(near) + len(peers))


def along_z(z_chips):
    return [d % z_chips for d in (1, -1, 2, -2, 3, -3)]


def eight(c):
    return 1 if c % 2 == 0 else -1


def down_tree(c):
    sends = [(0, 3), (0, -3), (0, 1), (0, -1)]
    for side in (1, -1):
        sends += [(3 * side, 3 * side), (3 * side, side), (3 * side, -side)]
    for side in (1, -1):
        sends += [(6 * side, side), (6 * side, -side)]
    return sends + [(6 * eight(c), 2 * eight(c))]


UP_LEAVES = (5, 7, 2, 4, 1)
UP = {1: -1, 2: 1, 3: -3, 4: -1, 5: 1, 6: -3, 7: -1, 8: -2}


def up_tree(c):
    roles = [(r * side, UP[r] * side) for r in range(1, 8) for side in (1, -1)]
    return roles + [(8 * eight(c), UP[8] * eight(c))]


def fused_kernel(
    z_chips,
    smp_size,
    picks_ref,
    length_ref,
    queries_ref,
    grad_ref,
    own_keys_ref,
    own_values_ref,
    keys_ref,
    values_ref,
    grad_queries_ref,
    grad_keys_ref,
    grad_values_ref,
    out_ref,
    log_0,
    log_1,
    log_2,
    log_3,
    staged,
    fetched,
    named,
    named_s,
    chosen,
    sums,
    q_all,
    g_all,
    k_own,
    v_own,
    dq_all,
    dk_own,
    dv_own,
    scores,
    grad_probs,
    strips,
    held,
    sending,
    arriving,
    final,
    gathered,
    load_sem,
    store_sem,
    spread_send,
    spread_recv,
    own_sem,
    name_send,
    name_recv,
    smem_sem,
    ring_send,
    ring_recv,
    pick_send,
    pick_recv,
    give_send,
    give_recv,
    back_send,
    back_recv,
    last_send,
    last_recv,
):
    y, z, smp = place(z_chips)
    planes = Y_CHIPS * smp_size
    mine = y * smp_size + smp
    peers = plane_of(y, z, smp, z_chips, smp_size)
    others = planes - 1
    log = (log_0, log_1, log_2, log_3)
    rows, cols = log_0.shape[1:]
    per_array = planes // 2
    chunk_heads = cols // HEAD
    tq = q_all.shape[0]
    group = q_all.shape[1] // (CHUNKS * cols)
    width = group * tq
    lane = lax.broadcasted_iota(jnp.int32, (1, 128), 1)

    loads = [
        pltpu.make_async_copy(ref.at[0], scratch, load_sem.at[n])
        for n, (ref, scratch) in enumerate(
            (
                (queries_ref, q_all),
                (grad_ref, g_all),
                (own_keys_ref, k_own),
                (own_values_ref, v_own),
            )
        )
    ]
    named[mine] = jnp.where(
        lane == 0,
        picks_ref[0, 0, 0],
        jnp.where(lane == 1, picks_ref[0, 0, 1], picks_ref[0, 0, 2]),
    )
    enter(y, z, smp, z_chips, peers)

    def piece(ref, owner, c):
        row = pl.multiple_of((owner % per_array) * rows, rows)
        return ref.at[0, pl.ds(row, rows), pl.ds(c * cols, cols)]

    def spread(py, c, ref):
        return pltpu.make_async_remote_copy(
            src_ref=piece(ref, py * smp_size + smp, c),
            dst_ref=log[c].at[z * Y_CHIPS + y],
            send_sem=spread_send.at[c, py],
            recv_sem=spread_recv.at[c, y],
            device_id=(py * z_chips + z, smp),
            device_id_type=MESH,
        )

    def spread_in(py, c):
        return pltpu.make_async_remote_copy(
            src_ref=piece(keys_ref, mine, c),
            dst_ref=log[c].at[z * Y_CHIPS + py],
            send_sem=spread_send.at[c, py],
            recv_sem=spread_recv.at[c, py],
            device_id=(py * z_chips + z, smp),
            device_id_type=MESH,
        )

    def own(c, ref):
        return pltpu.make_async_copy(
            piece(ref, mine, c), log[c].at[z * Y_CHIPS + y], own_sem.at[c]
        )

    for c in range(CHUNKS):
        for dy in range(1, Y_CHIPS):
            py = (y + dy) % Y_CHIPS

            @pl.when(py < Y_CHIPS // 2)
            def _():
                spread(py, c, keys_ref).start()

            @pl.when(py >= Y_CHIPS // 2)
            def _():
                spread(py, c, values_ref).start()

        @pl.when(y < Y_CHIPS // 2)
        def _():
            own(c, keys_ref).start()

        @pl.when(y >= Y_CHIPS // 2)
        def _():
            own(c, values_ref).start()

    def name(device, slots):
        return pltpu.make_async_remote_copy(
            src_ref=named.at[mine] if slots is None else named.at[slots],
            dst_ref=named.at[mine] if slots is None else named.at[slots],
            send_sem=name_send.at[0],
            recv_sem=name_recv.at[0],
            device_id=device,
            device_id_type=MESH,
        )

    one_peer = peers[0][0]
    for device, _ in peers:
        name(device, None).start()
    for load in loads:
        load.start()

    def pass_on(c, source, step):
        slot = lax.rem(z + (z_chips - source) % z_chips, z_chips)
        to = lax.rem(z + step % z_chips, z_chips)
        those = log[c].at[pl.ds(slot * Y_CHIPS, Y_CHIPS)]
        return pltpu.make_async_remote_copy(
            src_ref=those,
            dst_ref=those,
            send_sem=ring_send.at[c, down_tree(c).index((source, step))],
            recv_sem=ring_recv.at[c, slot],
            device_id=(y * z_chips + to, smp),
            device_id_type=MESH,
        )

    def arrived(c, source):
        slot = lax.rem(z + (z_chips - source) % z_chips, z_chips)
        those = log[c].at[pl.ds(slot * Y_CHIPS, Y_CHIPS)]
        pltpu.make_async_remote_copy(
            src_ref=those,
            dst_ref=those,
            send_sem=ring_send.at[c, 0],
            recv_sem=ring_recv.at[c, slot],
            device_id=one_peer,
            device_id_type=MESH,
        ).wait_recv()

    def begin(c):
        for dy in range(1, Y_CHIPS):
            spread_in((y + dy) % Y_CHIPS, c).wait_recv()
        own(c, keys_ref).wait()
        relay(c, 0)

    def relay(c, distance):
        for side in (1, -1) if distance else (1,):
            source = distance * side
            if distance:
                arrived(c, source)
            for start, step in down_tree(c):
                if start == source:
                    pass_on(c, start, step).start()

    def leaves(c):
        for distance in (1, 2, 4, 5, 7):
            for side in (1, -1):
                arrived(c, distance * side)
        arrived(c, 8 * eight(c))

    def choose():
        lane_of = lax.broadcasted_iota(jnp.int32, (1, 128), 1)
        slot, row = lane_of // rows, lane_of % rows
        per_vector = 128 // rows
        codes = []
        for first in range(0, TOP * planes, per_vector):
            code = jnp.zeros((1, 128), jnp.int32)
            for j in range(per_vector):
                pick = place_of((first + j) // TOP, (first + j) % TOP)
                code = jnp.where(slot == j, pick * rows, code)
            codes.append(code + row)
        step = Y_CHIPS * rows

        def one(n, carry):
            start = pl.multiple_of(n * step, step)
            number = lax.broadcasted_iota(jnp.int32, (step, 128), 0) + start
            for m, code in enumerate(codes):
                hit = jnp.where(number == code, 1.0, 0.0)
                chosen[pl.ds(start, step), m * 128 : (m + 1) * 128] = hit.astype(BF16)
            return carry

        lax.fori_loop(0, z_chips, one, 0)

    def give(c, device, slot_send, slot_recv):
        return pltpu.make_async_remote_copy(
            src_ref=staged.at[c, slot_send],
            dst_ref=fetched.at[c, slot_recv],
            send_sem=pick_send.at[c],
            recv_sem=pick_recv.at[c],
            device_id=device,
            device_id_type=MESH,
        )

    def place_of(target, i):
        block = named_s[target, 0, i]
        return lax.rem(block, z_chips) * Y_CHIPS + lax.div(block, z_chips)

    def send_picks(c, some):
        for device, target in some:
            for i in range(TOP):
                staged[c, target, i] = log[c][place_of(target, i)]
            give(c, device, target, mine).start()

    def keep_picks(c):
        for i in range(TOP):
            fetched[c, mine, i] = log[c][place_of(mine, i)]

    def all_picks(c):
        return give(c, one_peer, pl.ds(0, others), pl.ds(0, others))

    def grads(c):
        live_rows = length_ref[0] - lax.axis_index("ctx") * tq
        live = lax.broadcasted_iota(jnp.int32, (tq, HEAD), 0) < live_rows
        across = (((1,), (1,)), ((), ()))
        down = (((0,), (0,)), ((), ()))

        def one(n, carry):
            inner = pl.ds(pl.multiple_of(n * HEAD, HEAD), HEAD)
            lanes = pl.ds(pl.multiple_of(c * cols + n * HEAD, HEAD), HEAD)
            base = (c * chunk_heads + n) * group * HEAD
            wide = [pl.ds(pl.multiple_of(base + h * HEAD, HEAD), HEAD) for h in range(group)]
            q = jnp.concatenate([q_all[:, w] for w in wide], axis=0)
            raw = [g_all[:, w] for w in wide]
            g = jnp.concatenate([jnp.where(live, r, jnp.zeros_like(r)) for r in raw], axis=0)

            def keys_of(i):
                if i == TOP:
                    return k_own[:, lanes]
                return fetched[c, :per_array, i, :, inner].reshape(tq, HEAD)

            def values_of(i):
                if i == TOP:
                    return v_own[:, lanes]
                return fetched[c, per_array:, i, :, inner].reshape(tq, HEAD)

            top = None
            for i in range(TOP + 1):
                s = lax.dot_general(keys_of(i), q, across, preferred_element_type=F32)
                if i == TOP:
                    row = lax.broadcasted_iota(jnp.int32, (tq, width), 0)
                    col = lax.broadcasted_iota(jnp.int32, (tq, width), 1) % tq
                    s = jnp.where(col >= row, s, -1e30)
                scores[i] = s
                best = jnp.max(s, axis=0, keepdims=True)
                top = best if top is None else jnp.maximum(top, best)
                grad_probs[i] = lax.dot_general(
                    values_of(i), g, across, preferred_element_type=F32
                )
            total = jnp.zeros((1, width), F32)
            delta = jnp.zeros((1, width), F32)
            for i in range(TOP + 1):
                w = jnp.exp2((scores[i] - top) * (SCALE * LOG2_E))
                scores[i] = w
                total = total + jnp.sum(w, axis=0, keepdims=True)
                delta = delta + jnp.sum(w * grad_probs[i], axis=0, keepdims=True)
            inverse = 1.0 / total
            delta = delta * inverse
            dq = None
            for i in range(TOP + 1):
                probs = scores[i] * inverse
                grad_low = (probs * (grad_probs[i] - delta)).astype(BF16)
                probs_low = probs.astype(BF16)
                dv = jnp.dot(probs_low, g, preferred_element_type=F32).astype(BF16)
                dk = jnp.dot(grad_low, q, preferred_element_type=F32) * SCALE
                dk = dk.astype(BF16)
                some = lax.dot_general(grad_low, keys_of(i), down, preferred_element_type=F32)
                dq = some if dq is None else dq + some
                if i == TOP:
                    dk_own[:, lanes] = dk
                    dv_own[:, lanes] = dv
                else:
                    strips[c, :per_array, i, :, inner] = dk.reshape(per_array, rows, HEAD)
                    strips[c, per_array:, i, :, inner] = dv.reshape(per_array, rows, HEAD)
            for h in range(group):
                dq_all[:, wide[h]] = (dq[h * tq : (h + 1) * tq] * SCALE).astype(BF16)
            return carry

        lax.fori_loop(0, chunk_heads, one, 0)

    def back(c, device, slot_send, slot_recv):
        return pltpu.make_async_remote_copy(
            src_ref=strips.at[c, slot_send],
            dst_ref=held.at[c, slot_recv],
            send_sem=give_send.at[c],
            recv_sem=give_recv.at[c],
            device_id=device,
            device_id_type=MESH,
        )

    def send_partials(c):
        for device, target in peers:
            back(c, device, target, pl.ds(TOP * mine, TOP)).start()
        for i in range(TOP):
            held[c, TOP * mine + i] = strips[c, mine, i]

    def all_partials(c):
        return pltpu.make_async_remote_copy(
            src_ref=held.at[c, pl.ds(0, TOP * others)],
            dst_ref=held.at[c, pl.ds(0, TOP * others)],
            send_sem=give_send.at[c],
            recv_sem=give_recv.at[c],
            device_id=one_peer,
            device_id_type=MESH,
        )

    def add_up(c):
        step = 4 * Y_CHIPS * rows
        those = held[c].reshape(TOP * planes * rows, cols)

        def one(n, carry):
            part = pl.ds(pl.multiple_of(n * step, step), step)
            sums[c, part] = jnp.dot(chosen[part], those, preferred_element_type=F32)
            return carry

        lax.fori_loop(0, z_chips // 4, one, 0)

    def total_of(c, role, feeders):
        step = Y_CHIPS * rows
        dest = lax.rem(z + (z_chips - role) % z_chips, z_chips)
        acc = sums[c, pl.ds(pl.multiple_of(dest * step, step), step)]
        acc = acc.reshape(Y_CHIPS, rows, cols)
        for feeder in feeders:
            acc = acc + arriving[c, slot_of(c, feeder)].astype(F32)
        return acc

    def slot_of(c, role):
        return [r for r, _ in up_tree(c)].index(role)

    def pass_up(c, role):
        slot = slot_of(c, role)
        to = lax.rem(z + up_tree(c)[slot][1] % z_chips, z_chips)
        return pltpu.make_async_remote_copy(
            src_ref=sending.at[c, slot],
            dst_ref=arriving.at[c, slot],
            send_sem=back_send.at[c, slot],
            recv_sem=back_recv.at[c, slot],
            device_id=(y * z_chips + to, smp),
            device_id_type=MESH,
        )

    def feeders_of(c, role):
        side = 1 if role > 0 else -1
        if abs(role) == 3:
            return [2 * side, 4 * side, 6 * side]
        if abs(role) == 6:
            return [5 * side, 7 * side] + ([8 * side] if side == eight(c) else [])
        return [1, -1, 3, -3] if role == 0 else []

    def send_up(c, role):
        feeders = feeders_of(c, role)
        slot = slot_of(c, role)
        for feeder in feeders:
            pass_up(c, feeder).wait_recv()

        sending[c, slot] = total_of(c, role, feeders).astype(BF16)
        pass_up(c, role).start()

    def last(c, device, head, py, slot_recv):
        return pltpu.make_async_remote_copy(
            src_ref=final.at[c, head, py],
            dst_ref=gathered.at[slot_recv],
            send_sem=last_send.at[0],
            recv_sem=last_recv.at[0],
            device_id=device,
            device_id_type=MESH,
        )

    owners = smp_size // CHUNKS

    def close(c):
        for feeder in feeders_of(c, 0):
            pass_up(c, feeder).wait_recv()

        whole = total_of(c, 0, feeders_of(c, 0)).astype(BF16)
        for n in range(chunk_heads):
            final[c, n] = whole[:, :, n * HEAD : (n + 1) * HEAD]
        first = c * owners
        turns = [
            (lax.rem(y + n // owners, Y_CHIPS), first + lax.rem(smp + n % owners, owners))
            for n in range(Y_CHIPS * owners)
        ]
        for py, ps in turns:

            @pl.when(py * smp_size + ps != mine)
            def _():
                last(c, (py * z_chips + z, ps), (ps - first) // 2, py, mine).start()

    def stores(c):
        narrow = pl.ds(pl.multiple_of(c * cols, cols), cols)
        wide = pl.ds(pl.multiple_of(c * cols * group, cols), cols * group)
        return [
            pltpu.make_async_copy(
                scratch.at[:, part_of], ref.at[0, :, part_of], store_sem.at[c, n]
            )
            for n, (scratch, ref, part_of) in enumerate(
                (
                    (dq_all, grad_queries_ref, wide),
                    (dk_own, grad_keys_ref, narrow),
                    (dv_own, grad_values_ref, narrow),
                )
            )
        ]

    begin(0)
    name(one_peer, pl.ds(0, others)).wait_recv()
    to_smem = pltpu.make_async_copy(named, named_s, smem_sem.at[0])
    to_smem.start()
    def serve_picks(c):
        leaves(c)
        send_picks(c, peers)
        keep_picks(c)

    for stage in range(CHUNKS + 2):
        if stage == 2:
            to_smem.wait()
            choose()
        if 0 <= stage - 2 < CHUNKS:
            relay(stage - 2, 6)
        if 0 <= stage - 1 < CHUNKS:
            relay(stage - 1, 3)
        if 0 < stage < CHUNKS:
            begin(stage)
        if 0 <= stage - 3 < CHUNKS - 1:
            serve_picks(stage - 3)
    for load in loads:
        load.wait()

    def climb(c):
        all_partials(c).wait_recv()
        add_up(c)
        for role in UP_LEAVES:
            send_up(c, role)
            send_up(c, -role)
        send_up(c, 8 * eight(c))

    def heads(c, carry):
        all_picks(c).wait_recv()
        grads(c)
        send_partials(c)
        for copy in stores(c):
            copy.start()

        @pl.when(c == 0)
        def _():
            serve_picks(CHUNKS - 1)

        @pl.when(c == CHUNKS - 2)
        def _():
            climb(0)

        return carry

    lax.fori_loop(0, CHUNKS, heads, 0)
    for stage in range(1, CHUNKS + 3):
        if stage < CHUNKS:
            climb(stage)
        if 0 <= stage - 1 < CHUNKS:
            send_up(stage - 1, 6)
            send_up(stage - 1, -6)
        if 0 <= stage - 2 < CHUNKS:
            send_up(stage - 2, 3)
            send_up(stage - 2, -3)
        if 0 <= stage - 3 < CHUNKS:
            close(stage - 3)

    for c in range(CHUNKS):

        @pl.when(smp // owners == c)
        def _():
            gathered[mine] = final[c, (smp // 2) % chunk_heads, y]

    all_last = pltpu.make_async_remote_copy(
        src_ref=gathered.at[pl.ds(0, others)],
        dst_ref=gathered.at[pl.ds(0, others)],
        send_sem=last_send.at[0],
        recv_sem=last_recv.at[0],
        device_id=one_peer,
        device_id_type=MESH,
    )
    all_last.wait_recv()
    got_keys = gathered[:per_array].reshape(per_array * rows, HEAD).astype(F32)
    got_values = gathered[per_array:].reshape(per_array * rows, HEAD).astype(F32)
    low = lax.broadcasted_iota(jnp.int32, got_keys.shape, 1) < HEAD // 2
    even = jnp.where(low, got_keys, pltpu.roll(got_values, HEAD // 2, 1))
    odd = jnp.where(low, pltpu.roll(got_keys, HEAD // 2, 1), got_values)
    out_ref[...] = jnp.where(smp % 2 == 0, even, odd).T.astype(BF16)

    name(one_peer, pl.ds(0, others)).wait_send()
    for c in range(CHUNKS):
        for dy in range(1, Y_CHIPS):
            spread((y + dy) % Y_CHIPS, c, keys_ref).wait_send()
        for source, step in down_tree(c):
            pass_on(c, source, step).wait_send()
        for role, _ in up_tree(c):
            pass_up(c, role).wait_send()
        for copy in stores(c):
            copy.wait()
        all_picks(c).wait_send()
        all_partials(c).wait_send()
    all_last.wait_send()


def hand_over_kernel(
    grad_queries, grad_keys, grad_values, summed, out_q, out_k, out_v, out_gk, out_gv, q, k, v, both,
    load_sem, store_sem
):
    quarter = q.shape[1] // 4
    steps = []
    for n in range(4):
        rows = pl.ds(n * quarter, quarter)
        steps.append((grad_queries.at[:, rows], q.at[:, rows], out_q.at[:, rows]))
    steps.append((grad_keys, k, out_k))
    steps.append((grad_values, v, out_v))
    steps.append((summed.at[: HEAD // 2], both.at[: HEAD // 2], out_gk))
    steps.append((summed.at[HEAD // 2 :], both.at[HEAD // 2 :], out_gv))
    loads = [
        pltpu.make_async_copy(source, held, load_sem.at[n])
        for n, (source, held, _) in enumerate(steps)
    ]
    stores = [
        pltpu.make_async_copy(held, target, store_sem.at[n])
        for n, (_, held, target) in enumerate(steps)
    ]
    for load in loads:
        load.start()
    for load, store in zip(loads, stores):
        load.wait()
        store.start()
    for store in stores:
        store.wait()


def body(
    queries, out_grad, local_keys, trajectory_values, journal_keys, journal_values, picks, lengths
):
    smp_size = lax.axis_size("smp")
    z_chips = lax.axis_size("ctx") // Y_CHIPS
    planes = Y_CHIPS * smp_size
    block_rows, features = journal_keys.shape[1:]
    blocks = Y_CHIPS * z_chips
    rows = 2 * block_rows // planes
    cols = features // CHUNKS
    tq = queries.shape[1]
    width = queries.shape[2] // (features // HEAD) // HEAD * tq
    heads = cols // HEAD
    dma = pltpu.SemaphoreType.DMA
    vmem = pltpu.VMEM
    any_space = pl.BlockSpec(memory_space=pl.ANY)
    in_smem = pl.BlockSpec(memory_space=pltpu.SMEM)
    in_vmem = pl.BlockSpec(memory_space=pltpu.VMEM)
    grad_queries, grad_local_keys, grad_local_values, summed = pl.pallas_call(
        functools.partial(fused_kernel, z_chips, smp_size),
        out_shape=(
            jax.ShapeDtypeStruct(queries.shape, BF16),
            jax.ShapeDtypeStruct(local_keys.shape, BF16),
            jax.ShapeDtypeStruct(local_keys.shape, BF16),
            jax.ShapeDtypeStruct((HEAD, block_rows), BF16),
        ),
        in_specs=[in_smem, in_smem] + [any_space] * 6,
        out_specs=(any_space, any_space, any_space, in_vmem),
        scratch_shapes=[
            vmem((blocks, rows, cols), BF16),
            vmem((blocks, rows, cols), BF16),
            vmem((blocks, rows, cols), BF16),
            vmem((blocks, rows, cols), BF16),
            vmem((CHUNKS, planes, TOP, rows, cols), BF16),
            vmem((CHUNKS, planes, TOP, rows, cols), BF16),
            vmem((planes, 1, 128), jnp.int32),
            pltpu.SMEM((planes, 1, 128), jnp.int32),
            vmem((blocks * rows, TOP * planes * rows), BF16),
            vmem((CHUNKS, blocks * rows, cols), F32),
            vmem(queries.shape[1:], BF16),
            vmem(queries.shape[1:], BF16),
            vmem(local_keys.shape[1:], BF16),
            vmem(local_keys.shape[1:], BF16),
            vmem(queries.shape[1:], BF16),
            vmem(local_keys.shape[1:], BF16),
            vmem(local_keys.shape[1:], BF16),
            vmem((TOP + 1, tq, width), F32),
            vmem((TOP + 1, tq, width), F32),
            vmem((CHUNKS, planes, TOP, rows, cols), BF16),
            vmem((CHUNKS, TOP * planes, rows, cols), BF16),
            vmem((CHUNKS, z_chips - 1, Y_CHIPS, rows, cols), BF16),
            vmem((CHUNKS, z_chips - 1, Y_CHIPS, rows, cols), BF16),
            vmem((CHUNKS, heads, Y_CHIPS, rows, HEAD), BF16),
            vmem((planes, rows, HEAD), BF16),
            dma((4,)),
            dma((CHUNKS, 3)),
            dma((CHUNKS, Y_CHIPS)),
            dma((CHUNKS, Y_CHIPS)),
            dma((CHUNKS,)),
            dma((1,)),
            dma((1,)),
            dma((2,)),
            dma((CHUNKS, z_chips - 1)),
            dma((CHUNKS, z_chips)),
            dma((CHUNKS,)),
            dma((CHUNKS,)),
            dma((CHUNKS,)),
            dma((CHUNKS,)),
            dma((CHUNKS, z_chips - 1)),
            dma((CHUNKS, z_chips - 1)),
            dma((1,)),
            dma((1,)),
        ],
        compiler_params=pltpu.CompilerParams(
            collective_id=0, has_side_effects=True, vmem_limit_bytes=56 << 20
        ),
        name="sparse_attention_grads",
    )(
        picks,
        lengths,
        queries,
        out_grad,
        local_keys,
        trajectory_values,
        journal_keys,
        journal_values,
    )
    half_head = jax.ShapeDtypeStruct((HEAD // 2, block_rows), BF16)
    results = pl.pallas_call(
        hand_over_kernel,
        out_shape=(
            jax.ShapeDtypeStruct(queries.shape, BF16),
            jax.ShapeDtypeStruct(local_keys.shape, BF16),
            jax.ShapeDtypeStruct(local_keys.shape, BF16),
            half_head,
            half_head,
        ),
        in_specs=[any_space] * 4,
        out_specs=(any_space,) * 5,
        scratch_shapes=[
            vmem(queries.shape, BF16),
            vmem(local_keys.shape, BF16),
            vmem(local_keys.shape, BF16),
            vmem((HEAD, block_rows), BF16),
            dma((8,)),
            dma((8,)),
        ],
        compiler_params=pltpu.CompilerParams(vmem_limit_bytes=56 << 20),
        name="hand_over",
    )(grad_queries, grad_local_keys, grad_local_values, summed)
    return results[:3] + (results[3].T[None], results[4].T[None])


def solution(mesh):
    in_specs = (
        P("smp", "ctx", None),
        P("smp", "ctx", None),
        P("smp", "ctx", None),
        P("smp", "ctx", None),
        P("ctx", None, None),
        P("ctx", None, None),
        P("smp", "ctx", None),
        P("smp"),
    )
    out_specs = (
        P("smp", "ctx", None),
        P("smp", "ctx", None),
        P("smp", "ctx", None),
        P("ctx", None, "smp"),
        P("ctx", None, "smp"),
    )
    return jax.shard_map(body, mesh=mesh, in_specs=in_specs, out_specs=out_specs, check_vma=False)
```

```python
import functools
import math

import jax
import jax.numpy as jnp
from jax import lax
from jax.experimental import pallas as pl
from jax.experimental.pallas import tpu as pltpu
from jax.sharding import PartitionSpec as P

HEAD = 128
Y_CHIPS = 4
SCALE = 1.0 / math.sqrt(HEAD)
LOG2_E = math.log2(math.e)
CHUNKS = 4
TOP = 3
MESH = pl.DeviceIdType.MESH
BF16 = jnp.bfloat16
F32 = jnp.float32


def place(z_chips):
    ctx = lax.axis_index("ctx")
    return ctx // z_chips, ctx % z_chips, lax.axis_index("smp")


def plane_of(y, z, smp, z_chips, smp_size):
    xs = smp_size // 2
    x, core = smp // 2, lax.rem(smp, 2)
    along_y = [lax.rem(y + d, Y_CHIPS) for d in range(Y_CHIPS)]
    along_smp = [
        lax.rem(x + d // 2, xs) * 2 + lax.rem(core + d % 2, 2) for d in range(smp_size)
    ]
    peers = []
    for dy in range(Y_CHIPS):
        for ds in range(smp_size):
            if dy + ds > 0:
                peers.append(
                    (
                        (along_y[dy] * z_chips + z, along_smp[ds]),
                        along_y[dy] * smp_size + along_smp[ds],
                    )
                )
    return [peers[(12 * n) % len(peers)] for n in range(len(peers))]


def enter(y, z, smp, z_chips, peers):
    barrier = pltpu.get_barrier_semaphore()
    near = [(y * z_chips + lax.rem(z + d, z_chips), smp) for d in along_z(z_chips)]
    for device in near + [device for device, _ in peers]:
        pl.semaphore_signal(barrier, 1, device_id=device, device_id_type=MESH)
    pl.semaphore_wait(barrier, len(near) + len(peers))


def along_z(z_chips):
    return [d % z_chips for d in (1, -1, 2, -2, 3, -3)]


def eight(c):
    return 1 if c % 2 == 0 else -1


def down_tree(c):
    sends = [(0, 3), (0, -3), (0, 1), (0, -1)]
    for side in (1, -1):
        sends += [(3 * side, 3 * side), (3 * side, side), (3 * side, -side)]
    for side in (1, -1):
        sends += [(6 * side, side), (6 * side, -side)]
    return sends + [(6 * eight(c), 2 * eight(c))]


UP_LEAVES = (5, 7, 2, 4, 1)
UP = {1: -1, 2: 1, 3: -3, 4: -1, 5: 1, 6: -3, 7: -1, 8: -2}


def up_tree(c):
    roles = [(r * side, UP[r] * side) for r in range(1, 8) for side in (1, -1)]
    return roles + [(8 * eight(c), UP[8] * eight(c))]


def fused_kernel(
    z_chips,
    smp_size,
    picks_ref,
    length_ref,
    queries_ref,
    grad_ref,
    own_keys_ref,
    own_values_ref,
    keys_ref,
    values_ref,
    grad_queries_ref,
    grad_keys_ref,
    grad_values_ref,
    out_ref,
    log_0,
    log_1,
    log_2,
    log_3,
    staged,
    fetched,
    named,
    named_s,
    chosen,
    sums,
    q_all,
    g_all,
    k_own,
    v_own,
    dq_all,
    dk_own,
    dv_own,
    scores,
    grad_probs,
    strips,
    held,
    sending,
    arriving,
    final,
    gathered,
    load_sem,
    store_sem,
    spread_send,
    spread_recv,
    own_sem,
    name_send,
    name_recv,
    smem_sem,
    ring_send,
    ring_recv,
    pick_send,
    pick_recv,
    give_send,
    give_recv,
    back_send,
    back_recv,
    last_send,
    last_recv,
):
    y, z, smp = place(z_chips)
    planes = Y_CHIPS * smp_size
    mine = y * smp_size + smp
    peers = plane_of(y, z, smp, z_chips, smp_size)
    others = planes - 1
    log = (log_0, log_1, log_2, log_3)
    rows, cols = log_0.shape[1:]
    per_array = planes // 2
    chunk_heads = cols // HEAD
    tq = q_all.shape[0]
    group = q_all.shape[1] // (CHUNKS * cols)
    width = group * tq
    lane = lax.broadcasted_iota(jnp.int32, (1, 128), 1)

    loads = [
        pltpu.make_async_copy(ref.at[0], scratch, load_sem.at[n])
        for n, (ref, scratch) in enumerate(
            (
                (queries_ref, q_all),
                (grad_ref, g_all),
                (own_keys_ref, k_own),
                (own_values_ref, v_own),
            )
        )
    ]
    named[mine] = jnp.where(
        lane == 0,
        picks_ref[0, 0, 0],
        jnp.where(lane == 1, picks_ref[0, 0, 1], picks_ref[0, 0, 2]),
    )
    enter(y, z, smp, z_chips, peers)

    def piece(ref, owner, c):
        row = pl.multiple_of((owner % per_array) * rows, rows)
        return ref.at[0, pl.ds(row, rows), pl.ds(c * cols, cols)]

    def spread(py, c, ref):
        return pltpu.make_async_remote_copy(
            src_ref=piece(ref, py * smp_size + smp, c),
            dst_ref=log[c].at[z * Y_CHIPS + y],
            send_sem=spread_send.at[c, py],
            recv_sem=spread_recv.at[c, y],
            device_id=(py * z_chips + z, smp),
            device_id_type=MESH,
        )

    def spread_in(py, c):
        return pltpu.make_async_remote_copy(
            src_ref=piece(keys_ref, mine, c),
            dst_ref=log[c].at[z * Y_CHIPS + py],
            send_sem=spread_send.at[c, py],
            recv_sem=spread_recv.at[c, py],
            device_id=(py * z_chips + z, smp),
            device_id_type=MESH,
        )

    def own(c, ref):
        return pltpu.make_async_copy(
            piece(ref, mine, c), log[c].at[z * Y_CHIPS + y], own_sem.at[c]
        )

    for c in range(CHUNKS):
        for dy in range(1, Y_CHIPS):
            py = (y + dy) % Y_CHIPS

            @pl.when(py < Y_CHIPS // 2)
            def _():
                spread(py, c, keys_ref).start()

            @pl.when(py >= Y_CHIPS // 2)
            def _():
                spread(py, c, values_ref).start()

        @pl.when(y < Y_CHIPS // 2)
        def _():
            own(c, keys_ref).start()

        @pl.when(y >= Y_CHIPS // 2)
        def _():
            own(c, values_ref).start()

    def name(device, slots):
        return pltpu.make_async_remote_copy(
            src_ref=named.at[mine] if slots is None else named.at[slots],
            dst_ref=named.at[mine] if slots is None else named.at[slots],
            send_sem=name_send.at[0],
            recv_sem=name_recv.at[0],
            device_id=device,
            device_id_type=MESH,
        )

    one_peer = peers[0][0]
    for device, _ in peers:
        name(device, None).start()
    for load in loads:
        load.start()

    def pass_on(c, source, step):
        slot = lax.rem(z + (z_chips - source) % z_chips, z_chips)
        to = lax.rem(z + step % z_chips, z_chips)
        those = log[c].at[pl.ds(slot * Y_CHIPS, Y_CHIPS)]
        return pltpu.make_async_remote_copy(
            src_ref=those,
            dst_ref=those,
            send_sem=ring_send.at[c, down_tree(c).index((source, step))],
            recv_sem=ring_recv.at[c, slot],
            device_id=(y * z_chips + to, smp),
            device_id_type=MESH,
        )

    def arrived(c, source):
        slot = lax.rem(z + (z_chips - source) % z_chips, z_chips)
        those = log[c].at[pl.ds(slot * Y_CHIPS, Y_CHIPS)]
        pltpu.make_async_remote_copy(
            src_ref=those,
            dst_ref=those,
            send_sem=ring_send.at[c, 0],
            recv_sem=ring_recv.at[c, slot],
            device_id=one_peer,
            device_id_type=MESH,
        ).wait_recv()

    def begin(c):
        for dy in range(1, Y_CHIPS):
            spread_in((y + dy) % Y_CHIPS, c).wait_recv()
        own(c, keys_ref).wait()
        relay(c, 0)

    def relay(c, distance):
        for side in (1, -1) if distance else (1,):
            source = distance * side
            if distance:
                arrived(c, source)
            for start, step in down_tree(c):
                if start == source:
                    pass_on(c, start, step).start()

    def leaves(c):
        for distance in (1, 2, 4, 5, 7):
            for side in (1, -1):
                arrived(c, distance * side)
        arrived(c, 8 * eight(c))

    def choose():
        lane_of = lax.broadcasted_iota(jnp.int32, (1, 128), 1)
        slot, row = lane_of // rows, lane_of % rows
        per_vector = 128 // rows
        codes = []
        for first in range(0, TOP * planes, per_vector):
            code = jnp.zeros((1, 128), jnp.int32)
            for j in range(per_vector):
                pick = place_of((first + j) // TOP, (first + j) % TOP)
                code = jnp.where(slot == j, pick * rows, code)
            codes.append(code + row)
        step = Y_CHIPS * rows

        def one(n, carry):
            start = pl.multiple_of(n * step, step)
            number = lax.broadcasted_iota(jnp.int32, (step, 128), 0) + start
            for m, code in enumerate(codes):
                hit = jnp.where(number == code, 1.0, 0.0)
                chosen[pl.ds(start, step), m * 128 : (m + 1) * 128] = hit.astype(BF16)
            return carry

        lax.fori_loop(0, z_chips, one, 0)

    def give(c, device, slot_send, slot_recv):
        return pltpu.make_async_remote_copy(
            src_ref=staged.at[c, slot_send],
            dst_ref=fetched.at[c, slot_recv],
            send_sem=pick_send.at[c],
            recv_sem=pick_recv.at[c],
            device_id=device,
            device_id_type=MESH,
        )

    def place_of(target, i):
        block = named_s[target, 0, i]
        return lax.rem(block, z_chips) * Y_CHIPS + lax.div(block, z_chips)

    def send_picks(c, some):
        for device, target in some:
            for i in range(TOP):
                staged[c, target, i] = log[c][place_of(target, i)]
            give(c, device, target, mine).start()

    def keep_picks(c):
        for i in range(TOP):
            fetched[c, mine, i] = log[c][place_of(mine, i)]

    def all_picks(c):
        return give(c, one_peer, pl.ds(0, others), pl.ds(0, others))

    def grads(c):
        live_rows = length_ref[0] - lax.axis_index("ctx") * tq
        live = lax.broadcasted_iota(jnp.int32, (tq, HEAD), 0) < live_rows
        across = (((1,), (1,)), ((), ()))
        down = (((0,), (0,)), ((), ()))

        def one(n, carry):
            inner = pl.ds(pl.multiple_of(n * HEAD, HEAD), HEAD)
            lanes = pl.ds(pl.multiple_of(c * cols + n * HEAD, HEAD), HEAD)
            base = (c * chunk_heads + n) * group * HEAD
            wide = [pl.ds(pl.multiple_of(base + h * HEAD, HEAD), HEAD) for h in range(group)]
            q = jnp.concatenate([q_all[:, w] for w in wide], axis=0)
            raw = [g_all[:, w] for w in wide]
            g = jnp.concatenate([jnp.where(live, r, jnp.zeros_like(r)) for r in raw], axis=0)

            def keys_of(i):
                if i == TOP:
                    return k_own[:, lanes]
                return fetched[c, :per_array, i, :, inner].reshape(tq, HEAD)

            def values_of(i):
                if i == TOP:
                    return v_own[:, lanes]
                return fetched[c, per_array:, i, :, inner].reshape(tq, HEAD)

            top = None
            for i in range(TOP + 1):
                s = lax.dot_general(keys_of(i), q, across, preferred_element_type=F32)
                if i == TOP:
                    row = lax.broadcasted_iota(jnp.int32, (tq, width), 0)
                    col = lax.broadcasted_iota(jnp.int32, (tq, width), 1) % tq
                    s = jnp.where(col >= row, s, -1e30)
                scores[i] = s
                best = jnp.max(s, axis=0, keepdims=True)
                top = best if top is None else jnp.maximum(top, best)
                grad_probs[i] = lax.dot_general(
                    values_of(i), g, across, preferred_element_type=F32
                )
            total = jnp.zeros((1, width), F32)
            delta = jnp.zeros((1, width), F32)
            for i in range(TOP + 1):
                w = jnp.exp2((scores[i] - top) * (SCALE * LOG2_E))
                scores[i] = w
                total = total + jnp.sum(w, axis=0, keepdims=True)
                delta = delta + jnp.sum(w * grad_probs[i], axis=0, keepdims=True)
            inverse = 1.0 / total
            delta = delta * inverse
            dq = None
            for i in range(TOP + 1):
                probs = scores[i] * inverse
                grad_low = (probs * (grad_probs[i] - delta)).astype(BF16)
                probs_low = probs.astype(BF16)
                dv = jnp.dot(probs_low, g, preferred_element_type=F32).astype(BF16)
                dk = jnp.dot(grad_low, q, preferred_element_type=F32) * SCALE
                dk = dk.astype(BF16)
                some = lax.dot_general(grad_low, keys_of(i), down, preferred_element_type=F32)
                dq = some if dq is None else dq + some
                if i == TOP:
                    dk_own[:, lanes] = dk
                    dv_own[:, lanes] = dv
                else:
                    strips[c, :per_array, i, :, inner] = dk.reshape(per_array, rows, HEAD)
                    strips[c, per_array:, i, :, inner] = dv.reshape(per_array, rows, HEAD)
            for h in range(group):
                dq_all[:, wide[h]] = (dq[h * tq : (h + 1) * tq] * SCALE).astype(BF16)
            return carry

        lax.fori_loop(0, chunk_heads, one, 0)

    def back(c, device, slot_send, slot_recv):
        return pltpu.make_async_remote_copy(
            src_ref=strips.at[c, slot_send],
            dst_ref=held.at[c, slot_recv],
            send_sem=give_send.at[c],
            recv_sem=give_recv.at[c],
            device_id=device,
            device_id_type=MESH,
        )

    def send_partials(c):
        for device, target in peers:
            back(c, device, target, pl.ds(TOP * mine, TOP)).start()
        for i in range(TOP):
            held[c, TOP * mine + i] = strips[c, mine, i]

    def all_partials(c):
        return pltpu.make_async_remote_copy(
            src_ref=held.at[c, pl.ds(0, TOP * others)],
            dst_ref=held.at[c, pl.ds(0, TOP * others)],
            send_sem=give_send.at[c],
            recv_sem=give_recv.at[c],
            device_id=one_peer,
            device_id_type=MESH,
        )

    def add_up(c):
        step = 4 * Y_CHIPS * rows
        those = held[c].reshape(TOP * planes * rows, cols)

        def one(n, carry):
            part = pl.ds(pl.multiple_of(n * step, step), step)
            sums[c, part] = jnp.dot(chosen[part], those, preferred_element_type=F32)
            return carry

        lax.fori_loop(0, z_chips // 4, one, 0)

    def total_of(c, role, feeders):
        step = Y_CHIPS * rows
        dest = lax.rem(z + (z_chips - role) % z_chips, z_chips)
        acc = sums[c, pl.ds(pl.multiple_of(dest * step, step), step)]
        acc = acc.reshape(Y_CHIPS, rows, cols)
        for feeder in feeders:
            acc = acc + arriving[c, slot_of(c, feeder)].astype(F32)
        return acc

    def slot_of(c, role):
        return [r for r, _ in up_tree(c)].index(role)

    def pass_up(c, role):
        slot = slot_of(c, role)
        to = lax.rem(z + up_tree(c)[slot][1] % z_chips, z_chips)
        return pltpu.make_async_remote_copy(
            src_ref=sending.at[c, slot],
            dst_ref=arriving.at[c, slot],
            send_sem=back_send.at[c, slot],
            recv_sem=back_recv.at[c, slot],
            device_id=(y * z_chips + to, smp),
            device_id_type=MESH,
        )

    def feeders_of(c, role):
        side = 1 if role > 0 else -1
        if abs(role) == 3:
            return [2 * side, 4 * side, 6 * side]
        if abs(role) == 6:
            return [5 * side, 7 * side] + ([8 * side] if side == eight(c) else [])
        return [1, -1, 3, -3] if role == 0 else []

    def send_up(c, role):
        feeders = feeders_of(c, role)
        slot = slot_of(c, role)
        for feeder in feeders:
            pass_up(c, feeder).wait_recv()

        sending[c, slot] = total_of(c, role, feeders).astype(BF16)
        pass_up(c, role).start()

    def last(c, device, head, py, slot_recv):
        return pltpu.make_async_remote_copy(
            src_ref=final.at[c, head, py],
            dst_ref=gathered.at[slot_recv],
            send_sem=last_send.at[0],
            recv_sem=last_recv.at[0],
            device_id=device,
            device_id_type=MESH,
        )

    owners = smp_size // CHUNKS

    def close(c):
        for feeder in feeders_of(c, 0):
            pass_up(c, feeder).wait_recv()

        whole = total_of(c, 0, feeders_of(c, 0)).astype(BF16)
        for n in range(chunk_heads):
            final[c, n] = whole[:, :, n * HEAD : (n + 1) * HEAD]
        first = c * owners
        turns = [
            (lax.rem(y + n // owners, Y_CHIPS), first + lax.rem(smp + n % owners, owners))
            for n in range(Y_CHIPS * owners)
        ]
        for py, ps in turns:

            @pl.when(py * smp_size + ps != mine)
            def _():
                last(c, (py * z_chips + z, ps), (ps - first) // 2, py, mine).start()

    def stores(c):
        narrow = pl.ds(pl.multiple_of(c * cols, cols), cols)
        wide = pl.ds(pl.multiple_of(c * cols * group, cols), cols * group)
        return [
            pltpu.make_async_copy(
                scratch.at[:, part_of], ref.at[0, :, part_of], store_sem.at[c, n]
            )
            for n, (scratch, ref, part_of) in enumerate(
                (
                    (dq_all, grad_queries_ref, wide),
                    (dk_own, grad_keys_ref, narrow),
                    (dv_own, grad_values_ref, narrow),
                )
            )
        ]

    begin(0)
    name(one_peer, pl.ds(0, others)).wait_recv()
    to_smem = pltpu.make_async_copy(named, named_s, smem_sem.at[0])
    to_smem.start()
    def serve_picks(c):
        leaves(c)
        send_picks(c, peers)
        keep_picks(c)

    for stage in range(CHUNKS + 2):
        if stage == 2:
            to_smem.wait()
            choose()
        if 0 <= stage - 2 < CHUNKS:
            relay(stage - 2, 6)
        if 0 <= stage - 1 < CHUNKS:
            relay(stage - 1, 3)
        if 0 < stage < CHUNKS:
            begin(stage)
        if 0 <= stage - 3 < CHUNKS - 1:
            serve_picks(stage - 3)
    for load in loads:
        load.wait()

    def climb(c):
        all_partials(c).wait_recv()
        add_up(c)
        for role in UP_LEAVES:
            send_up(c, role)
            send_up(c, -role)
        send_up(c, 8 * eight(c))

    def heads(c, carry):
        all_picks(c).wait_recv()
        grads(c)
        send_partials(c)
        for copy in stores(c):
            copy.start()

        @pl.when(c == 0)
        def _():
            serve_picks(CHUNKS - 1)

        @pl.when(c == CHUNKS - 2)
        def _():
            climb(0)

        return carry

    lax.fori_loop(0, CHUNKS, heads, 0)
    ahead = [1] + [0] * (CHUNKS - 1)
    for stage in range(CHUNKS + 3):
        if 0 < stage < CHUNKS:
            climb(stage)
        for c in range(CHUNKS):
            if stage == c + 1 - ahead[c]:
                send_up(c, 6)
                send_up(c, -6)
            if stage == c + 2 - ahead[c]:
                send_up(c, 3)
                send_up(c, -3)
            if stage == c + 3 - ahead[c]:
                close(c)

    for c in range(CHUNKS):

        @pl.when(smp // owners == c)
        def _():
            gathered[mine] = final[c, (smp // 2) % chunk_heads, y]

    all_last = pltpu.make_async_remote_copy(
        src_ref=gathered.at[pl.ds(0, others)],
        dst_ref=gathered.at[pl.ds(0, others)],
        send_sem=last_send.at[0],
        recv_sem=last_recv.at[0],
        device_id=one_peer,
        device_id_type=MESH,
    )
    all_last.wait_recv()
    got_keys = gathered[:per_array].reshape(per_array * rows, HEAD).astype(F32)
    got_values = gathered[per_array:].reshape(per_array * rows, HEAD).astype(F32)
    low = lax.broadcasted_iota(jnp.int32, got_keys.shape, 1) < HEAD // 2
    even = jnp.where(low, got_keys, pltpu.roll(got_values, HEAD // 2, 1))
    odd = jnp.where(low, pltpu.roll(got_keys, HEAD // 2, 1), got_values)
    out_ref[...] = jnp.where(smp % 2 == 0, even, odd).T.astype(BF16)

    name(one_peer, pl.ds(0, others)).wait_send()
    for c in range(CHUNKS):
        for dy in range(1, Y_CHIPS):
            spread((y + dy) % Y_CHIPS, c, keys_ref).wait_send()
        for source, step in down_tree(c):
            pass_on(c, source, step).wait_send()
        for role, _ in up_tree(c):
            pass_up(c, role).wait_send()
        for copy in stores(c):
            copy.wait()
        all_picks(c).wait_send()
        all_partials(c).wait_send()
    all_last.wait_send()


def hand_over_kernel(
    grad_queries, grad_keys, grad_values, summed, out_q, out_k, out_v, out_gk, out_gv, q, k, v, both,
    load_sem, store_sem
):
    quarter = q.shape[1] // 4
    steps = []
    for n in range(4):
        rows = pl.ds(n * quarter, quarter)
        steps.append((grad_queries.at[:, rows], q.at[:, rows], out_q.at[:, rows]))
    steps.append((grad_keys, k, out_k))
    steps.append((grad_values, v, out_v))
    steps.append((summed.at[: HEAD // 2], both.at[: HEAD // 2], out_gk))
    steps.append((summed.at[HEAD // 2 :], both.at[HEAD // 2 :], out_gv))
    loads = [
        pltpu.make_async_copy(source, held, load_sem.at[n])
        for n, (source, held, _) in enumerate(steps)
    ]
    stores = [
        pltpu.make_async_copy(held, target, store_sem.at[n])
        for n, (_, held, target) in enumerate(steps)
    ]
    for load in loads:
        load.start()
    for load, store in zip(loads, stores):
        load.wait()
        store.start()
    for store in stores:
        store.wait()


def body(
    queries, out_grad, local_keys, trajectory_values, journal_keys, journal_values, picks, lengths
):
    smp_size = lax.axis_size("smp")
    z_chips = lax.axis_size("ctx") // Y_CHIPS
    planes = Y_CHIPS * smp_size
    block_rows, features = journal_keys.shape[1:]
    blocks = Y_CHIPS * z_chips
    rows = 2 * block_rows // planes
    cols = features // CHUNKS
    tq = queries.shape[1]
    width = queries.shape[2] // (features // HEAD) // HEAD * tq
    heads = cols // HEAD
    dma = pltpu.SemaphoreType.DMA
    vmem = pltpu.VMEM
    any_space = pl.BlockSpec(memory_space=pl.ANY)
    in_smem = pl.BlockSpec(memory_space=pltpu.SMEM)
    in_vmem = pl.BlockSpec(memory_space=pltpu.VMEM)
    grad_queries, grad_local_keys, grad_local_values, summed = pl.pallas_call(
        functools.partial(fused_kernel, z_chips, smp_size),
        out_shape=(
            jax.ShapeDtypeStruct(queries.shape, BF16),
            jax.ShapeDtypeStruct(local_keys.shape, BF16),
            jax.ShapeDtypeStruct(local_keys.shape, BF16),
            jax.ShapeDtypeStruct((HEAD, block_rows), BF16),
        ),
        in_specs=[in_smem, in_smem] + [any_space] * 6,
        out_specs=(any_space, any_space, any_space, in_vmem),
        scratch_shapes=[
            vmem((blocks, rows, cols), BF16),
            vmem((blocks, rows, cols), BF16),
            vmem((blocks, rows, cols), BF16),
            vmem((blocks, rows, cols), BF16),
            vmem((CHUNKS, planes, TOP, rows, cols), BF16),
            vmem((CHUNKS, planes, TOP, rows, cols), BF16),
            vmem((planes, 1, 128), jnp.int32),
            pltpu.SMEM((planes, 1, 128), jnp.int32),
            vmem((blocks * rows, TOP * planes * rows), BF16),
            vmem((CHUNKS, blocks * rows, cols), F32),
            vmem(queries.shape[1:], BF16),
            vmem(queries.shape[1:], BF16),
            vmem(local_keys.shape[1:], BF16),
            vmem(local_keys.shape[1:], BF16),
            vmem(queries.shape[1:], BF16),
            vmem(local_keys.shape[1:], BF16),
            vmem(local_keys.shape[1:], BF16),
            vmem((TOP + 1, tq, width), F32),
            vmem((TOP + 1, tq, width), F32),
            vmem((CHUNKS, planes, TOP, rows, cols), BF16),
            vmem((CHUNKS, TOP * planes, rows, cols), BF16),
            vmem((CHUNKS, z_chips - 1, Y_CHIPS, rows, cols), BF16),
            vmem((CHUNKS, z_chips - 1, Y_CHIPS, rows, cols), BF16),
            vmem((CHUNKS, heads, Y_CHIPS, rows, HEAD), BF16),
            vmem((planes, rows, HEAD), BF16),
            dma((4,)),
            dma((CHUNKS, 3)),
            dma((CHUNKS, Y_CHIPS)),
            dma((CHUNKS, Y_CHIPS)),
            dma((CHUNKS,)),
            dma((1,)),
            dma((1,)),
            dma((2,)),
            dma((CHUNKS, z_chips - 1)),
            dma((CHUNKS, z_chips)),
            dma((CHUNKS,)),
            dma((CHUNKS,)),
            dma((CHUNKS,)),
            dma((CHUNKS,)),
            dma((CHUNKS, z_chips - 1)),
            dma((CHUNKS, z_chips - 1)),
            dma((1,)),
            dma((1,)),
        ],
        compiler_params=pltpu.CompilerParams(
            collective_id=0, has_side_effects=True, vmem_limit_bytes=56 << 20
        ),
        name="sparse_attention_grads",
    )(
        picks,
        lengths,
        queries,
        out_grad,
        local_keys,
        trajectory_values,
        journal_keys,
        journal_values,
    )
    half_head = jax.ShapeDtypeStruct((HEAD // 2, block_rows), BF16)
    results = pl.pallas_call(
        hand_over_kernel,
        out_shape=(
            jax.ShapeDtypeStruct(queries.shape, BF16),
            jax.ShapeDtypeStruct(local_keys.shape, BF16),
            jax.ShapeDtypeStruct(local_keys.shape, BF16),
            half_head,
            half_head,
        ),
        in_specs=[any_space] * 4,
        out_specs=(any_space,) * 5,
        scratch_shapes=[
            vmem(queries.shape, BF16),
            vmem(local_keys.shape, BF16),
            vmem(local_keys.shape, BF16),
            vmem((HEAD, block_rows), BF16),
            dma((8,)),
            dma((8,)),
        ],
        compiler_params=pltpu.CompilerParams(vmem_limit_bytes=56 << 20),
        name="hand_over",
    )(grad_queries, grad_local_keys, grad_local_values, summed)
    return results[:3] + (results[3].T[None], results[4].T[None])


def solution(mesh):
    in_specs = (
        P("smp", "ctx", None),
        P("smp", "ctx", None),
        P("smp", "ctx", None),
        P("smp", "ctx", None),
        P("ctx", None, None),
        P("ctx", None, None),
        P("smp", "ctx", None),
        P("smp"),
    )
    out_specs = (
        P("smp", "ctx", None),
        P("smp", "ctx", None),
        P("smp", "ctx", None),
        P("ctx", None, "smp"),
        P("ctx", None, "smp"),
    )
    return jax.shard_map(body, mesh=mesh, in_specs=in_specs, out_specs=out_specs, check_vma=False)
```
